32 devices in a mesh: expert: 4 (over z), context: 4 (over y, core), dp: 2 (over x).
Axes of the slice: x: 2, y: 2, z: 4, core: 2. Of those that a mesh axis runs over, the one named last changes fastest.
Arguments:
- hidden_in: bfloat16 [8, 1024, 2048], P(('expert', 'dp'), 'context'), may hold values from -6 to 6
- out_grad: bfloat16 [8, 1024, 2048], P(('expert', 'dp'), 'context'), may hold values from -6 to 6
- routes: int32 [8, 1024, 8], P(('expert', 'dp'), 'context'), may hold values from 0 to 15, all different within a row; in each aligned block of 256 rows (0 to 255, 256 to 511, ..., all dimensions but the last counted through in order) at most 144 rows name the same one
- attn_gain: bfloat16 [2048], P(('expert', 'context')), may hold values from 0.25 to 1.75
- w_query: bfloat16 [2048, 2048], P(('expert', 'context')), may hold values from -0.125 to 0.125
- w_key: bfloat16 [2048, 2048], P(('expert', 'context')), may hold values from -0.125 to 0.125
- w_value: bfloat16 [2048, 2048], P(('expert', 'context')), may hold values from -0.125 to 0.125
- q_gain: bfloat16 [2048], P(('expert', 'context')), may hold values from 0.25 to 1.75
- k_gain: bfloat16 [2048], P(('expert', 'context')), may hold values from 0.25 to 1.75
- w_out: bfloat16 [2048, 2048], P(('expert', 'context')), may hold values from -2.5 to 2.5
- ffn_gain: bfloat16 [2048], P(('expert', 'context')), may hold values from 0.25 to 1.75
- w_router: bfloat16 [2048, 16], P(('expert', 'context')), may hold values from -0.0625 to 0.0625
- w_gate: bfloat16 [16, 2048, 1024], P('expert'), may hold values from -0.125 to 0.125
- w_up: bfloat16 [16, 2048, 1024], P('expert'), may hold values from -0.125 to 0.125
- w_down: bfloat16 [16, 1024, 2048], P('expert'), may hold values from -0.75 to 0.75
Outputs:
- hidden_out: bfloat16 [8, 1024, 2048], P(('expert', 'dp'), 'context')
- input_grad: bfloat16 [8, 1024, 2048], P(('expert', 'dp'), 'context')
- attn_gain_grad: float32 [2048], P(('expert', 'context'))
- w_query_grad: float32 [2048, 2048], P(('expert', 'context'))
- w_key_grad: float32 [2048, 2048], P(('expert', 'context'))
- w_value_grad: float32 [2048, 2048], P(('expert', 'context'))
- q_gain_grad: float32 [2048], P(('expert', 'context'))
- k_gain_grad: float32 [2048], P(('expert', 'context'))
- w_out_grad: float32 [2048, 2048], P(('expert', 'context'))
- ffn_gain_grad: float32 [2048], P(('expert', 'context'))
- w_router_grad: float32 [2048, 16], P(('expert', 'context'))
- w_gate_grad: float32 [16, 2048, 1024], P('expert')
- w_up_grad: float32 [16, 2048, 1024], P('expert')
- w_down_grad: float32 [16, 1024, 2048], P('expert')
The draws below stay inside these ranges and needn't reach their ends.
Inputs may be any that keep to these rules, and one draw needn't show every extreme that they name: `routes`: each token names 8 different experts. At most 144 tokens of one device name the same expert, a bound that some block reaches of one device.
All inputs are finite; a program needn't handle non-finite values.
Results may differ from the reference program's by a relative error of at most 0.02.
Values may be sent and summed in bfloat16 or wider, within the bound.
No kernel may reach another device: no remote copies, remote signals or barrier semaphores. Data moves between devices by JAX's collectives and lax.ppermute only.
A program may use at most 512 MiB of HBM per device.

```python
import math
import jax
import jax.numpy as jnp
import numpy as np
from jax import lax

D = 2048
HEADS = 16
HDIM = 128
FF = 1024
TOPK = 8
EXPERTS = 16
TOK_DEV = 256
LEN = 1024
SEQS = 8
CAP = 144


def level_of(rng, dims, split, low, largest):
    def one(axis_at, parts):
        steps = jax.random.uniform(jax.random.fold_in(jax.random.fold_in(rng, 6), axis_at), (parts,), jnp.float32, low / len(split), largest / len(split))
        return jnp.repeat(jnp.exp(steps), dims[axis_at] // parts).reshape((-1,) + (1,) * (len(dims) - axis_at - 1))

    loudness = one(*split[0])
    for cut in split[1:]:
        loudness = loudness * one(*cut)
    return loudness


def shared_out(key, own, number, rows, count, top, most, lean):
    sequence = jax.random.permutation(key, count)
    heavy_load, common = load_shares(count, rows * top, most, lean, True), load_shares(count, rows * top, most, lean, False)
    places = jnp.arange(count)

    def named(lengths, turn):
        used = int((lengths > 0).sum())
        fixed = max(1, used // 4)
        passed = fixed + (places - fixed + turn * (used - fixed)) % max(1, count - fixed)
        return jnp.zeros((count,), jnp.int32).at[sequence[jnp.where(places < fixed, places, passed)]].set(jnp.asarray(lengths, jnp.int32))

    lengths = jnp.where(number % 4 == 0, named(heavy_load, number // 4), named(common, number - number // 4 - 1))
    mixed = jax.random.permutation(jax.random.fold_in(own, 3), count)
    giver, taker = mixed[0:count // 2 * 2:2], mixed[1:count // 2 * 2:2]
    margin = jnp.minimum(lengths[giver] - 1, most - lengths[taker]) // 2
    margin = jnp.where((giver == sequence[0]) | (taker == sequence[0]) | (lengths[taker] == 0), 0, jnp.maximum(margin, 0))
    passed = jax.random.randint(jax.random.fold_in(own, 4), (count // 2,), 0, 1 << 20) % (margin + 1)
    lengths = lengths.at[giver].add(-passed).at[taker].add(passed)
    items = jnp.searchsorted(jnp.cumsum(lengths), jnp.arange(rows * top), side="right").astype(jnp.int32)
    table = items.reshape(top, rows).T
    table = table[jax.random.permutation(jax.random.fold_in(own, 1), rows)]
    turn = jax.random.randint(jax.random.fold_in(own, 2), (rows, 1), 0, top)
    return jnp.take_along_axis(table, (jnp.arange(top)[None, :] + turn) % top, axis=1)


def load_shares(amount, total, bound, slope, full):
    loads = [(1 << 20) // math.isqrt(standing ** slope) + 1 for standing in range(1, amount + 1)]
    largest = bound if full else min(bound, max(-(-total // amount), total * loads[0] // sum(loads)))
    least = 1 if total - largest >= amount - 1 else 0
    counts, surplus = [largest] + [least] * (amount - 1), total - largest - least * (amount - 1)
    while surplus > 0:
        free = [i for i in range(1, amount) if counts[i] < largest] or [i for i in range(1, amount) if counts[i] < bound]
        whole, left = sum([loads[i] for i in free]), surplus
        for i in free:
            extra = min(bound - counts[i], max(1, left * loads[i] // whole), surplus)
            counts[i] = counts[i] + extra
            surplus = surplus - extra
    return np.array(counts)


def scatter_about(stream_key, dims, deviation, most, cuts=(), held_as=jnp.bfloat16):
    drawn = jax.random.normal(stream_key, dims, jnp.float32) * deviation
    if len(cuts) > 0:
        drawn = level_of(stream_key, dims, cuts, -0.22, 0.18) * drawn
    return jnp.clip(drawn, min=-most, max=most).astype(held_as)


def setup_inputs(seed: int = 0) -> dict:
    key_list = jax.random.split(jax.random.key(seed), 16)
    hidden_in = scatter_about(key_list[0], (SEQS, LEN, D), 1.0, 6.0, ((0, 8), (1, 4)))
    out_grad = scatter_about(key_list[1], (SEQS, LEN, D), 1.0, 6.0, ((0, 8), (1, 4)))
    routes_keys = jax.random.split(jax.random.fold_in(key_list[2], 1), SEQS * LEN // TOK_DEV)
    routes_turns = jax.random.permutation(jax.random.fold_in(key_list[2], 3), SEQS * LEN // TOK_DEV)
    routes = jax.vmap(lambda own, number: shared_out(jax.random.fold_in(key_list[2], 2), own, number, TOK_DEV, EXPERTS, TOPK, CAP, 0))(routes_keys, routes_turns).reshape((SEQS, LEN, TOPK))
    attn_gain = jnp.clip(1.0 + 0.15 * jax.random.normal(key_list[3], (D,), jnp.float32), 0.25, 1.75).astype(jnp.bfloat16)
    w_query = scatter_about(key_list[4], (D, D), D ** -0.5, 0.125, ((0, 16),))
    w_key = scatter_about(key_list[5], (D, D), D ** -0.5, 0.125, ((0, 16),))
    w_value = scatter_about(key_list[6], (D, D), D ** -0.5, 0.125, ((0, 16),))
    q_gain = jnp.clip(1.0 + 0.15 * jax.random.normal(key_list[7], (D,), jnp.float32), 0.25, 1.75).astype(jnp.bfloat16)
    k_gain = jnp.clip(1.0 + 0.15 * jax.random.normal(key_list[8], (D,), jnp.float32), 0.25, 1.75).astype(jnp.bfloat16)
    w_out = scatter_about(key_list[9], (D, D), (max(3 * D // LEN, 1)) ** -0.5, 2.5, ((0, 16),))
    ffn_gain = jnp.clip(1.0 + 0.15 * jax.random.normal(key_list[10], (D,), jnp.float32), 0.25, 1.75).astype(jnp.bfloat16)
    w_router = scatter_about(key_list[11], (D, EXPERTS), (4 * D) ** -0.5, 0.0625, ((0, 16),))
    w_gate = scatter_about(key_list[12], (EXPERTS, D, FF), D ** -0.5, 0.125, ((0, 4),))
    w_up = scatter_about(key_list[13], (EXPERTS, D, FF), D ** -0.5, 0.125, ((0, 4),))
    w_down = scatter_about(key_list[14], (EXPERTS, FF, D), (FF // 16) ** -0.5, 0.75, ((0, 4),))
    return {"hidden_in": hidden_in, "out_grad": out_grad, "routes": routes, "attn_gain": attn_gain, "w_query": w_query, "w_key": w_key, "w_value": w_value, "q_gain": q_gain, "k_gain": k_gain, "w_out": w_out, "ffn_gain": ffn_gain, "w_router": w_router, "w_gate": w_gate, "w_up": w_up, "w_down": w_down}


@jax.custom_vjp
def low(v):
    return lax.optimization_barrier(v.astype(jnp.bfloat16)).astype(jnp.float32)

@jax.custom_vjp
def low_back(v):
    return v

def low_keep(v):
    return (low(v), None)

def low_pass(kept, grad):
    return (grad,)

def back_keep(v):
    return (v, None)

def back_low(kept, grad):
    return (low(grad),)
low.defvjp(low_keep, low_pass)
low_back.defvjp(back_keep, back_low)
epsilon = 1e-06
rope_base = 10000.0
highest = lax.Precision.HIGHEST

def product(left, right):
    return jnp.dot(left, right, preferred_element_type=jnp.float32, precision=highest)

def normalize(values, gain_vector):
    return values * lax.rsqrt(lax.optimization_barrier(jnp.mean(values * values, axis=-1, keepdims=True)) + epsilon) * gain_vector

def rotate(values, cosine, sine_part, direction):
    half_width = values.shape[-1] // 2
    first_half = values[..., :half_width]
    second_half = values[..., half_width:]
    turned = sine_part * direction
    return jnp.concatenate([first_half * cosine - second_half * turned, second_half * cosine + first_half * turned], axis=-1)

def attend(queries, keys_in, values_in):
    scores = low_back(jnp.einsum('qhd,khd->hqk', queries, keys_in, precision=highest) * HDIM ** (-0.5))
    weights = low(jax.nn.softmax(scores, axis=-1))
    return jnp.einsum('hqk,khd->qhd', weights, values_in, precision=highest)

def expert_term(inputs, gate_w, up_w, down_w, column):
    copied = low_back(inputs)
    gate_pre = low_back(product(copied, gate_w))
    up_pre = low_back(product(copied, up_w))
    hidden = low(jax.nn.silu(gate_pre) * up_pre)
    result = low(low_back(product(hidden, down_w)))
    return result * column[:, None]

def whole_layer(block_in, block_routes, weights):
    attn_gain, w_query, w_key, w_value, q_gain, k_gain, w_out, ffn_gain, w_router, w_gate, w_up, w_down = weights
    members, length, width = block_in.shape
    flat_rows = block_in.reshape(members * length, width)
    normed = low(normalize(flat_rows, attn_gain))
    queries = low_back(product(normed, w_query))
    keys_raw = low_back(product(normed, w_key))
    values_low = low(low_back(product(normed, w_value)))
    positions = jnp.arange(length, dtype=jnp.float32)
    frequency = rope_base ** (-jnp.arange(HDIM // 2, dtype=jnp.float32) * 2.0 / HDIM)
    angles = positions[:, None] * frequency[None, :]
    cosine = jnp.cos(angles)[None, :, None, :]
    sine_part = jnp.sin(angles)[None, :, None, :]
    head_shape = (members, length, HEADS, HDIM)
    query_rot = low(rotate(normalize(queries, q_gain).reshape(head_shape), cosine, sine_part, 1.0))
    key_rot = low(rotate(normalize(keys_raw, k_gain).reshape(head_shape), cosine, sine_part, 1.0))
    value_heads = values_low.reshape(head_shape)
    attend_one = jax.checkpoint(lambda triple: attend(triple[0], triple[1], triple[2]))
    attended = lax.map(attend_one, (query_rot, key_rot, value_heads))
    mixed_low = low(low_back(attended.reshape(members * length, width)))
    residual = flat_rows + low_back(product(mixed_low, w_out))
    normed_two = low(normalize(residual, ffn_gain))
    logits = low_back(product(normed_two, w_router))
    chosen_hot = (block_routes.reshape(members * length, TOPK)[:, :, None] == jnp.arange(EXPERTS, dtype=jnp.int32)).astype(jnp.float32)
    picked = lax.optimization_barrier(jnp.sum(chosen_hot * logits[:, None, :], axis=-1))
    gate_weights = jax.nn.softmax(picked, axis=-1)
    weight_table = lax.optimization_barrier(jnp.sum(gate_weights[:, :, None] * chosen_hot, axis=1))

    def add_expert(running, pieces):
        gate_w, up_w, down_w, column = pieces
        return (running + expert_term(normed_two, gate_w, up_w, down_w, column), None)
    combined, unused = lax.scan(jax.checkpoint(add_expert), jnp.zeros_like(residual), (w_gate, w_up, w_down, weight_table.T))
    return (residual + combined).reshape(members, length, width)

def reference(hidden_in, out_grad, routes, attn_gain, w_query, w_key, w_value, q_gain, k_gain, w_out, ffn_gain, w_router, w_gate, w_up, w_down):
    weights = tuple((array_in.astype(jnp.float32) for array_in in (attn_gain, w_query, w_key, w_value, q_gain, k_gain, w_out, ffn_gain, w_router, w_gate, w_up, w_down)))
    members = max([candidate for candidate in range(1, SEQS + 1) if SEQS % candidate == 0 and candidate * LEN <= 4096] + [1])
    blocks = SEQS // members
    inputs = hidden_in.astype(jnp.float32).reshape(blocks, members, LEN, D)
    cotangents = out_grad.astype(jnp.float32).reshape(blocks, members, LEN, D)
    indices = routes.reshape(blocks, members, LEN, TOPK)

    def one_group(totals, pieces):
        block_in, block_grad, block_routes = pieces
        result, pullback = jax.vjp(lambda inner, params: whole_layer(inner, block_routes, params), block_in, weights)
        input_cot, weight_cots = pullback(block_grad)
        totals = tuple((running + cotangent for running, cotangent in zip(totals, weight_cots)))
        return (totals, (result, input_cot))
    initial = tuple((jnp.zeros_like(array_in) for array_in in weights))
    totals, outputs = lax.scan(one_group, initial, (inputs, cotangents, indices))
    results, input_cots = outputs
    hidden_out = results.reshape(SEQS, LEN, D).astype(jnp.bfloat16)
    input_grad = input_cots.reshape(SEQS, LEN, D).astype(jnp.bfloat16)
    return (hidden_out, input_grad, totals[0], totals[1], totals[2], totals[3], totals[4], totals[5], totals[6], totals[7], totals[8], totals[9], totals[10], totals[11])
```

```python
import functools

import jax
import jax.numpy as jnp
from jax import lax
from jax.sharding import PartitionSpec as P

HEADS = 16
HDIM = 128

epsilon = 1e-06
rope_base = 10000.0
F32 = jnp.float32
BF16 = jnp.bfloat16


def dot(left, right, contract):
    return lax.dot_general(
        left, right, (((contract[0],), (contract[1],)), ((), ())), preferred_element_type=F32
    )


def rms_factor(values):
    return lax.rsqrt(jnp.mean(values * values, axis=-1, keepdims=True) + epsilon)


def norm_back(grad_out, values, factor, gain_vector):
    scaled = grad_out * gain_vector
    grad_in = factor * scaled - values * factor**3 * jnp.mean(
        scaled * values, axis=-1, keepdims=True
    )
    gain_grad = jnp.sum(grad_out * values * factor, axis=0)
    return (grad_in, gain_grad)


def rotate(values, cosine, sine_part):
    first_half = values[..., : HDIM // 2]
    second_half = values[..., HDIM // 2 :]
    return jnp.concatenate(
        [
            first_half * cosine - second_half * sine_part,
            second_half * cosine + first_half * sine_part,
        ],
        axis=-1,
    )


def gather(values, axis):
    return lax.all_gather(values, axis, axis=0, tiled=True)


def scatter_sum(values, axis):
    return lax.psum_scatter(values, axis, scatter_dimension=0, tiled=True)


def head_rows(weight, context, mine):
    rows, width = weight.shape
    per = HEADS // context
    split = weight.reshape(rows, per, context, HDIM)
    return split.transpose(2, 0, 1, 3).reshape(context, rows, per * HDIM)


def body(
    hidden_in,
    out_grad,
    routes,
    attn_gain,
    w_query,
    w_key,
    w_value,
    q_gain,
    k_gain,
    w_out,
    ffn_gain,
    w_router,
    w_gate,
    w_up,
    w_down,
):
    groups = lax.axis_size("expert")
    context = lax.axis_size("context")
    my_group = lax.axis_index("expert")
    my_context = lax.axis_index("context")
    tokens = hidden_in.shape[1]
    width = hidden_in.shape[2]
    rows = w_query.shape[0]
    local_experts = w_gate.shape[0]
    experts_all = w_router.shape[1]
    length = tokens * context
    per = HEADS // context
    local = per * HDIM
    score_scale = HDIM ** (-0.5)

    hidden_all = gather(hidden_in[0], "context")
    small = jnp.concatenate(
        [
            attn_gain[:, None],
            q_gain[:, None],
            k_gain[:, None],
            ffn_gain[:, None],
            w_router,
        ],
        axis=1,
    )
    small_all = gather(small, ("expert", "context"))
    columns = jnp.concatenate(
        [head_rows(w, context, my_context) for w in (w_query, w_key, w_value)], axis=2
    )
    columns = lax.all_to_all(columns, "context", split_axis=0, concat_axis=0, tiled=True)
    qkv_w = gather(columns.reshape(context * rows, 3 * local), "expert")
    whole_heads = rows == HDIM
    if whole_heads:
        out_w = gather(w_out, "expert")
    else:
        out_w = gather(w_out, ("expert", "context")).reshape(per, context, HDIM, width)
        out_w = lax.dynamic_index_in_dim(out_w, my_context, 1, keepdims=False)
        out_w = out_w.reshape(local, width)
    upstream_all = gather(out_grad[0], "expert")
    routes_all = gather(routes[0], "expert")

    gain_attn = small_all[:, 0].astype(F32)
    gain_ffn = small_all[:, 3].astype(F32)
    router_w = small_all[:, 4:]

    def mine(vector):
        table = vector.reshape(per, context, HDIM)
        return lax.dynamic_index_in_dim(table, my_context, 1, keepdims=False).astype(F32)

    gain_query, gain_key = mine(small_all[:, 1]), mine(small_all[:, 2])

    source_all = hidden_all.astype(F32)
    factor_all = rms_factor(source_all)
    normed = (source_all * factor_all * gain_attn).astype(BF16)
    source = hidden_in[0].astype(F32)
    factor_one = rms_factor(source)
    qkv = dot(normed, qkv_w, (1, 0))
    query_raw = qkv[:, :local]
    key_raw = qkv[:, local : 2 * local]
    value_low = qkv[:, 2 * local :].astype(BF16).reshape(length, per, HDIM)
    squares = jnp.stack(
        [jnp.sum(query_raw * query_raw, axis=-1), jnp.sum(key_raw * key_raw, axis=-1)], axis=0
    )
    squares = lax.psum(squares, "context")
    factors = lax.rsqrt(squares / width + epsilon)
    factor_query, factor_key = factors[0][:, None, None], factors[1][:, None, None]
    query_raw = query_raw.reshape(length, per, HDIM)
    key_raw = key_raw.reshape(length, per, HDIM)
    positions = jnp.arange(length, dtype=jnp.int32).astype(F32)
    frequency = rope_base ** (-jnp.arange(HDIM // 2, dtype=F32) * 2.0 / HDIM)
    angles = positions[:, None] * frequency[None, :]
    cosine = jnp.cos(angles)[:, None, :]
    sine_part = jnp.sin(angles)[:, None, :]
    query_low = rotate(query_raw * factor_query * gain_query, cosine, sine_part).astype(BF16)
    key_low = rotate(key_raw * factor_key * gain_key, cosine, sine_part).astype(BF16)
    scores = (
        jnp.einsum("qhd,khd->hqk", query_low, key_low, preferred_element_type=F32) * score_scale
    )
    score_max = jnp.max(scores, axis=-1, keepdims=True)
    denominator = jnp.sum(jnp.exp(scores - score_max), axis=-1, keepdims=True)
    logsum = score_max + jnp.log(denominator)
    probs = jnp.exp(scores - logsum)
    mixed_low = (
        jnp.einsum("hqk,khd->qhd", probs.astype(BF16), value_low, preferred_element_type=F32)
        .reshape(length, local)
        .astype(BF16)
    )
    mixed_out = scatter_sum(dot(mixed_low, out_w, (1, 0)).astype(BF16), "context")
    residual = source + mixed_out.astype(F32)
    factor_two = rms_factor(residual)
    normed_two = (residual * factor_two * gain_ffn).astype(BF16)

    rows_all = gather(normed_two, "expert")
    logits = dot(rows_all, router_w, (1, 0))
    ids = jnp.arange(experts_all, dtype=jnp.int32)
    chosen = jnp.any(routes_all[:, :, None] == ids, axis=1)
    top = jnp.max(jnp.where(chosen, logits, -jnp.inf), axis=-1, keepdims=True)
    raised = jnp.where(chosen, jnp.exp(jnp.where(chosen, logits - top, 0.0)), 0.0)
    weights_all = raised / jnp.sum(raised, axis=-1, keepdims=True)
    weights_here = lax.dynamic_slice_in_dim(
        weights_all, my_group * local_experts, local_experts, axis=1
    )
    out_part = 0.0
    row_part = 0.0
    gate_grads, grads = [], []
    for e in range(local_experts):
        weight = weights_here[:, e : e + 1]
        gate_pre = dot(rows_all, w_gate[e], (1, 0))
        up_pre = dot(rows_all, w_up[e], (1, 0))
        sigmoid = jax.nn.sigmoid(gate_pre)
        activated = gate_pre * sigmoid
        hidden = activated * up_pre
        hidden_low = (weight * hidden).astype(BF16)
        out_part = out_part + dot(hidden_low, w_down[e], (1, 0))
        hidden_grad = dot(upstream_all, w_down[e], (1, 1))
        gate_grads.append(jnp.sum(hidden * hidden_grad, axis=-1))
        hidden_grad = hidden_grad * weight
        gate_pre_grad = (hidden_grad * up_pre * sigmoid * (1.0 + gate_pre * (1.0 - sigmoid))).astype(
            BF16
        )
        up_pre_grad = (hidden_grad * activated).astype(BF16)
        row_part = (
            row_part + dot(gate_pre_grad, w_gate[e], (1, 1)) + dot(up_pre_grad, w_up[e], (1, 1))
        )
        local_grads = (
            dot(rows_all, gate_pre_grad, (0, 0)).astype(BF16),
            dot(rows_all, up_pre_grad, (0, 0)).astype(BF16),
            dot(hidden_low, upstream_all, (0, 0)).astype(BF16),
        )
        grads.append(lax.psum(local_grads, ("context", "dp")))
    expert_grads = [jnp.stack([g[i].astype(F32) for g in grads]) for i in range(3)]

    row_back = scatter_sum(row_part.astype(BF16), "expert").astype(F32)
    gate_grad = jnp.stack(gate_grads, axis=1).reshape(groups, tokens, local_experts)
    gate_grad = lax.all_to_all(gate_grad, "expert", split_axis=0, concat_axis=0, tiled=True)
    gate_grad = gate_grad.transpose(1, 0, 2).reshape(tokens, experts_all)
    produced_sum = scatter_sum(out_part.astype(BF16), "expert").astype(F32)
    hidden_out = (residual + produced_sum).astype(BF16)[None]

    upstream = out_grad[0].astype(F32)
    weights_own = lax.dynamic_slice_in_dim(weights_all, my_group * tokens, tokens, axis=0)
    weighted = jnp.sum(weights_own * gate_grad, axis=-1, keepdims=True)
    logit_grad = (weights_own * (gate_grad - weighted)).astype(BF16)
    router_grad = dot(normed_two, logit_grad, (0, 0))
    normed_two_grad = dot(logit_grad, router_w, (1, 1)) + row_back
    residual_part, ffn_gain_grad = norm_back(normed_two_grad, residual, factor_two, gain_ffn)
    residual_grad = upstream + residual_part

    attn_grad = gather(residual_grad.astype(BF16), "context")
    out_w_grad = dot(mixed_low, attn_grad, (0, 0))
    mixed_grad = dot(attn_grad, out_w, (1, 1)).astype(BF16).reshape(length, per, HDIM)
    scores = (
        jnp.einsum("qhd,khd->hqk", query_low, key_low, preferred_element_type=F32) * score_scale
    )
    probs = jnp.exp(scores - logsum)
    prob_grad = jnp.einsum("qhd,khd->hqk", mixed_grad, value_low, preferred_element_type=F32)
    row_shift = jnp.sum(probs * prob_grad, axis=-1, keepdims=True)
    score_grad = (probs * (prob_grad - row_shift)).astype(BF16)
    query_rot = (
        jnp.einsum("hqk,khd->qhd", score_grad, key_low, preferred_element_type=F32) * score_scale
    )
    key_rot = (
        jnp.einsum("hqk,qhd->khd", score_grad, query_low, preferred_element_type=F32) * score_scale
    )
    value_grad = jnp.einsum(
        "hqk,qhd->khd", probs.astype(BF16), mixed_grad, preferred_element_type=F32
    )
    query_back = rotate(query_rot, cosine, -sine_part)
    key_back = rotate(key_rot, cosine, -sine_part)
    sums = jnp.stack(
        [
            jnp.sum(query_back * gain_query * query_raw, axis=(1, 2)),
            jnp.sum(key_back * gain_key * key_raw, axis=(1, 2)),
        ],
        axis=0,
    )
    sums = lax.psum(sums, "context") / width
    query_grad = (
        factor_query * query_back * gain_query
        - query_raw * factor_query**3 * sums[0][:, None, None]
    )
    key_grad = (
        factor_key * key_back * gain_key - key_raw * factor_key**3 * sums[1][:, None, None]
    )
    q_gain_grad = jnp.sum(query_back * query_raw * factor_query, axis=0)
    k_gain_grad = jnp.sum(key_back * key_raw * factor_key, axis=0)
    qkv_grad = jnp.concatenate(
        [g.reshape(length, local).astype(BF16) for g in (query_grad, key_grad, value_grad)], axis=1
    )
    normed_grad = scatter_sum(dot(qkv_grad, qkv_w, (1, 1)).astype(BF16), "context").astype(F32)
    source_part, attn_gain_grad = norm_back(normed_grad, source, factor_one, gain_attn)
    input_grad = (residual_grad + source_part).astype(BF16)[None]

    qkv_w_grad = dot(normed, qkv_grad, (0, 0)).astype(BF16)
    qkv_w_grad = lax.psum(scatter_sum(qkv_w_grad, "expert"), "dp")
    qkv_w_grad = lax.all_to_all(
        qkv_w_grad.reshape(context, rows, 3 * local),
        "context",
        split_axis=0,
        concat_axis=0,
        tiled=True,
    ).astype(F32)
    qkv_w_grad = qkv_w_grad.reshape(context, rows, 3, per, HDIM).transpose(2, 1, 3, 0, 4)
    qkv_w_grad = qkv_w_grad.reshape(3, rows, width)
    if whole_heads:
        out_w_grad = lax.psum(scatter_sum(out_w_grad.astype(BF16), "expert"), "dp").astype(F32)
        head_gains = jnp.stack([q_gain_grad, k_gain_grad], axis=1)
        head_gains = lax.psum(scatter_sum(head_gains, "expert"), "dp")[0]
        q_gain_grad, k_gain_grad = head_gains[0], head_gains[1]
    else:
        spread = jnp.zeros((per, context, HDIM, width), BF16)
        spread = lax.dynamic_update_slice_in_dim(
            spread, out_w_grad.astype(BF16).reshape(per, 1, HDIM, width), my_context, 1
        )
        spread = scatter_sum(spread.reshape(width, width), ("expert", "context"))
        out_w_grad = lax.psum(spread, "dp").astype(F32)
        head_gains = jnp.stack([q_gain_grad, k_gain_grad], axis=2)
        spread = jnp.zeros((per, context, HDIM, 2), F32)
        spread = lax.dynamic_update_slice_in_dim(spread, head_gains[:, None], my_context, 1)
        spread = scatter_sum(spread.reshape(width, 2), ("expert", "context"))
        head_gains = lax.psum(spread, "dp")
        q_gain_grad, k_gain_grad = head_gains[:, 0], head_gains[:, 1]
    small_grad = jnp.concatenate(
        [router_grad, attn_gain_grad[:, None], ffn_gain_grad[:, None]], axis=1
    )
    small_grad = lax.psum(scatter_sum(small_grad, ("expert", "context")), "dp")
    return (
        hidden_out,
        input_grad,
        small_grad[:, experts_all],
        qkv_w_grad[0],
        qkv_w_grad[1],
        qkv_w_grad[2],
        q_gain_grad,
        k_gain_grad,
        out_w_grad,
        small_grad[:, experts_all + 1],
        small_grad[:, :experts_all],
        expert_grads[0],
        expert_grads[1],
        expert_grads[2],
    )


def solution(mesh):
    tokens = P(("expert", "dp"), "context", None)
    vector = P(("expert", "context"))
    matrix = P(("expert", "context"), None)
    expert = P("expert", None, None)
    in_specs = (
        tokens,
        tokens,
        tokens,
        vector,
        matrix,
        matrix,
        matrix,
        vector,
        vector,
        matrix,
        vector,
        matrix,
        expert,
        expert,
        expert,
    )
    out_specs = (
        tokens,
        tokens,
        vector,
        matrix,
        matrix,
        matrix,
        vector,
        vector,
        matrix,
        vector,
        matrix,
        expert,
        expert,
        expert,
    )
    return jax.shard_map(body, mesh=mesh, in_specs=in_specs, out_specs=out_specs, check_vma=False)
```

```python
import functools

import jax
import jax.numpy as jnp
from jax import lax
from jax.experimental import pallas as pl
from jax.experimental.pallas import tpu as pltpu
from jax.sharding import PartitionSpec as P

HEADS = 16
HDIM = 128
CHUNK = 256
ROWS = 1024
PIECES = 4

epsilon = 1e-06
rope_base = 10000.0
F32 = jnp.float32
BF16 = jnp.bfloat16
MIB = 1024 * 1024


def dot(left, right, contract):
    return lax.dot_general(
        left, right, (((contract[0],), (contract[1],)), ((), ())), preferred_element_type=F32
    )


def add_low(left, right):
    return (left.astype(F32) + right.astype(F32)).astype(BF16)


def total_low(terms):
    return functools.reduce(lambda a, b: a + b, [t.astype(F32) for t in terms]).astype(BF16)


FIRST = (("dp", 1), ("context", 2))
SECOND = (("context", 2), ("dp", 1))


class Order:
    def __init__(self):
        self.last = None

    def tie(self, values):
        if self.last is None:
            return values
        return lax.optimization_barrier((values, self.last))[0]

    def did(self, result):
        self.last = result

    def run(self, step, first, *rest):
        result = step(self.tie(first), *rest)
        self.did(result)
        return result


def rms_factor(values):
    return lax.rsqrt(jnp.mean(values * values, axis=-1, keepdims=True) + epsilon)


def norm_back(grad_out, values, factor, gain_vector):
    scaled = grad_out * gain_vector
    grad_in = factor * scaled - values * factor**3 * jnp.mean(
        scaled * values, axis=-1, keepdims=True
    )
    gain_grad = jnp.sum(grad_out * values * factor, axis=0)
    return (grad_in, gain_grad)


def rotate(values, cosine, sine_part):
    first_half = values[..., : HDIM // 2]
    second_half = values[..., HDIM // 2 :]
    return jnp.concatenate(
        [
            first_half * cosine - second_half * sine_part,
            second_half * cosine + first_half * sine_part,
        ],
        axis=-1,
    )


def swap(values, axis, bit):
    return lax.ppermute(values, axis, [(i, i ^ bit) for i in range(lax.axis_size(axis))])


def shift(values, by):
    n = lax.axis_size("expert")
    return lax.ppermute(values, "expert", [(i, (i + by) % n) for i in range(n)])


def context_gather(own):
    far = swap(own, "context", 2)
    near = swap(own, "context", 1)
    return [own, near, far, swap(far, "context", 1)]


def context_sum(blocks):
    got = swap(jnp.stack([blocks[1], blocks[3]]), "context", 1)
    far = swap(add_low(blocks[2], got[1]), "context", 2)
    return blocks[0].astype(F32) + got[0].astype(F32) + far.astype(F32)


def context_total(terms):
    got = swap(terms, "context", 1)
    terms = terms + jnp.stack([got[:, s ^ 1] for s in range(4)], axis=1)
    got = swap(terms, "context", 2)
    return terms + jnp.stack([got[:, s ^ 2] for s in range(4)], axis=1)


def ring_gather(own):
    held = [own]
    for _ in range(lax.axis_size("expert") - 1):
        held.append(shift(held[-1], 1))
    return held


def ring_sum(blocks, combine):
    n = len(blocks)
    total = blocks[1 % n]
    for s in range(2, n + 1):
        total = combine(blocks[s % n], shift(total, 1))
    return total


def take(blocks, index):
    return jnp.stack([lax.dynamic_index_in_dim(blocks, i, 0, keepdims=False) for i in index])


def rows_kernel(
    first,
    at_ref,
    x_ref,
    u_ref,
    mask_ref,
    router_ref,
    wg_ref,
    wu_ref,
    wd_ref,
    out_ref,
    row_ref,
    gate_ref,
    weights_ref,
    turned_ref,
    both_ref,
    hidden_ref,
    out_acc,
    row_acc,
    lanes,
    both_w,
):
    e, step = pl.program_id(0), pl.program_id(1)
    start = jnp.logical_and(e == 0, step == 0)
    rows, width = x_ref.shape
    chunk = wg_ref.shape[1]
    lane = lax.broadcasted_iota(jnp.int32, (rows, 128), 1)

    @pl.when(start)
    def _():
        out_acc[...] = jnp.zeros_like(out_acc)
        row_acc[...] = jnp.zeros_like(row_acc)
        gate_ref[...] = jnp.zeros_like(gate_ref)
        turned_ref[...] = x_ref[...].T
        logits = dot(x_ref[...], router_ref[...], (1, 0))
        chosen = mask_ref[...] > 0.5
        top = jnp.max(jnp.where(chosen, logits, -1e30), axis=-1, keepdims=True)
        raised = jnp.where(chosen, jnp.exp(jnp.where(chosen, logits - top, 0.0)), 0.0)
        weights_ref[...] = raised / jnp.sum(raised, axis=-1, keepdims=True)

    @pl.when(step == 0)
    def _():
        lanes[...] = jnp.zeros_like(lanes)

    both_w[:, :chunk] = wg_ref[...]
    both_w[:, chunk:] = wu_ref[...]
    weight = jnp.sum(
        jnp.where(lane == at_ref[0] + first + e, weights_ref[...], 0.0), axis=-1, keepdims=True
    )
    pre = dot(x_ref[...], both_w[...], (1, 0))
    gate_pre, up_pre = pre[:, :chunk], pre[:, chunk:]
    hidden_grad = dot(u_ref[...], wd_ref[...], (1, 1))
    sigmoid = 1.0 / (1.0 + jnp.exp(-gate_pre))
    activated = gate_pre * sigmoid
    hidden = activated * up_pre
    part = hidden * hidden_grad
    total = part[:, :128]
    for j in range(1, chunk // 128):
        total = total + part[:, j * 128 : (j + 1) * 128]
    lanes[...] += total
    hidden_low = (weight * hidden).astype(BF16)
    hidden_grad = weight * hidden_grad
    gate_low = (hidden_grad * up_pre * (sigmoid + activated * (1.0 - sigmoid))).astype(BF16)
    up_low = (hidden_grad * activated).astype(BF16)
    hidden_ref[...] = hidden_low
    both_ref[:, :chunk] = gate_low
    both_ref[:, chunk:] = up_low
    out_acc[...] += dot(hidden_low, wd_ref[...], (1, 0))
    row_acc[...] += dot(both_ref[...], both_w[...], (1, 1))

    @pl.when(step == pl.num_programs(1) - 1)
    def _():
        sums = jnp.sum(lanes[...], axis=-1, keepdims=True)
        gate_ref[...] += jnp.where(lane == first + e, sums, 0.0)
        out_ref[...] = out_acc[...].astype(BF16)
        row_ref[...] = row_acc[...].astype(BF16)


def run_rows(at, first, count, x, u, mask, router, w_gate, w_up, w_down):
    rows, width = x.shape
    ff = w_gate.shape[2]
    steps = ff // CHUNK

    def whole(shape):
        return pl.BlockSpec(
            shape, lambda e, s, a: (0,) * len(shape), pipeline_mode=pl.Buffered(1)
        )

    return pl.pallas_call(
        functools.partial(rows_kernel, first),
        grid_spec=pltpu.PrefetchScalarGridSpec(
            num_scalar_prefetch=1,
            grid=(count, steps),
            in_specs=[
                whole((rows, width)),
                whole((rows, width)),
                whole((rows, 128)),
                whole((width, 128)),
                pl.BlockSpec((None, width, CHUNK), lambda e, s, a: (first + e, 0, s)),
                pl.BlockSpec((None, width, CHUNK), lambda e, s, a: (first + e, 0, s)),
                pl.BlockSpec((None, CHUNK, width), lambda e, s, a: (first + e, s, 0)),
            ],
            out_specs=[
                whole((rows, width)),
                whole((rows, width)),
                whole((rows, 128)),
                whole((rows, 128)),
                whole((width, rows)),
                pl.BlockSpec((None, None, rows, 2 * CHUNK), lambda e, s, a: (e, s, 0, 0)),
                pl.BlockSpec((None, None, rows, CHUNK), lambda e, s, a: (e, s, 0, 0)),
            ],
            scratch_shapes=[
                pltpu.VMEM((rows, width), F32),
                pltpu.VMEM((rows, width), F32),
                pltpu.VMEM((rows, 128), F32),
                pltpu.VMEM((width, 2 * CHUNK), BF16),
            ],
        ),
        out_shape=[
            jax.ShapeDtypeStruct((rows, width), BF16),
            jax.ShapeDtypeStruct((rows, width), BF16),
            jax.ShapeDtypeStruct((rows, 128), F32),
            jax.ShapeDtypeStruct((rows, 128), F32),
            jax.ShapeDtypeStruct((width, rows), BF16),
            jax.ShapeDtypeStruct((count, steps, rows, 2 * CHUNK), BF16),
            jax.ShapeDtypeStruct((count, steps, rows, CHUNK), BF16),
        ],
        compiler_params=pltpu.CompilerParams(vmem_limit_bytes=56 * MIB),
        cost_estimate=pl.CostEstimate(
            flops=12 * rows * width * ff * count,
            bytes_accessed=6 * width * ff * count,
            transcendentals=rows * ff * count,
        ),
        name="rows",
    )(at, x, u, mask, router, w_gate, w_up, w_down)


def grads_kernel(sizes, bits_ref, *refs):
    n = len(sizes)
    turned, ups, boths, hiddens = (refs[i * n : (i + 1) * n] for i in range(4))
    send_ref, keep_ref, x_all, u_all, both, hidden = refs[4 * n :]
    step, steps = pl.program_id(0), pl.num_programs(0)
    width = x_all.shape[0]
    chunk = hidden.shape[1]

    spans, at = [], 0
    for size in sizes:
        spans.append(slice(at, at + size))
        at += size

    @pl.when(step == 0)
    def _():
        for span, t, u in zip(spans, turned, ups):
            x_all[:, span] = t[...]
            u_all[span, :] = u[...]

    for span, b, h in zip(spans, boths, hiddens):
        both[span, :] = b[...]
        hidden[span, :] = h[...]
    hidden_turned = hidden[...].T
    piece_rows = width // PIECES

    def store(ref):
        mask = jnp.where(step % 2 == 0, bits_ref[1], bits_ref[2])
        for p in range(PIECES):
            place = p ^ mask
            r = slice(p * piece_rows, (p + 1) * piece_rows)
            got = dot(x_all[r, :], both[...], (1, 0)).astype(BF16)
            ref[place, 0] = got[:, :chunk]
            ref[place, 1] = got[:, chunk:]
            down = dot(hidden_turned, u_all[:, r], (1, 0)).astype(BF16)
            for j in range(piece_rows // chunk):
                ref[place, 2, j * chunk : (j + 1) * chunk, :] = down[:, j * chunk : (j + 1) * chunk]

    @pl.when(step < steps // 2)
    def _():
        store(send_ref.at[0])

    @pl.when(step >= steps // 2)
    def _():
        store(keep_ref.at[0])


def run_grads(bits, segments):
    turned, ups, boths, hiddens, places = zip(*segments)
    width = turned[0].shape[0]
    sizes = tuple(u.shape[0] for u in ups)
    total = sum(sizes)
    steps = boths[0].shape[1]
    half = steps // 2
    piece_rows = width // PIECES

    def chunk_at(s, b):
        return ((1 - s // half) ^ b[0]) * half + s % half

    def whole(shape):
        return pl.BlockSpec(shape, lambda s, b: (0, 0), pipeline_mode=pl.Buffered(1))

    def chunked(size, columns, place):
        return pl.BlockSpec(
            (None, None, size, columns), lambda s, b: (place, chunk_at(s, b), 0, 0)
        )

    grads = (1, PIECES, 3, piece_rows, CHUNK)
    grads_out = jax.ShapeDtypeStruct((half,) + grads[1:], BF16)
    return pl.pallas_call(
        functools.partial(grads_kernel, sizes),
        grid_spec=pltpu.PrefetchScalarGridSpec(
            num_scalar_prefetch=1,
            grid=(steps,),
            in_specs=[whole((width, size)) for size in sizes]
            + [whole((size, width)) for size in sizes]
            + [chunked(size, 2 * CHUNK, p) for size, p in zip(sizes, places)]
            + [chunked(size, CHUNK, p) for size, p in zip(sizes, places)],
            out_specs=[
                pl.BlockSpec(grads, lambda s, b: (jnp.minimum(s, half - 1), 0, 0, 0, 0)),
                pl.BlockSpec(grads, lambda s, b: (jnp.maximum(s - half, 0), 0, 0, 0, 0)),
            ],
            scratch_shapes=[
                pltpu.VMEM((width, total), BF16),
                pltpu.VMEM((total, width), BF16),
                pltpu.VMEM((total, 2 * CHUNK), BF16),
                pltpu.VMEM((total, CHUNK), BF16),
            ],
        ),
        out_shape=[grads_out, grads_out],
        compiler_params=pltpu.CompilerParams(vmem_limit_bytes=56 * MIB),
        cost_estimate=pl.CostEstimate(
            flops=6 * total * width * steps * CHUNK,
            bytes_accessed=6 * width * steps * CHUNK + 8 * total * width,
            transcendentals=0,
        ),
        name="grads",
    )(bits, *turned, *ups, *boths, *hiddens)


class Summed:
    def __init__(self, order, send, keep):
        self.order, self.keep = order, keep
        self.ahead = ["halves", "quarters", "finals", "spread", "cross"]
        self.got = swap(send, "context", 1)

    def reach(self, name):
        while name in self.ahead:
            getattr(self, self.ahead.pop(0))()

    def halves(self):
        self.kept, self.coming = [], []
        for path in range(2):
            kept, got = self.keep[path], self.got[path]
            away = self.order.run(add_low, kept[2:], got[2:])
            self.coming.append(swap(away, *FIRST[path]))
        for path in range(2):
            self.kept.append(self.order.run(add_low, self.keep[path, :2], self.got[path, :2]))

    def quarters(self):
        kept, self.kept, coming, self.coming = self.kept, [], self.coming, []
        for path in range(2):
            away = self.order.run(add_low, kept[path][1], coming[path][1])
            self.coming.append(swap(away, *SECOND[path]))
        for path in range(2):
            self.kept.append(self.order.run(add_low, kept[path][0], coming[path][0]))

    def finals(self):
        self.own = []
        for path in range(2):
            final = self.order.run(add_low, self.kept[path], self.coming[path])
            self.own.append([final, swap(final, *SECOND[path]), swap(final, *FIRST[path])])

    def spread(self):
        for path in range(2):
            beside = self.order.tie(self.own[path][1])
            self.own[path].append(swap(beside, *FIRST[path]))
        self.other = [[swap(p, "context", 1) for p in path[:2]] for path in self.own]

    def cross(self):
        for path in range(2):
            ready = [self.order.tie(p) for p in self.own[path][2:]]
            self.other[path] += [swap(p, "context", 1) for p in ready]

    def place(self, bits, e, outs, shapes):
        pieces = [p for half in (self.own, self.other) for path in half for p in path]
        outs = place_grads(self.order.tie(bits), e, pieces, outs, shapes)
        self.order.did(outs[2])
        return outs


def place_kernel(e, first, bits_ref, *refs):
    ins = refs[:16]
    outs = refs[16:19] if first else refs[19:22]
    low, wide, in_sem, out_sem = refs[-4:]
    rows = low.shape[2]

    def fetch(i):
        return pltpu.make_async_copy(ins[i], low.at[i % 2], in_sem.at[i % 2])

    def drain(i):
        core, path, place = i // 8, i // 4 % 2, i % 4
        chunk = (core ^ bits_ref[0]) * 2 + path
        piece = place ^ bits_ref[1 + path]
        columns = pl.ds(pl.multiple_of(chunk * CHUNK, CHUNK), CHUNK)
        copies = []
        for k in range(2):
            copies.append(
                pltpu.make_async_copy(
                    wide.at[i % 2, k],
                    outs[k].at[e, pl.ds(pl.multiple_of(piece * rows, rows), rows), columns],
                    out_sem.at[i % 2, k],
                )
            )
        for j in range(rows // CHUNK):
            across = pl.ds(pl.multiple_of(piece * rows + j * CHUNK, CHUNK), CHUNK)
            copies.append(
                pltpu.make_async_copy(
                    wide.at[i % 2, 2, pl.ds(j * CHUNK, CHUNK)],
                    outs[2].at[e, columns, across],
                    out_sem.at[i % 2, 2 + j],
                )
            )
        return copies

    fetch(0).start()
    for i in range(16):
        if i + 1 < 16:
            fetch(i + 1).start()
        fetch(i).wait()
        if i >= 2:
            for copy in drain(i - 2):
                copy.wait()
        for k in range(3):

            @pl.loop(0, rows // 64)
            def _(t):
                r = pl.ds(pl.multiple_of(t * 64, 64), 64)
                wide[i % 2, k, r, :] = low[i % 2, k, r, :].astype(F32)

        for copy in drain(i):
            copy.start()
    for i in (14, 15):
        for copy in drain(i):
            copy.wait()


def place_grads(bits, e, pieces, outs, shapes):
    first = outs is None
    rows = pieces[0].shape[1]
    anywhere = pl.BlockSpec(memory_space=pl.ANY)
    operands = list(pieces) + ([] if first else list(outs))
    return pl.pallas_call(
        functools.partial(place_kernel, e, first),
        grid_spec=pltpu.PrefetchScalarGridSpec(
            num_scalar_prefetch=1,
            grid=(1,),
            in_specs=[anywhere] * len(operands),
            out_specs=[anywhere] * 3,
            scratch_shapes=[
                pltpu.VMEM((2, 3, rows, CHUNK), BF16),
                pltpu.VMEM((2, 3, rows, CHUNK), F32),
                pltpu.SemaphoreType.DMA((2,)),
                pltpu.SemaphoreType.DMA((2, 2 + rows // CHUNK)),
            ],
        ),
        out_shape=[jax.ShapeDtypeStruct(s, F32) for s in shapes],
        input_output_aliases={} if first else {17: 0, 18: 1, 19: 2},
        compiler_params=pltpu.CompilerParams(vmem_limit_bytes=16 * MIB),
        cost_estimate=pl.CostEstimate(
            flops=0, bytes_accessed=16 * 9 * rows * CHUNK * 2, transcendentals=0
        ),
        name="place",
    )(bits, *operands)


def body(
    hidden_in,
    out_grad,
    routes,
    attn_gain,
    w_query,
    w_key,
    w_value,
    q_gain,
    k_gain,
    w_out,
    ffn_gain,
    w_router,
    w_gate,
    w_up,
    w_down,
):
    groups = lax.axis_size("expert")
    context = lax.axis_size("context")
    my_group = lax.axis_index("expert")
    my_context = lax.axis_index("context")
    my_dp = lax.axis_index("dp")
    tokens = hidden_in.shape[1]
    width = hidden_in.shape[2]
    rows = w_query.shape[0]
    local_experts = w_gate.shape[0]
    experts_all = w_router.shape[1]
    length = tokens * context
    per = HEADS // context
    local = per * HDIM
    score_scale = HDIM ** (-0.5)
    core, side = my_context % 2, my_context // 2
    bits = jnp.stack([core, my_dp * 2 + side, side * 2 + my_dp]).astype(jnp.int32)
    ring = [(my_group - s) % groups for s in range(groups)]
    members = [my_context ^ s for s in range(context)]

    def half_columns(weight):
        split = weight.reshape(rows, 2, per // 2, context, HDIM)
        split = lax.dynamic_index_in_dim(split, my_dp, 1, keepdims=False)
        return split.transpose(2, 0, 1, 3).reshape(context, rows, local // 2)

    columns = jnp.concatenate([half_columns(w) for w in (w_query, w_key, w_value)], axis=2)
    pieces = [lax.dynamic_index_in_dim(columns, m, 0, keepdims=False) for m in members]
    pieces = [pieces[0]] + [swap(pieces[s], "context", s) for s in range(1, context)]
    half_w = take(jnp.stack(pieces), members).reshape(context * rows, 3 * local // 2)
    hidden_all = lax.optimization_barrier((hidden_in[0], half_w))[0]
    hidden_all = jnp.concatenate(context_gather(hidden_all), axis=0)
    small = jnp.concatenate(
        [attn_gain[None], q_gain[None], k_gain[None], ffn_gain[None], w_router.T], axis=0
    )
    small = take(jnp.stack(context_gather(small)), members)
    small = take(jnp.stack(ring_gather(small)), ring)
    small_all = small.transpose(2, 0, 1, 3).reshape(4 + experts_all, width)
    routes_ring = ring_gather(routes[0])
    halves = ring_gather(half_w)
    others = [swap(h, "dp", 1) for h in halves]
    qkv_w = jnp.concatenate(
        [jnp.concatenate(halves, axis=0), jnp.concatenate(others, axis=0)], axis=1
    )
    heads = [my_dp * 2, my_dp * 2 + 1, (1 - my_dp) * 2, (1 - my_dp) * 2 + 1]
    whole_heads = rows == HDIM
    if whole_heads:
        held = lax.optimization_barrier((w_out, halves[-1]))[0]
        held = lax.all_gather(held, "expert", axis=0)
        out_w = take(held, heads).reshape(local, width)
    else:
        out_w = lax.all_gather(w_out, ("expert", "context"), axis=0, tiled=True)
        out_w = out_w.reshape(per, context, HDIM, width)
        out_w = lax.dynamic_index_in_dim(out_w, my_context, 1, keepdims=False)
        out_w = take(out_w, heads).reshape(local, width)
    upstream_all = lax.optimization_barrier((out_grad[0], halves[-1]))[0]
    upstream_all = lax.all_gather(upstream_all, "expert", axis=0)

    gain_attn = small_all[0].astype(F32)
    gain_ffn = small_all[3].astype(F32)
    router_w = small_all[4:]
    router_wide = jnp.pad(router_w.T, ((0, 0), (0, 128 - experts_all)))

    def mine(vector):
        table = vector.reshape(per, context, HDIM)
        table = lax.dynamic_index_in_dim(table, my_context, 1, keepdims=False)
        return take(table, heads).astype(F32)

    gain_query, gain_key = mine(small_all[1]), mine(small_all[2])
    block = width // groups

    def to_ring(values):
        parts = [lax.dynamic_slice_in_dim(values, m * block, block, axis=1) for m in ring]
        return jnp.concatenate(parts, axis=1)

    source_all = hidden_all.astype(F32)
    factor_all = rms_factor(source_all)
    normed = to_ring((source_all * factor_all * gain_attn).astype(BF16))
    source = hidden_in[0].astype(F32)
    factor_one = rms_factor(source)
    qkv = dot(normed, qkv_w, (1, 0)).reshape(length, 2, 3, local // 2)
    query_raw = qkv[:, :, 0].reshape(length, per, HDIM)
    key_raw = qkv[:, :, 1].reshape(length, per, HDIM)
    value_low = qkv[:, :, 2].astype(BF16).reshape(length, per, HDIM)

    def slots(query, key):
        return jnp.stack([jnp.sum(v, axis=(1, 2)).reshape(context, tokens) for v in (query, key)])

    def per_row(values):
        return values.reshape(length)[:, None, None]

    squares = context_total(slots(query_raw * query_raw, key_raw * key_raw))
    factors = lax.rsqrt(squares / width + epsilon)
    factor_query, factor_key = per_row(factors[0]), per_row(factors[1])
    starts = jnp.stack([m * tokens for m in members])
    positions = (starts[:, None] + jnp.arange(tokens, dtype=jnp.int32)).reshape(length).astype(F32)
    frequency = rope_base ** (-jnp.arange(HDIM // 2, dtype=F32) * 2.0 / HDIM)
    angles = positions[:, None] * frequency[None, :]
    cosine = jnp.cos(angles)[:, None, :]
    sine_part = jnp.sin(angles)[:, None, :]
    query_low = rotate(query_raw * factor_query * gain_query, cosine, sine_part).astype(BF16)
    key_low = rotate(key_raw * factor_key * gain_key, cosine, sine_part).astype(BF16)
    scores = (
        jnp.einsum("qhd,khd->hqk", query_low, key_low, preferred_element_type=F32) * score_scale
    )
    score_max = jnp.max(scores, axis=-1, keepdims=True)
    denominator = jnp.sum(jnp.exp(scores - score_max), axis=-1, keepdims=True)
    logsum = score_max + jnp.log(denominator)
    probs = jnp.exp(scores - logsum)
    mixed_low = (
        jnp.einsum("hqk,khd->qhd", probs.astype(BF16), value_low, preferred_element_type=F32)
        .reshape(length, local)
        .astype(BF16)
    )
    mixed_out = dot(mixed_low, out_w, (1, 0)).astype(BF16).reshape(context, tokens, width)
    residual = source + context_sum([mixed_out[s] for s in range(context)])
    factor_two = rms_factor(residual)
    normed_two = (residual * factor_two * gain_ffn).astype(BF16)

    ids = jnp.arange(128, dtype=jnp.int32)
    masks = [jnp.any(r[:, :, None] == ids, axis=1).astype(F32) for r in routes_ring]
    at = jnp.reshape(my_group * local_experts, (1,)).astype(jnp.int32)
    order = Order()

    def upstream_of(slot):
        return lax.dynamic_index_in_dim(upstream_all, ring[slot], 0, keepdims=False)

    def rows_of(first, count, x, u, mask):
        result = run_rows(order.tie(at), first, count, x, u, mask, router_wide, w_gate, w_up, w_down)
        order.did(result[0])
        return result

    near = [[(0, local_experts)], [(0, local_experts)]]
    if local_experts == 4:
        near = [[(0, 2), (2, 2)]] * 2
    blocks = [normed_two, shift(normed_two, 1)]
    segments = [([0], []), ([1], [])]
    ups = [out_grad[0], upstream_of(1)]
    for slot in range(2):
        for i, (first, count) in enumerate(near[slot]):
            result = rows_of(first, count, blocks[slot], ups[slot], masks[slot])
            segments[slot][1].append((first, count, result))
            if slot == 0 or i == 0:
                if len(blocks) < groups:
                    held = order.tie(blocks[-1])
                    order.did(held)
                    blocks.append(shift(held, 1))
    while len(blocks) < groups:
        blocks.append(shift(blocks[-1], 1))
    far = []
    for slot in range(2, groups, 2):
        pair = [slot, slot + 1]
        x, u, mask = (
            jnp.concatenate(v, axis=0)
            for v in (
                [blocks[s] for s in pair],
                [upstream_of(s) for s in pair],
                [masks[s] for s in pair],
            )
        )
        far.append((x, u, mask))
        segments.append((pair, []))
        ups.append(u)

    def segment_of(segment, e):
        for first, count, result in segments[segment][1]:
            if first <= e < first + count:
                return (result[4], ups[segment], result[5], result[6], e - first)

    summed = []

    def advance(events):
        for e, name in events:
            if e < len(summed):
                summed[e].reach(name)

    during = {
        1: ([(0, "halves")], []),
        2: ([(0, "quarters"), (1, "halves")], [(0, "finals")]),
        3: ([(2, "halves")], [(1, "quarters")]),
    }
    for e in range(local_experts):
        for i, (x, u, mask) in enumerate(far):
            segments[2 + i][1].append((e, 1, rows_of(e, 1, x, u, mask)))
        advance(during.get(e, ([], []))[0])
        bunches = [[0, 1, 2]] + [[s, s + 1] for s in range(3, len(segments), 2)]
        results = []
        for bunch in bunches:
            got = run_grads(order.tie(bits), [segment_of(s, e) for s in bunch if s < len(segments)])
            order.did(got[0])
            results.append(got)
        send, keep = (
            total_low([r[i] for r in results]) if len(results) > 1 else results[0][i]
            for i in range(2)
        )
        summed.append(Summed(order, send, keep))
        advance(during.get(e, ([], []))[1])

    def total_of(slot, index):
        for pair, calls in segments:
            if slot in pair:
                at_row = pair.index(slot) * tokens
                parts = [result[index][at_row : at_row + tokens] for _, _, result in calls]
                return total_low(parts)

    def hop(index, total, slot):
        term = total_of(slot % groups, index)
        return order.run(add_low, term, shift(total, 1))

    gate_grad = [
        functools.reduce(
            lambda a, b: a + b,
            [result[2][pair.index(s) * tokens : (pair.index(s) + 1) * tokens] for _, _, result in calls],
        )
        for pair, calls in segments
        for s in pair
    ]
    gate_grad = [g[:, :local_experts].T for g in gate_grad]
    gate_grad = jnp.stack([gate_grad[0]] + [shift(gate_grad[s], -s) for s in range(1, groups)])
    gate_grad = take(gate_grad, [(g - my_group) % groups for g in range(groups)])
    gate_grad = gate_grad.reshape(experts_all, tokens).T

    row_total = total_of(1, 1)
    events = [
        [(3, "halves")],
        [(2, "quarters")],
        [(1, "finals")],
    ]
    for slot in range(2, groups + 1):
        row_total = hop(1, row_total, slot)
        advance(events[slot - 2] if slot - 2 < len(events) else [])
    row_back = row_total.astype(F32)

    upstream = out_grad[0].astype(F32)
    weights_own = segments[0][1][0][2][3][:, :experts_all]
    weighted = jnp.sum(weights_own * gate_grad, axis=-1, keepdims=True)
    logit_grad = (weights_own * (gate_grad - weighted)).astype(BF16)
    router_grad = dot(logit_grad, normed_two, (0, 0))
    normed_two_grad = dot(logit_grad, router_w, (1, 0)) + row_back
    residual_part, ffn_gain_grad = norm_back(normed_two_grad, residual, factor_two, gain_ffn)
    residual_grad = upstream + residual_part

    attn_grad = order.tie(residual_grad.astype(BF16))
    order.did(attn_grad)
    attn_grad = context_gather(attn_grad)
    advance([(3, "quarters"), (0, "spread")])
    out_total = hop(0, total_of(1, 0), 2)
    advance([(2, "finals")])
    attn_grad = order.tie(jnp.concatenate(attn_grad, axis=0))
    order.did(attn_grad)
    out_w_grad = dot(mixed_low, attn_grad, (0, 0)).astype(BF16).reshape(per, HDIM, width)
    mixed_grad = dot(attn_grad, out_w, (1, 1)).astype(BF16).reshape(length, per, HDIM)
    order.did(mixed_grad)
    for slot in range(3, groups + 1):
        out_total = hop(0, out_total, slot)
    hidden_out = (residual + out_total.astype(F32)).astype(BF16)[None]
    scores = (
        jnp.einsum("qhd,khd->hqk", query_low, key_low, preferred_element_type=F32) * score_scale
    )
    probs = jnp.exp(scores - logsum)
    prob_grad = jnp.einsum("qhd,khd->hqk", mixed_grad, value_low, preferred_element_type=F32)
    row_shift = jnp.sum(probs * prob_grad, axis=-1, keepdims=True)
    score_grad = (probs * (prob_grad - row_shift)).astype(BF16)
    query_rot = (
        jnp.einsum("hqk,khd->qhd", score_grad, key_low, preferred_element_type=F32) * score_scale
    )
    key_rot = (
        jnp.einsum("hqk,qhd->khd", score_grad, query_low, preferred_element_type=F32) * score_scale
    )
    value_grad = jnp.einsum(
        "hqk,qhd->khd", probs.astype(BF16), mixed_grad, preferred_element_type=F32
    )
    order.did(value_grad)
    advance([(3, "finals"), (0, "cross"), (1, "spread")])
    query_rot = order.tie(query_rot)
    query_back = rotate(query_rot, cosine, -sine_part)
    key_back = rotate(key_rot, cosine, -sine_part)
    sums = context_total(slots(query_back * gain_query * query_raw, key_back * gain_key * key_raw))
    sums = sums / width
    query_grad = (
        factor_query * query_back * gain_query - query_raw * factor_query**3 * per_row(sums[0])
    )
    key_grad = factor_key * key_back * gain_key - key_raw * factor_key**3 * per_row(sums[1])
    q_gain_grad = jnp.sum(query_back * query_raw * factor_query, axis=0)
    k_gain_grad = jnp.sum(key_back * key_raw * factor_key, axis=0)
    qkv_grad = jnp.stack(
        [
            g.astype(BF16).reshape(length, 2, local // 2)
            for g in (query_grad, key_grad, value_grad)
        ],
        axis=2,
    ).reshape(length, 3 * local)
    normed_grad = dot(qkv_grad, qkv_w, (1, 1)).astype(BF16).reshape(context, tokens, width)
    order.did(normed_grad)
    advance([(2, "spread"), (1, "cross"), (3, "spread")])
    normed_grad = context_sum([normed_grad[s] for s in range(context)])
    parts = [
        lax.dynamic_slice_in_dim(normed_grad, (my_group - m) % groups * block, block, axis=1)
        for m in range(groups)
    ]
    normed_grad = jnp.concatenate(parts, axis=1)
    source_part, attn_gain_grad = norm_back(normed_grad, source, factor_one, gain_attn)
    input_grad = (residual_grad + source_part).astype(BF16)[None]

    qkv_w_grad = dot(normed, qkv_grad, (0, 0)).astype(BF16)
    mine_w = ring_sum(list(qkv_w_grad.reshape(groups, context * rows, 3 * local)), add_low)
    flipped = mine_w.reshape(context, rows, 2, 3 * local // 2)
    got = swap(flipped, "dp", 1)
    mine_w = jnp.stack(
        [add_low(flipped[:, :, 0], got[:, :, 1]), add_low(flipped[:, :, 1], got[:, :, 0])], axis=1
    )
    pieces = [lax.dynamic_index_in_dim(mine_w, m, 0, keepdims=False) for m in members]
    pieces = [pieces[0]] + [swap(pieces[s], "context", s) for s in range(1, context)]
    dense = take(jnp.stack(pieces), members)
    dense = jnp.where(my_dp == 0, dense, dense[:, ::-1]).astype(F32)
    dense = dense.reshape(context, 2, rows, 3, per // 2, HDIM).transpose(3, 2, 1, 4, 0, 5)
    dense = dense.reshape(3, rows, width)
    if whole_heads:
        ordered = take(out_w_grad, [(m // 2 ^ my_dp) * 2 + m % 2 for m in ring])
        mine_out = ring_sum(list(ordered), add_low)
        out_w_grad = mine_out.astype(F32) + swap(mine_out, "dp", 1).astype(F32)
    else:
        spread = jnp.zeros((per, context, HDIM, width), BF16)
        for h in range(per):
            spread = lax.dynamic_update_slice(
                spread, out_w_grad[h][None, None], (heads[h], my_context, 0, 0)
            )
        spread = lax.psum_scatter(
            spread.reshape(width, width), ("expert", "context"), scatter_dimension=0, tiled=True
        )
        out_w_grad = lax.psum(spread, "dp").astype(F32)
    gains = jnp.zeros((2, per, context, HDIM), F32)
    for h in range(per):
        pair = jnp.stack([q_gain_grad[h], k_gain_grad[h]])[:, None, None]
        gains = lax.dynamic_update_slice(gains, pair, (0, heads[h], my_context, 0))
    small_grad = jnp.concatenate(
        [attn_gain_grad[None], ffn_gain_grad[None], gains.reshape(2, width), router_grad], axis=0
    )
    small_grad = small_grad.reshape(4 + experts_all, groups, context, rows).transpose(1, 2, 0, 3)
    small_grad = ring_sum(list(take(small_grad, ring)), lambda a, b: a + b)
    small_grad = take(small_grad, members)
    got = swap(jnp.stack([small_grad[1], small_grad[3]]), "context", 1)
    small_grad = small_grad[0] + got[0] + swap(small_grad[2] + got[1], "context", 2)
    small_grad = small_grad + swap(small_grad, "dp", 1)
    advance([(2, "cross"), (3, "cross")])
    expert_grads = None
    shapes = (w_gate.shape, w_up.shape, w_down.shape)
    for e in range(local_experts):
        summed[e].reach("cross")
        expert_grads = summed[e].place(bits, e, expert_grads, shapes)
    return (
        hidden_out,
        input_grad,
        small_grad[0],
        dense[0],
        dense[1],
        dense[2],
        small_grad[2],
        small_grad[3],
        out_w_grad,
        small_grad[1],
        small_grad[4:].T,
        expert_grads[0],
        expert_grads[1],
        expert_grads[2],
    )


def solution(mesh):
    tokens = P(("expert", "dp"), "context", None)
    vector = P(("expert", "context"))
    matrix = P(("expert", "context"), None)
    expert = P("expert", None, None)
    in_specs = (
        tokens,
        tokens,
        tokens,
        vector,
        matrix,
        matrix,
        matrix,
        vector,
        vector,
        matrix,
        vector,
        matrix,
        expert,
        expert,
        expert,
    )
    out_specs = (
        tokens,
        tokens,
        vector,
        matrix,
        matrix,
        matrix,
        vector,
        vector,
        matrix,
        vector,
        matrix,
        expert,
        expert,
        expert,
    )
    return jax.shard_map(body, mesh=mesh, in_specs=in_specs, out_specs=out_specs, check_vma=False)
```

```python
import functools
import math

import jax
import jax.numpy as jnp
from jax import lax
from jax.experimental import pallas as pl
from jax.experimental.pallas import tpu as pltpu
from jax.sharding import PartitionSpec as P

HEADS = 16
HDIM = 128
CHUNK = 256
ROWS = 1024
PIECES = 4

epsilon = 1e-06
rope_base = 10000.0
F32 = jnp.float32
BF16 = jnp.bfloat16
MIB = 1024 * 1024


def dot(left, right, contract):
    return lax.dot_general(
        left, right, (((contract[0],), (contract[1],)), ((), ())), preferred_element_type=F32
    )


def add_low(left, right):
    return (left.astype(F32) + right.astype(F32)).astype(BF16)


def total_low(terms):
    return functools.reduce(lambda a, b: a + b, [t.astype(F32) for t in terms]).astype(BF16)


FIRST = (("dp", 1), ("context", 2))
SECOND = (("context", 2), ("dp", 1))


class Order:
    def __init__(self):
        self.last = None

    def tie(self, values):
        if self.last is None:
            return values
        return lax.optimization_barrier((values, self.last))[0]

    def did(self, result):
        self.last = result

    def run(self, step, first, *rest):
        result = step(self.tie(first), *rest)
        self.did(result)
        return result


def rms_factor(values):
    return lax.rsqrt(jnp.mean(values * values, axis=-1, keepdims=True) + epsilon)


def norm_back(grad_out, values, factor, gain_vector):
    scaled = grad_out * gain_vector
    grad_in = factor * scaled - values * factor**3 * jnp.mean(
        scaled * values, axis=-1, keepdims=True
    )
    gain_grad = jnp.sum(grad_out * values * factor, axis=0)
    return (grad_in, gain_grad)


def half_turn(values):
    return pltpu.roll(values, HDIM // 2, 1)


def attend_kernel(
    q_ref, k_ref, v_ref, fq_ref, fk_ref, gq_ref, gk_ref, cos_ref, sin_ref,
    ql_ref, kl_ref, vl_ref, mixed_ref, logsum_ref,
):
    length = q_ref.shape[0]
    block = min(256, length)
    cosine, sine = cos_ref[...], sin_ref[...]
    query = q_ref[...] * fq_ref[...] * gq_ref[0]
    key = k_ref[...] * fk_ref[...] * gk_ref[0]
    ql_ref[...] = (query * cosine + half_turn(query) * sine).astype(BF16)
    kl_ref[...] = (key * cosine + half_turn(key) * sine).astype(BF16)
    value = v_ref[...].astype(BF16)
    vl_ref[...] = value
    turned = value.T
    for b in range(length // block):
        r = slice(b * block, (b + 1) * block)
        scores = dot(kl_ref[...], ql_ref[r, :], (1, 1)) * HDIM ** (-0.5)
        top = jnp.max(scores, axis=0, keepdims=True)
        raised = jnp.exp(scores - top)
        total = jnp.sum(raised, axis=0, keepdims=True)
        mixed = dot(turned, raised.astype(BF16), (1, 0)) / total
        mixed_ref[r, :] = mixed.T.astype(BF16)
        logsum_ref[0, :, r] = top + jnp.log(total)


def attend_back_kernel(
    ql_ref, kl_ref, vl_ref, grad_ref, logsum_ref, q_ref, k_ref, fq_ref, fk_ref, gq_ref, gk_ref,
    cos_ref, sin_ref, qb_ref, kb_ref, vg_ref, qs_ref, ks_ref, qg_ref, kg_ref, k_acc, v_acc, q_acc,
):
    length = ql_ref.shape[0]
    block = min(256, length)
    scale = HDIM ** (-0.5)

    @pl.when(pl.program_id(0) == 0)
    def _():
        qs_ref[...] = jnp.zeros_like(qs_ref)
        ks_ref[...] = jnp.zeros_like(ks_ref)

    for b in range(length // block):
        r = slice(b * block, (b + 1) * block)
        query, grad = ql_ref[r, :], grad_ref[r, :]
        scores = dot(kl_ref[...], query, (1, 1)) * scale
        probs = jnp.exp(scores - logsum_ref[0, :, r])
        prob_grad = dot(vl_ref[...], grad, (1, 1))
        moved = jnp.sum(probs * prob_grad, axis=0, keepdims=True)
        score_grad = (probs * (prob_grad - moved)).astype(BF16)
        value_part = dot(probs.astype(BF16), grad, (1, 0))
        key_part = dot(score_grad, query, (1, 0))
        if b == 0:
            v_acc[...] = value_part
            k_acc[...] = key_part
        else:
            v_acc[...] += value_part
            k_acc[...] += key_part
        q_acc[r, :] = dot(score_grad, kl_ref[...], (0, 0))
    vg_ref[...] = v_acc[...].astype(BF16)
    cosine, sine = cos_ref[...], sin_ref[...]
    for acc, back_ref, raw_ref, f_ref, g_ref, sum_ref, gain_ref in (
        (q_acc, qb_ref, q_ref, fq_ref, gq_ref, qs_ref, qg_ref),
        (k_acc, kb_ref, k_ref, fk_ref, gk_ref, ks_ref, kg_ref),
    ):
        turned = acc[...] * scale
        back = turned * cosine - half_turn(turned) * sine
        product = back * raw_ref[...]
        back_ref[...] = back
        sum_ref[...] += product * g_ref[0]
        gain_ref[0] = jnp.sum(product * f_ref[...], axis=0, keepdims=True)


def head_specs(length):
    return {
        "head": pl.BlockSpec((length, HDIM), lambda h: (0, h)),
        "whole": pl.BlockSpec((length, HDIM), lambda h: (0, 0)),
        "column": pl.BlockSpec((length, 1), lambda h: (0, 0)),
        "gain": pl.BlockSpec((1, 1, HDIM), lambda h: (h, 0, 0)),
        "row": pl.BlockSpec((1, 1, length), lambda h: (h, 0, 0)),
    }


def attend(qkv, fq, fk, gq, gk, cosine, sine):
    length, heads = qkv.shape[0], gq.shape[0]
    spec = head_specs(length)

    def part(i):
        return pl.BlockSpec((length, HDIM), lambda h: (0, i * heads + h))

    low = jax.ShapeDtypeStruct((length, heads * HDIM), BF16)
    return pl.pallas_call(
        attend_kernel,
        grid=(heads,),
        in_specs=[part(0), part(1), part(2)]
        + [spec[n] for n in ("column", "column", "gain", "gain", "whole", "whole")],
        out_specs=[spec["head"]] * 4 + [spec["row"]],
        out_shape=[low] * 4 + [jax.ShapeDtypeStruct((heads, 1, length), F32)],
        compiler_params=pltpu.CompilerParams(vmem_limit_bytes=40 * MIB),
        cost_estimate=pl.CostEstimate(
            flops=10 * heads * length * length * HDIM,
            bytes_accessed=20 * length * heads * HDIM,
            transcendentals=heads * length * length,
        ),
        name="attend",
    )(qkv, qkv, qkv, fq, fk, gq, gk, cosine, sine)


def attend_back(ql, kl, vl, grad, logsum, qkv, fq, fk, gq, gk, cosine, sine):
    length, heads = qkv.shape[0], gq.shape[0]
    spec = head_specs(length)

    def part(i):
        return pl.BlockSpec((length, HDIM), lambda h: (0, i * heads + h))

    def shape(kind, *dims):
        return jax.ShapeDtypeStruct(dims, kind)

    return pl.pallas_call(
        attend_back_kernel,
        grid=(heads,),
        in_specs=[spec["head"]] * 4
        + [spec["row"], part(0), part(1)]
        + [spec[n] for n in ("column", "column", "gain", "gain", "whole", "whole")],
        out_specs=[spec["head"]] * 3 + [spec["whole"]] * 2 + [spec["gain"]] * 2,
        out_shape=[
            shape(F32, length, heads * HDIM),
            shape(F32, length, heads * HDIM),
            shape(BF16, length, heads * HDIM),
            shape(F32, length, HDIM),
            shape(F32, length, HDIM),
            shape(F32, heads, 1, HDIM),
            shape(F32, heads, 1, HDIM),
        ],
        scratch_shapes=[pltpu.VMEM((length, HDIM), F32)] * 3,
        compiler_params=pltpu.CompilerParams(vmem_limit_bytes=48 * MIB),
        cost_estimate=pl.CostEstimate(
            flops=20 * heads * length * length * HDIM,
            bytes_accessed=30 * length * heads * HDIM,
            transcendentals=heads * length * length,
        ),
        name="attend_back",
    )(ql, kl, vl, grad, logsum, qkv, qkv, fq, fk, gq, gk, cosine, sine)


def swap(values, axis, bit):
    return lax.ppermute(values, axis, [(i, i ^ bit) for i in range(lax.axis_size(axis))])


def shift(values, by):
    n = lax.axis_size("expert")
    return lax.ppermute(values, "expert", [(i, (i + by) % n) for i in range(n)])


def context_gather(own):
    far = swap(own, "context", 2)
    near = swap(own, "context", 1)
    return [own, near, far, swap(far, "context", 1)]


def context_sum(blocks):
    got = swap(jnp.stack([blocks[1], blocks[3]]), "context", 1)
    far = swap(add_low(blocks[2], got[1]), "context", 2)
    return blocks[0].astype(F32) + got[0].astype(F32) + far.astype(F32)


def context_total(terms):
    got = swap(terms, "context", 1)
    terms = terms + jnp.stack([got[:, s ^ 1] for s in range(4)], axis=1)
    got = swap(terms, "context", 2)
    return terms + jnp.stack([got[:, s ^ 2] for s in range(4)], axis=1)


def ring_gather(own):
    held = [own]
    for _ in range(lax.axis_size("expert") - 1):
        held.append(shift(held[-1], 1))
    return held


def ring_sum(blocks, combine):
    n = len(blocks)
    total = blocks[1 % n]
    for s in range(2, n + 1):
        total = combine(blocks[s % n], shift(total, 1))
    return total


def take(blocks, index):
    return jnp.stack([lax.dynamic_index_in_dim(blocks, i, 0, keepdims=False) for i in index])


def rows_kernel(
    first,
    at_ref,
    x_ref,
    u_ref,
    mask_ref,
    router_ref,
    wg_ref,
    wu_ref,
    wd_ref,
    out_ref,
    row_ref,
    gate_ref,
    weights_ref,
    turned_ref,
    both_ref,
    hidden_ref,
    out_acc,
    row_acc,
    lanes,
    both_w,
):
    e, step = pl.program_id(0), pl.program_id(1)
    start = jnp.logical_and(e == 0, step == 0)
    rows, width = x_ref.shape
    chunk = wg_ref.shape[1]
    lane = lax.broadcasted_iota(jnp.int32, (rows, 128), 1)

    @pl.when(start)
    def _():
        out_acc[...] = jnp.zeros_like(out_acc)
        row_acc[...] = jnp.zeros_like(row_acc)
        gate_ref[...] = jnp.zeros_like(gate_ref)
        turned_ref[...] = x_ref[...].T
        logits = dot(x_ref[...], router_ref[...], (1, 0))
        chosen = mask_ref[...] > 0.5
        top = jnp.max(jnp.where(chosen, logits, -1e30), axis=-1, keepdims=True)
        raised = jnp.where(chosen, jnp.exp(jnp.where(chosen, logits - top, 0.0)), 0.0)
        weights_ref[...] = raised / jnp.sum(raised, axis=-1, keepdims=True)

    @pl.when(step == 0)
    def _():
        lanes[...] = jnp.zeros_like(lanes)

    both_w[:, :chunk] = wg_ref[...]
    both_w[:, chunk:] = wu_ref[...]
    weight = jnp.sum(
        jnp.where(lane == at_ref[0] + first + e, weights_ref[...], 0.0), axis=-1, keepdims=True
    )
    pre = dot(x_ref[...], both_w[...], (1, 0))
    gate_pre, up_pre = pre[:, :chunk], pre[:, chunk:]
    hidden_grad = dot(u_ref[...], wd_ref[...], (1, 1))
    sigmoid = 1.0 / (1.0 + jnp.exp(-gate_pre))
    activated = gate_pre * sigmoid
    hidden = activated * up_pre
    part = hidden * hidden_grad
    total = part[:, :128]
    for j in range(1, chunk // 128):
        total = total + part[:, j * 128 : (j + 1) * 128]
    lanes[...] += total
    hidden_low = (weight * hidden).astype(BF16)
    hidden_grad = weight * hidden_grad
    gate_low = (hidden_grad * up_pre * (sigmoid + activated * (1.0 - sigmoid))).astype(BF16)
    up_low = (hidden_grad * activated).astype(BF16)
    hidden_ref[...] = hidden_low
    both_ref[:, :chunk] = gate_low
    both_ref[:, chunk:] = up_low
    out_acc[...] += dot(hidden_low, wd_ref[...], (1, 0))
    row_acc[...] += dot(both_ref[...], both_w[...], (1, 1))

    @pl.when(step == pl.num_programs(1) - 1)
    def _():
        sums = jnp.sum(lanes[...], axis=-1, keepdims=True)
        gate_ref[...] += jnp.where(lane == first + e, sums, 0.0)
        out_ref[...] = out_acc[...].astype(BF16)
        row_ref[...] = row_acc[...].astype(BF16)


def run_rows(at, first, count, x, u, mask, router, w_gate, w_up, w_down):
    rows, width = x.shape
    ff = w_gate.shape[2]
    steps = ff // CHUNK

    def whole(shape):
        return pl.BlockSpec(
            shape, lambda e, s, a: (0,) * len(shape), pipeline_mode=pl.Buffered(1)
        )

    return pl.pallas_call(
        functools.partial(rows_kernel, first),
        grid_spec=pltpu.PrefetchScalarGridSpec(
            num_scalar_prefetch=1,
            grid=(count, steps),
            in_specs=[
                whole((rows, width)),
                whole((rows, width)),
                whole((rows, 128)),
                whole((width, 128)),
                pl.BlockSpec((None, width, CHUNK), lambda e, s, a: (first + e, 0, s)),
                pl.BlockSpec((None, width, CHUNK), lambda e, s, a: (first + e, 0, s)),
                pl.BlockSpec((None, CHUNK, width), lambda e, s, a: (first + e, s, 0)),
            ],
            out_specs=[
                whole((rows, width)),
                whole((rows, width)),
                whole((rows, 128)),
                whole((rows, 128)),
                whole((width, rows)),
                pl.BlockSpec((None, None, rows, 2 * CHUNK), lambda e, s, a: (e, s, 0, 0)),
                pl.BlockSpec((None, None, rows, CHUNK), lambda e, s, a: (e, s, 0, 0)),
            ],
            scratch_shapes=[
                pltpu.VMEM((rows, width), F32),
                pltpu.VMEM((rows, width), F32),
                pltpu.VMEM((rows, 128), F32),
                pltpu.VMEM((width, 2 * CHUNK), BF16),
            ],
        ),
        out_shape=[
            jax.ShapeDtypeStruct((rows, width), BF16),
            jax.ShapeDtypeStruct((rows, width), BF16),
            jax.ShapeDtypeStruct((rows, 128), F32),
            jax.ShapeDtypeStruct((rows, 128), F32),
            jax.ShapeDtypeStruct((width, rows), BF16),
            jax.ShapeDtypeStruct((count, steps, rows, 2 * CHUNK), BF16),
            jax.ShapeDtypeStruct((count, steps, rows, CHUNK), BF16),
        ],
        compiler_params=pltpu.CompilerParams(vmem_limit_bytes=56 * MIB),
        cost_estimate=pl.CostEstimate(
            flops=12 * rows * width * ff * count,
            bytes_accessed=6 * width * ff * count,
            transcendentals=rows * ff * count,
        ),
        name="rows",
    )(at, x, u, mask, router, w_gate, w_up, w_down)


def grads_kernel(sizes, bits_ref, *refs):
    n = len(sizes)
    turned, ups, boths, hiddens = (refs[i * n : (i + 1) * n] for i in range(4))
    send_ref, keep_ref, x_all, u_all, both, hidden = refs[4 * n :]
    step, steps = pl.program_id(0), pl.num_programs(0)
    width = x_all.shape[0]
    chunk = hidden.shape[1]

    spans, at = [], 0
    for size in sizes:
        spans.append(slice(at, at + size))
        at += size

    @pl.when(step == 0)
    def _():
        for span, t, u in zip(spans, turned, ups):
            x_all[:, span] = t[...]
            u_all[span, :] = u[...]

    for span, b, h in zip(spans, boths, hiddens):
        both[span, :] = b[...]
        hidden[span, :] = h[...]
    hidden_turned = hidden[...].T
    piece_rows = width // PIECES

    def store(ref):
        mask = jnp.where(step % 2 == 0, bits_ref[1], bits_ref[2])
        for p in range(PIECES):
            place = p ^ mask
            r = slice(p * piece_rows, (p + 1) * piece_rows)
            got = dot(x_all[r, :], both[...], (1, 0)).astype(BF16)
            ref[place, 0] = got[:, :chunk]
            ref[place, 1] = got[:, chunk:]
            down = dot(hidden_turned, u_all[:, r], (1, 0)).astype(BF16)
            for j in range(piece_rows // chunk):
                ref[place, 2, j * chunk : (j + 1) * chunk, :] = down[:, j * chunk : (j + 1) * chunk]

    @pl.when(step < steps // 2)
    def _():
        store(send_ref.at[0])

    @pl.when(step >= steps // 2)
    def _():
        store(keep_ref.at[0])


def run_grads(bits, segments):
    turned, ups, boths, hiddens, places = zip(*segments)
    width = turned[0].shape[0]
    sizes = tuple(u.shape[0] for u in ups)
    total = sum(sizes)
    steps = boths[0].shape[1]
    half = steps // 2
    piece_rows = width // PIECES

    def chunk_at(s, b):
        return ((1 - s // half) ^ b[0]) * half + s % half

    def whole(shape):
        return pl.BlockSpec(shape, lambda s, b: (0, 0), pipeline_mode=pl.Buffered(1))

    def chunked(size, columns, place):
        return pl.BlockSpec(
            (None, None, size, columns), lambda s, b: (place, chunk_at(s, b), 0, 0)
        )

    grads = (1, PIECES, 3, piece_rows, CHUNK)
    grads_out = jax.ShapeDtypeStruct((half,) + grads[1:], BF16)
    return pl.pallas_call(
        functools.partial(grads_kernel, sizes),
        grid_spec=pltpu.PrefetchScalarGridSpec(
            num_scalar_prefetch=1,
            grid=(steps,),
            in_specs=[whole((width, size)) for size in sizes]
            + [whole((size, width)) for size in sizes]
            + [chunked(size, 2 * CHUNK, p) for size, p in zip(sizes, places)]
            + [chunked(size, CHUNK, p) for size, p in zip(sizes, places)],
            out_specs=[
                pl.BlockSpec(grads, lambda s, b: (jnp.minimum(s, half - 1), 0, 0, 0, 0)),
                pl.BlockSpec(grads, lambda s, b: (jnp.maximum(s - half, 0), 0, 0, 0, 0)),
            ],
            scratch_shapes=[
                pltpu.VMEM((width, total), BF16),
                pltpu.VMEM((total, width), BF16),
                pltpu.VMEM((total, 2 * CHUNK), BF16),
                pltpu.VMEM((total, CHUNK), BF16),
            ],
        ),
        out_shape=[grads_out, grads_out],
        compiler_params=pltpu.CompilerParams(vmem_limit_bytes=56 * MIB),
        cost_estimate=pl.CostEstimate(
            flops=6 * total * width * steps * CHUNK,
            bytes_accessed=6 * width * steps * CHUNK + 8 * total * width,
            transcendentals=0,
        ),
        name="grads",
    )(bits, *turned, *ups, *boths, *hiddens)


def add_kernel(picks, joined, *refs):
    outs = [refs[-1].at[i] for i in range(len(picks))] if joined else refs[-len(picks) :]

    def at(ref, index):
        return ref[index] if index is not None else ref[...]

    for out, terms in zip(outs, picks):
        left, right = (at(refs[i], index) for i, index in terms)
        out[...] = (left.astype(F32) + right.astype(F32)).astype(BF16)


def add_pieces(picks, shapes, ins, last, joined=False):

    parts = 4

    def cut(shape):
        block = shape[:-2] + (shape[-2] // parts, shape[-1])
        return pl.BlockSpec(block, lambda i: (0,) * (len(shape) - 2) + (i, 0))

    moved = sum(i.size for i in ins) + sum(math.prod(s) for s in shapes)
    return pl.pallas_call(
        functools.partial(add_kernel, picks, joined),
        grid=(parts,),
        in_specs=[cut(i.shape) for i in ins] + [pl.BlockSpec(memory_space=pl.ANY)],
        out_specs=[cut(s) for s in shapes],
        out_shape=[jax.ShapeDtypeStruct(s, BF16) for s in shapes],
        compiler_params=pltpu.CompilerParams(vmem_limit_bytes=32 * MIB),
        cost_estimate=pl.CostEstimate(flops=moved, bytes_accessed=2 * moved, transcendentals=0),
        name="add_pieces",
    )(*ins, last)


class Summed:
    def __init__(self, order, send, keep):
        self.order, self.keep = order, keep
        self.ahead = ["halves", "quarters", "finals"]
        self.got = swap(send, "context", 1)

    def reach(self, name):
        while name in self.ahead:
            getattr(self, self.ahead.pop(0))()

    def add(self, picks, shapes, ins, joined=False):
        outs = add_pieces(picks, shapes, ins, self.order.last, joined)
        self.order.did(outs[0])
        return outs

    def halves(self):
        shape = (2,) + self.keep.shape[2:]
        picks = [
            [(0, (path, slice(at, at + 2))), (1, (path, slice(at, at + 2)))]
            for at in (2, 0)
            for path in range(2)
        ]
        outs = self.add(picks, [shape] * 4, [self.keep, self.got])
        self.coming = [swap(outs[path], *FIRST[path]) for path in range(2)]
        self.kept = outs[2:]

    def quarters(self):
        shape = self.keep.shape[2:]
        picks = [[(path, at), (2 + path, at)] for at in (1, 0) for path in range(2)]
        outs = self.add(picks, [shape] * 4, [*self.kept, *self.coming])
        self.coming = [swap(outs[path], *SECOND[path]) for path in range(2)]
        self.kept = outs[2:]

    def finals(self):
        shape = self.keep.shape[2:]
        picks = [[(path, None), (2 + path, None)] for path in range(2)]
        own = self.add(picks, [(2,) + shape], [*self.kept, *self.coming], True)[0]
        self.all = lax.all_gather(own, ("context", "dp"), axis=0)


def place_kernel(e, first, last_ref, *refs):
    source = refs[0]
    outs = refs[1:4] if first else refs[4:7]
    token_ref, low, wide, in_sem, out_sem = refs[-5:]
    rows = low.shape[2]
    count = 2 * source.shape[0]
    token_ref[...] = jnp.zeros_like(token_ref)

    def fetch(i):
        return pltpu.make_async_copy(source.at[i // 2, i % 2], low.at[i % 2], in_sem.at[i % 2])

    def drain(i):
        path, member = i % 2, i // 2
        side, core, dp = member // 4, member // 2 % 2, member % 2
        chunk = core * 2 + path
        piece = (dp * 2 + side, side * 2 + dp)[path]
        columns = pl.ds(chunk * CHUNK, CHUNK)
        copies = []
        for k in range(2):
            copies.append(
                pltpu.make_async_copy(
                    wide.at[i % 2, k],
                    outs[k].at[e, pl.ds(piece * rows, rows), columns],
                    out_sem.at[i % 2, k],
                )
            )
        for j in range(rows // CHUNK):
            copies.append(
                pltpu.make_async_copy(
                    wide.at[i % 2, 2, pl.ds(j * CHUNK, CHUNK)],
                    outs[2].at[e, columns, pl.ds(piece * rows + j * CHUNK, CHUNK)],
                    out_sem.at[i % 2, 2 + j],
                )
            )
        return copies

    fetch(0).start()
    for i in range(count):
        if i + 1 < count:
            fetch(i + 1).start()
        fetch(i).wait()
        if i >= 2:
            for copy in drain(i - 2):
                copy.wait()
        for k in range(3):

            @pl.loop(0, rows // 64)
            def _(t):
                r = pl.ds(pl.multiple_of(t * 64, 64), 64)
                wide[i % 2, k, r, :] = low[i % 2, k, r, :].astype(F32)

        for copy in drain(i):
            copy.start()
    for i in (count - 2, count - 1):
        for copy in drain(i):
            copy.wait()


def place_grads(e, gathered, last, outs, shapes):
    first = outs is None
    rows = gathered.shape[3]
    anywhere = pl.BlockSpec(memory_space=pl.ANY)
    operands = [last, gathered] + ([] if first else list(outs[:3]))
    return pl.pallas_call(
        functools.partial(place_kernel, e, first),
        in_specs=[anywhere] * len(operands),
        out_specs=[anywhere] * 3 + [pl.BlockSpec((8, 128), lambda: (0, 0))],
        scratch_shapes=[
            pltpu.VMEM((2, 3, rows, CHUNK), BF16),
            pltpu.VMEM((2, 3, rows, CHUNK), F32),
            pltpu.SemaphoreType.DMA((2,)),
            pltpu.SemaphoreType.DMA((2, 2 + rows // CHUNK)),
        ],
        out_shape=[jax.ShapeDtypeStruct(s, F32) for s in (*shapes, (8, 128))],
        input_output_aliases={} if first else {2: 0, 3: 1, 4: 2},
        compiler_params=pltpu.CompilerParams(vmem_limit_bytes=16 * MIB),
        cost_estimate=pl.CostEstimate(
            flops=0, bytes_accessed=16 * 9 * rows * CHUNK * 2, transcendentals=0
        ),
        name="place",
    )(*operands)


def body(
    hidden_in,
    out_grad,
    routes,
    attn_gain,
    w_query,
    w_key,
    w_value,
    q_gain,
    k_gain,
    w_out,
    ffn_gain,
    w_router,
    w_gate,
    w_up,
    w_down,
):
    groups = lax.axis_size("expert")
    context = lax.axis_size("context")
    my_group = lax.axis_index("expert")
    my_context = lax.axis_index("context")
    my_dp = lax.axis_index("dp")
    tokens = hidden_in.shape[1]
    width = hidden_in.shape[2]
    rows = w_query.shape[0]
    local_experts = w_gate.shape[0]
    experts_all = w_router.shape[1]
    length = tokens * context
    per = HEADS // context
    local = per * HDIM
    core, side = my_context % 2, my_context // 2
    bits = jnp.stack([core, my_dp * 2 + side, side * 2 + my_dp]).astype(jnp.int32)
    ring = [(my_group - s) % groups for s in range(groups)]
    members = [my_context ^ s for s in range(context)]

    def half_columns(weight):
        split = weight.reshape(rows, 2, per // 2, context, HDIM)
        split = lax.dynamic_index_in_dim(split, my_dp, 1, keepdims=False)
        return split.transpose(2, 0, 1, 3).reshape(context, rows, local // 2)

    columns = jnp.concatenate([half_columns(w) for w in (w_query, w_key, w_value)], axis=2)
    pieces = [lax.dynamic_index_in_dim(columns, m, 0, keepdims=False) for m in members]
    pieces = [pieces[0]] + [swap(pieces[s], "context", s) for s in range(1, context)]
    half_w = take(jnp.stack(pieces), members).reshape(context * rows, 3 * local // 2)
    small = jnp.concatenate(
        [attn_gain[None], q_gain[None], k_gain[None], ffn_gain[None], w_router.T], axis=0
    )
    small = [small] + [swap(small, "context", s) for s in range(1, context)]
    small = take(jnp.stack(small), members)
    hidden_all = lax.optimization_barrier((hidden_in[0], half_w, small))[0]
    hidden_all = jnp.concatenate(context_gather(hidden_all), axis=0)
    small = take(jnp.stack(ring_gather(small)), ring)
    small_all = small.transpose(2, 0, 1, 3).reshape(4 + experts_all, width)
    halves, others = [half_w], [swap(half_w, "dp", 1)]
    for s in range(1, groups):
        before = lax.optimization_barrier((halves[-1], others[s - 2]))[0] if s > 1 else half_w
        halves.append(shift(before, 1))
        others.append(swap(halves[-1], "dp", 1))
    routes_ring = ring_gather(lax.optimization_barrier((routes[0], halves[-1]))[0])
    some = local // 2
    qkv_w = jnp.concatenate(
        [
            jnp.concatenate(
                [w[:, i * some : (i + 1) * some] for i in range(3) for w in pair], axis=1
            )
            for pair in zip(halves, others)
        ],
        axis=0,
    )
    heads = [my_dp * 2, my_dp * 2 + 1, (1 - my_dp) * 2, (1 - my_dp) * 2 + 1]
    whole_heads = rows == HDIM
    if whole_heads:
        held = lax.optimization_barrier((w_out, halves[-1]))[0]
        held = jnp.stack(ring_gather(held))
        out_w = take(held, [(my_group - h) % groups for h in heads]).reshape(local, width)
    else:
        out_w = lax.all_gather(w_out, ("expert", "context"), axis=0, tiled=True)
        out_w = out_w.reshape(per, context, HDIM, width)
        out_w = lax.dynamic_index_in_dim(out_w, my_context, 1, keepdims=False)
        out_w = take(out_w, heads).reshape(local, width)
    upstream_all = lax.optimization_barrier((out_grad[0], halves[-1]))[0]
    upstream_all = lax.all_gather(upstream_all, "expert", axis=0)

    gain_attn = small_all[0].astype(F32)
    gain_ffn = small_all[3].astype(F32)
    router_w = small_all[4:]
    router_wide = jnp.pad(router_w.T, ((0, 0), (0, 128 - experts_all)))

    def mine(vector):
        table = vector.reshape(per, context, HDIM)
        table = lax.dynamic_index_in_dim(table, my_context, 1, keepdims=False)
        return take(table, heads).astype(F32)

    gain_query, gain_key = mine(small_all[1]), mine(small_all[2])
    block = width // groups

    def to_ring(values):
        parts = [lax.dynamic_slice_in_dim(values, m * block, block, axis=1) for m in ring]
        return jnp.concatenate(parts, axis=1)

    source_all = hidden_all.astype(F32)
    factor_all = rms_factor(source_all)
    normed = to_ring((source_all * factor_all * gain_attn).astype(BF16))
    source = hidden_in[0].astype(F32)
    factor_one = rms_factor(source)
    qkv = dot(normed, qkv_w, (1, 0))

    def slots(query, key):
        return jnp.stack([v.reshape(context, tokens) for v in (query, key)])

    def per_row(values):
        return values.reshape(length)[:, None]

    squares = jnp.sum(jnp.square(qkv[:, : 2 * local]).reshape(length, 2, local), axis=-1)
    squares = context_total(slots(squares[:, 0], squares[:, 1]))
    factors = lax.rsqrt(squares / width + epsilon)
    factor_query, factor_key = per_row(factors[0]), per_row(factors[1])
    starts = jnp.stack([m * tokens for m in members])
    positions = (starts[:, None] + jnp.arange(tokens, dtype=jnp.int32)).reshape(length).astype(F32)
    frequency = rope_base ** (-jnp.arange(HDIM // 2, dtype=F32) * 2.0 / HDIM)
    angles = positions[:, None] * frequency[None, :]
    cosine = jnp.tile(jnp.cos(angles), (1, 2))
    sine_part = jnp.sin(angles)
    sine_part = jnp.concatenate([-sine_part, sine_part], axis=1)
    turn = (factor_query, factor_key, gain_query[:, None], gain_key[:, None], cosine, sine_part)
    query_low, key_low, value_low, mixed_low, logsum = attend(qkv, *turn)
    mixed_out = dot(mixed_low, out_w, (1, 0)).astype(BF16).reshape(context, tokens, width)
    residual = source + context_sum([mixed_out[s] for s in range(context)])
    factor_two = rms_factor(residual)
    normed_two = (residual * factor_two * gain_ffn).astype(BF16)

    ids = jnp.arange(128, dtype=jnp.int32)
    masks = [jnp.any(r[:, :, None] == ids, axis=1).astype(F32) for r in routes_ring]
    at = jnp.reshape(my_group * local_experts, (1,)).astype(jnp.int32)
    order = Order()

    def upstream_of(slot):
        return lax.dynamic_index_in_dim(order.tie(upstream_all), ring[slot], 0, keepdims=False)

    def rows_of(first, count, x, u, mask):
        result = run_rows(order.tie(at), first, count, x, u, mask, router_wide, w_gate, w_up, w_down)
        order.did(result[0])
        return result

    near = [[(0, local_experts)], [(0, local_experts)]]
    if local_experts == 4:
        near = [[(0, 2), (2, 2)]] * 2
    blocks = [normed_two, shift(normed_two, 1)]
    segments = [([0], []), ([1], [])]
    ups = [out_grad[0]]
    for slot in range(2):
        if slot == 1:
            ups.append(upstream_of(1))
        for i, (first, count) in enumerate(near[slot]):
            result = rows_of(first, count, blocks[slot], ups[slot], masks[slot])
            segments[slot][1].append((first, count, result))
            if slot == 0 or i == 0:
                if len(blocks) < groups:
                    held = order.tie(blocks[-1])
                    order.did(held)
                    blocks.append(shift(held, 1))
    while len(blocks) < groups:
        blocks.append(shift(blocks[-1], 1))
    far = []
    for slot in range(2, groups, 2):
        pair = [slot, slot + 1]
        x, u, mask = (
            jnp.concatenate(v, axis=0)
            for v in (
                [blocks[s] for s in pair],
                [upstream_of(s) for s in pair],
                [masks[s] for s in pair],
            )
        )
        far.append((x, u, mask))
        segments.append((pair, []))
        ups.append(u)

    def segment_of(segment, e):
        for first, count, result in segments[segment][1]:
            if first <= e < first + count:
                return (result[4], ups[segment], result[5], result[6], e - first)

    summed = []

    def advance(events):
        for e, name in events:
            if e < len(summed):
                summed[e].reach(name)

    during = {
        1: ([(0, "halves")], []),
        2: ([(0, "quarters"), (1, "halves")], [(0, "finals")]),
        3: ([(1, "quarters"), (2, "halves")], []),
    }

    def total_of(slot, index):
        for pair, calls in segments:
            if slot in pair:
                at_row = pair.index(slot) * tokens
                parts = [result[index][at_row : at_row + tokens] for _, _, result in calls]
                return total_low(parts)

    def hop(index, total, slot):
        term = total_of(slot % groups, index)
        return order.run(add_low, term, shift(total, 1))

    row_total = total_of(1, 1)
    for e in range(local_experts):
        for i, (x, u, mask) in enumerate(far):
            segments[2 + i][1].append((e, 1, rows_of(e, 1, x, u, mask)))
        advance(during.get(e, ([], []))[0])
        if e == local_experts - 1:
            row_total = hop(1, row_total, 2)
        bunches = [[0, 1, 2]] + [[s, s + 1] for s in range(3, len(segments), 2)]
        results = []
        for bunch in bunches:
            got = run_grads(order.tie(bits), [segment_of(s, e) for s in bunch if s < len(segments)])
            order.did(got[0])
            results.append(got)
        send, keep = (
            total_low([r[i] for r in results]) if len(results) > 1 else results[0][i]
            for i in range(2)
        )
        summed.append(Summed(order, send, keep))
        advance(during.get(e, ([], []))[1])

    gate_grad = [
        functools.reduce(
            lambda a, b: a + b,
            [result[2][pair.index(s) * tokens : (pair.index(s) + 1) * tokens] for _, _, result in calls],
        )
        for pair, calls in segments
        for s in pair
    ]
    gate_grad = [g[:, :local_experts].T for g in gate_grad]
    gate_grad = jnp.stack([gate_grad[0]] + [shift(gate_grad[s], -s) for s in range(1, groups)])
    gate_grad = take(gate_grad, [(g - my_group) % groups for g in range(groups)])
    gate_grad = gate_grad.reshape(experts_all, tokens).T

    events = [
        [],
    ]
    for slot in range(3, groups + 1):
        row_total = hop(1, row_total, slot)
        advance(events[slot - 3] if slot - 3 < len(events) else [])
    row_back = row_total.astype(F32)

    upstream = out_grad[0].astype(F32)
    weights_own = segments[0][1][0][2][3][:, :experts_all]
    weighted = jnp.sum(weights_own * gate_grad, axis=-1, keepdims=True)
    logit_grad = (weights_own * (gate_grad - weighted)).astype(BF16)
    router_grad = dot(logit_grad, normed_two, (0, 0))
    normed_two_grad = dot(logit_grad, router_w, (1, 0)) + row_back
    residual_part, ffn_gain_grad = norm_back(normed_two_grad, residual, factor_two, gain_ffn)
    residual_grad = upstream + residual_part

    attn_grad = order.tie(residual_grad.astype(BF16))
    order.did(attn_grad)
    attn_grad = context_gather(attn_grad)
    advance([(1, "finals"), (3, "halves"), (2, "quarters")])
    out_total = hop(0, total_of(1, 0), 2)
    attn_grad = order.tie(jnp.concatenate(attn_grad, axis=0))
    order.did(attn_grad)
    out_w_grad = dot(mixed_low, attn_grad, (0, 0)).astype(BF16).reshape(per, HDIM, width)
    mixed_grad = dot(attn_grad, out_w, (1, 1)).astype(BF16)
    order.did(mixed_grad)
    advance([(2, "finals"), (3, "quarters")])
    out_total = hop(0, out_total, 3) if groups > 2 else out_total
    mixed_grad = order.tie(mixed_grad)
    query_back, key_back, value_grad, query_sum, key_sum, q_gain_grad, k_gain_grad = attend_back(
        query_low, key_low, value_low, mixed_grad, logsum, qkv, *turn
    )
    order.did(value_grad)
    value_w_grad = dot(normed, value_grad, (0, 0)).astype(BF16)
    value_w_grad = ring_sum(list(value_w_grad.reshape(groups, context * rows, local)), add_low)
    sums = context_total(slots(jnp.sum(query_sum, axis=1), jnp.sum(key_sum, axis=1))) / width
    advance([(3, "finals")])
    for slot in range(4, groups + 1):
        out_total = hop(0, out_total, slot)
    hidden_out = (residual + out_total.astype(F32)).astype(BF16)[None]
    shapes = (w_gate.shape, w_up.shape, w_down.shape)
    expert_grads = None

    def place(experts):
        outs = expert_grads
        for e in experts:
            if e < local_experts:
                summed[e].reach("finals")
                outs = place_grads(e, summed[e].all, order.last, outs, shapes)
                order.did(outs[3])
        return outs

    def low_grad(back, raw, factor, gain, total):
        return (
            factor * back * gain.reshape(1, local) - raw * factor**3 * per_row(total)
        ).astype(BF16)

    query_grad = low_grad(query_back, qkv[:, :local], factor_query, gain_query, sums[0])
    key_grad = low_grad(key_back, qkv[:, local : 2 * local], factor_key, gain_key, sums[1])
    qkv_grad = order.tie(jnp.concatenate([query_grad, key_grad, value_grad], axis=1))
    normed_grad = dot(qkv_grad, qkv_w, (1, 1)).astype(BF16).reshape(context, tokens, width)
    normed_grad = context_sum([normed_grad[s] for s in range(context)])
    qk_w_grad = dot(normed, qkv_grad[:, : 2 * local], (0, 0)).astype(BF16)
    order.did(qk_w_grad)
    qk_w_grad = ring_sum(list(qk_w_grad.reshape(groups, context * rows, 2 * local)), add_low)
    expert_grads = place([0, 1, 2])
    parts = [
        lax.dynamic_slice_in_dim(normed_grad, (my_group - m) % groups * block, block, axis=1)
        for m in range(groups)
    ]
    normed_grad = jnp.concatenate(parts, axis=1)
    source_part, attn_gain_grad = norm_back(normed_grad, source, factor_one, gain_attn)
    input_grad = (residual_grad + source_part).astype(BF16)[None]

    mine_w = jnp.concatenate([qk_w_grad, value_w_grad], axis=1).reshape(context, rows, 3, 2, some)
    got = swap(mine_w, "dp", 1)
    mine_w = jnp.stack(
        [add_low(mine_w[:, :, :, i], got[:, :, :, 1 - i]) for i in range(2)], axis=3
    )
    pieces = [lax.dynamic_index_in_dim(mine_w, m, 0, keepdims=False) for m in members]
    pieces = [pieces[0]] + [swap(pieces[s], "context", s) for s in range(1, context)]
    dense = take(jnp.stack(pieces), members)
    dense = jnp.where(my_dp == 0, dense, dense[:, :, :, ::-1]).astype(F32)
    dense = dense.reshape(context, rows, 3, per, HDIM).transpose(2, 1, 3, 0, 4)
    dense = dense.reshape(3, rows, width)
    if whole_heads:
        ordered = take(out_w_grad, [(m // 2 ^ my_dp) * 2 + m % 2 for m in ring])
        mine_out = ring_sum(list(ordered), add_low)
        out_w_grad = mine_out.astype(F32) + swap(mine_out, "dp", 1).astype(F32)
    else:
        spread = jnp.zeros((per, context, HDIM, width), BF16)
        for h in range(per):
            spread = lax.dynamic_update_slice(
                spread, out_w_grad[h][None, None], (heads[h], my_context, 0, 0)
            )
        spread = lax.psum_scatter(
            spread.reshape(width, width), ("expert", "context"), scatter_dimension=0, tiled=True
        )
        out_w_grad = lax.psum(spread, "dp").astype(F32)
    gains = jnp.zeros((2, per, context, HDIM), F32)
    for h in range(per):
        pair = jnp.stack([q_gain_grad[h], k_gain_grad[h]])[:, None]
        gains = lax.dynamic_update_slice(gains, pair, (0, heads[h], my_context, 0))
    small_grad = jnp.concatenate(
        [attn_gain_grad[None], ffn_gain_grad[None], gains.reshape(2, width), router_grad], axis=0
    )
    small_grad = small_grad.reshape(4 + experts_all, groups, context, rows).transpose(1, 2, 0, 3)
    small_grad = ring_sum(list(take(small_grad, ring)), lambda a, b: a + b)
    small_grad = take(small_grad, members)
    got = swap(jnp.stack([small_grad[1], small_grad[3]]), "context", 1)
    small_grad = small_grad[0] + got[0] + swap(small_grad[2] + got[1], "context", 2)
    small_grad = small_grad + swap(small_grad, "dp", 1)
    expert_grads = place([3])
    return (
        hidden_out,
        input_grad,
        small_grad[0],
        dense[0],
        dense[1],
        dense[2],
        small_grad[2],
        small_grad[3],
        out_w_grad,
        small_grad[1],
        small_grad[4:].T,
        expert_grads[0],
        expert_grads[1],
        expert_grads[2],
    )


def solution(mesh):
    tokens = P(("expert", "dp"), "context", None)
    vector = P(("expert", "context"))
    matrix = P(("expert", "context"), None)
    expert = P("expert", None, None)
    in_specs = (
        tokens,
        tokens,
        tokens,
        vector,
        matrix,
        matrix,
        matrix,
        vector,
        vector,
        matrix,
        vector,
        matrix,
        expert,
        expert,
        expert,
    )
    out_specs = (
        tokens,
        tokens,
        vector,
        matrix,
        matrix,
        matrix,
        vector,
        vector,
        matrix,
        vector,
        matrix,
        expert,
        expert,
        expert,
    )
    return jax.shard_map(body, mesh=mesh, in_specs=in_specs, out_specs=out_specs, check_vma=False)
```

```python
import functools
import math

import jax
import jax.numpy as jnp
from jax import lax
from jax.experimental import pallas as pl
from jax.experimental.pallas import tpu as pltpu
from jax.sharding import PartitionSpec as P

HEADS = 16
HDIM = 128
CHUNK = 256
ROWS = 1024

epsilon = 1e-06
rope_base = 10000.0
F32 = jnp.float32
BF16 = jnp.bfloat16
MIB = 1024 * 1024


def dot(left, right, contract):
    return lax.dot_general(
        left, right, (((contract[0],), (contract[1],)), ((), ())), preferred_element_type=F32
    )


def add_low(left, right):
    return (left.astype(F32) + right.astype(F32)).astype(BF16)


def total_low(terms):
    return functools.reduce(lambda a, b: a + b, [t.astype(F32) for t in terms]).astype(BF16)


FIRST = (("dp", 1), ("context", 2))
SECOND = (("context", 2), ("dp", 1))
PIECES = 4


def nothing_of(values, dtype):
    return (values[(0,) * values.ndim].astype(F32) * 0.0).astype(dtype)


def after(values, *others):
    for other in others:
        values = values + nothing_of(other, values.dtype)
    return values


ANYWHERE = pl.BlockSpec(memory_space=pl.ANY)
TOKEN = jax.ShapeDtypeStruct((8, 128), F32)


def token_spec():
    return pl.BlockSpec((8, 128), lambda *_: (0, 0))


class Order:
    def __init__(self):
        self.token = jnp.zeros((8, 128), F32)

    def run(self, call, *args):
        *results, self.token = call(self.token, *args)
        return results


def rms_factor(values):
    return lax.rsqrt(jnp.mean(values * values, axis=-1, keepdims=True) + epsilon)


def norm_back(grad_out, values, factor, gain_vector):
    scaled = grad_out * gain_vector
    grad_in = factor * scaled - values * factor**3 * jnp.mean(
        scaled * values, axis=-1, keepdims=True
    )
    gain_grad = jnp.sum(grad_out * values * factor, axis=0)
    return (grad_in, gain_grad)


def half_turn(values):
    return pltpu.roll(values, HDIM // 2, 1)


def attend_kernel(
    q_ref, k_ref, v_ref, fq_ref, fk_ref, gq_ref, gk_ref, cos_ref, sin_ref, *refs
):
    ql_ref, kl_ref, vl_ref, mixed_ref, logsum_ref = refs[-5:]
    length = q_ref.shape[0]
    block = min(256, length)
    cosine, sine = cos_ref[...], sin_ref[...]
    query = q_ref[...] * fq_ref[...] * gq_ref[0]
    key = k_ref[...] * fk_ref[...] * gk_ref[0]
    ql_ref[...] = (query * cosine + half_turn(query) * sine).astype(BF16)
    kl_ref[...] = (key * cosine + half_turn(key) * sine).astype(BF16)
    value = v_ref[...].astype(BF16)
    vl_ref[...] = value
    turned = value.T
    for b in range(length // block):
        r = slice(b * block, (b + 1) * block)
        scores = dot(kl_ref[...], ql_ref[r, :], (1, 1)) * HDIM ** (-0.5)
        top = jnp.max(scores, axis=0, keepdims=True)
        raised = jnp.exp(scores - top)
        total = jnp.sum(raised, axis=0, keepdims=True)
        mixed = dot(turned, raised.astype(BF16), (1, 0)) / total
        mixed_ref[r, :] = mixed.T.astype(BF16)
        logsum_ref[0, :, r] = top + jnp.log(total)


def attend_back_kernel(
    ql_ref, kl_ref, vl_ref, grad_ref, logsum_ref, q_ref, k_ref, fq_ref, fk_ref, gq_ref, gk_ref,
    cos_ref, sin_ref, _, qb_ref, kb_ref, vg_ref, qs_ref, ks_ref, qg_ref, kg_ref, token_ref,
    k_acc, v_acc, q_acc,
):
    token_ref[...] = jnp.zeros_like(token_ref)
    length = ql_ref.shape[0]
    block = min(256, length)
    scale = HDIM ** (-0.5)

    @pl.when(pl.program_id(0) == 0)
    def _():
        qs_ref[...] = jnp.zeros_like(qs_ref)
        ks_ref[...] = jnp.zeros_like(ks_ref)

    for b in range(length // block):
        r = slice(b * block, (b + 1) * block)
        query, grad = ql_ref[r, :], grad_ref[r, :]
        scores = dot(kl_ref[...], query, (1, 1)) * scale
        probs = jnp.exp(scores - logsum_ref[0, :, r])
        prob_grad = dot(vl_ref[...], grad, (1, 1))
        moved = jnp.sum(probs * prob_grad, axis=0, keepdims=True)
        score_grad = (probs * (prob_grad - moved)).astype(BF16)
        value_part = dot(probs.astype(BF16), grad, (1, 0))
        key_part = dot(score_grad, query, (1, 0))
        if b == 0:
            v_acc[...] = value_part
            k_acc[...] = key_part
        else:
            v_acc[...] += value_part
            k_acc[...] += key_part
        q_acc[r, :] = dot(score_grad, kl_ref[...], (0, 0))
    vg_ref[...] = v_acc[...].astype(BF16)
    cosine, sine = cos_ref[...], sin_ref[...]
    for acc, back_ref, raw_ref, f_ref, g_ref, sum_ref, gain_ref in (
        (q_acc, qb_ref, q_ref, fq_ref, gq_ref, qs_ref, qg_ref),
        (k_acc, kb_ref, k_ref, fk_ref, gk_ref, ks_ref, kg_ref),
    ):
        turned = acc[...] * scale
        back = turned * cosine - half_turn(turned) * sine
        product = back * raw_ref[...]
        back_ref[...] = back
        sum_ref[...] += product * g_ref[0]
        gain_ref[0] = jnp.sum(product * f_ref[...], axis=0, keepdims=True)


def head_specs(length):
    return {
        "head": pl.BlockSpec((length, HDIM), lambda h: (0, h)),
        "whole": pl.BlockSpec((length, HDIM), lambda h: (0, 0)),
        "column": pl.BlockSpec((length, 1), lambda h: (0, 0)),
        "gain": pl.BlockSpec((1, 1, HDIM), lambda h: (h, 0, 0)),
        "row": pl.BlockSpec((1, 1, length), lambda h: (h, 0, 0)),
    }


def attend(qkv, fq, fk, gq, gk, cosine, sine, before):
    length, heads = qkv.shape[0], gq.shape[0]
    spec = head_specs(length)

    def part(i):
        return pl.BlockSpec((length, HDIM), lambda h: (0, i * heads + h))

    low = jax.ShapeDtypeStruct((length, heads * HDIM), BF16)
    return pl.pallas_call(
        attend_kernel,
        grid=(heads,),
        in_specs=[part(0), part(1), part(2)]
        + [spec[n] for n in ("column", "column", "gain", "gain", "whole", "whole")]
        + [ANYWHERE] * len(before),
        out_specs=[spec["head"]] * 4 + [spec["row"]],
        out_shape=[low] * 4 + [jax.ShapeDtypeStruct((heads, 1, length), F32)],
        compiler_params=pltpu.CompilerParams(vmem_limit_bytes=60 * MIB),
        cost_estimate=pl.CostEstimate(
            flops=10 * heads * length * length * HDIM,
            bytes_accessed=20 * length * heads * HDIM,
            transcendentals=heads * length * length,
        ),
        name="attend",
    )(qkv, qkv, qkv, fq, fk, gq, gk, cosine, sine, *before)


def attend_back(token, ql, kl, vl, grad, logsum, qkv, fq, fk, gq, gk, cosine, sine):
    length, heads = qkv.shape[0], gq.shape[0]
    spec = head_specs(length)

    def part(i):
        return pl.BlockSpec((length, HDIM), lambda h: (0, i * heads + h))

    def shape(kind, *dims):
        return jax.ShapeDtypeStruct(dims, kind)

    return pl.pallas_call(
        attend_back_kernel,
        grid=(heads,),
        in_specs=[spec["head"]] * 4
        + [spec["row"], part(0), part(1)]
        + [spec[n] for n in ("column", "column", "gain", "gain", "whole", "whole")]
        + [ANYWHERE],
        out_specs=[spec["head"]] * 3 + [spec["whole"]] * 2 + [spec["gain"]] * 2 + [token_spec()],
        out_shape=[
            shape(F32, length, heads * HDIM),
            shape(F32, length, heads * HDIM),
            shape(BF16, length, heads * HDIM),
            shape(F32, length, HDIM),
            shape(F32, length, HDIM),
            shape(F32, heads, 1, HDIM),
            shape(F32, heads, 1, HDIM),
            TOKEN,
        ],
        scratch_shapes=[pltpu.VMEM((length, HDIM), F32)] * 3,
        compiler_params=pltpu.CompilerParams(vmem_limit_bytes=60 * MIB),
        cost_estimate=pl.CostEstimate(
            flops=20 * heads * length * length * HDIM,
            bytes_accessed=30 * length * heads * HDIM,
            transcendentals=heads * length * length,
        ),
        name="attend_back",
    )(ql, kl, vl, grad, logsum, qkv, qkv, fq, fk, gq, gk, cosine, sine, token)


def swap(values, axis, bit):
    return lax.ppermute(values, axis, [(i, i ^ bit) for i in range(lax.axis_size(axis))])


def shift(values, by):
    n = lax.axis_size("expert")
    return lax.ppermute(values, "expert", [(i, (i + by) % n) for i in range(n)])


def context_gather(own):
    far = swap(own, "context", 2)
    near = swap(own, "context", 1)
    return [own, near, far, swap(far, "context", 1)]


def context_sum(blocks):
    got = swap(jnp.stack([blocks[1], blocks[3]]), "context", 1)
    far = swap(add_low(blocks[2], got[1]), "context", 2)
    return blocks[0].astype(F32) + got[0].astype(F32) + far.astype(F32)


def context_total(terms):
    got = swap(terms, "context", 1)
    terms = terms + jnp.stack([got[:, s ^ 1] for s in range(4)], axis=1)
    got = swap(terms, "context", 2)
    return terms + jnp.stack([got[:, s ^ 2] for s in range(4)], axis=1)


def ring_gather(own):
    held = [own]
    for _ in range(lax.axis_size("expert") - 1):
        held.append(shift(held[-1], 1))
    return held


def ring_direct(own):
    return [own] + [shift(own, s) for s in range(1, lax.axis_size("expert"))]


def take(blocks, index):
    return jnp.stack([lax.dynamic_index_in_dim(blocks, i, 0, keepdims=False) for i in index])


def rows_kernel(
    first,
    at_ref,
    x_ref,
    u_ref,
    mask_ref,
    router_ref,
    wg_ref,
    wu_ref,
    wd_ref,
    *refs,
):
    (
        out_ref,
        row_ref,
        gate_ref,
        weights_ref,
        turned_ref,
        both_ref,
        hidden_ref,
        token_ref,
        out_acc,
        row_acc,
        lanes,
        both_w,
    ) = refs[-12:]
    e, step = pl.program_id(0), pl.program_id(1)
    start = jnp.logical_and(e == 0, step == 0)
    rows, width = x_ref.shape
    chunk = wg_ref.shape[1]
    lane = lax.broadcasted_iota(jnp.int32, (rows, 128), 1)
    token_ref[...] = jnp.zeros_like(token_ref)

    @pl.when(start)
    def _():
        out_acc[...] = jnp.zeros_like(out_acc)
        row_acc[...] = jnp.zeros_like(row_acc)
        gate_ref[...] = jnp.zeros_like(gate_ref)
        turned_ref[...] = x_ref[...].T
        logits = dot(x_ref[...], router_ref[...], (1, 0))
        chosen = mask_ref[...] > 0.5
        top = jnp.max(jnp.where(chosen, logits, -1e30), axis=-1, keepdims=True)
        raised = jnp.where(chosen, jnp.exp(jnp.where(chosen, logits - top, 0.0)), 0.0)
        weights_ref[...] = raised / jnp.sum(raised, axis=-1, keepdims=True)

    @pl.when(step == 0)
    def _():
        lanes[...] = jnp.zeros_like(lanes)

    both_w[:, :chunk] = wg_ref[...]
    both_w[:, chunk:] = wu_ref[...]
    weight = jnp.sum(
        jnp.where(lane == at_ref[0] + first + e, weights_ref[...], 0.0), axis=-1, keepdims=True
    )
    pre = dot(x_ref[...], both_w[...], (1, 0))
    gate_pre, up_pre = pre[:, :chunk], pre[:, chunk:]
    hidden_grad = dot(u_ref[...], wd_ref[...], (1, 1))
    sigmoid = 1.0 / (1.0 + jnp.exp(-gate_pre))
    activated = gate_pre * sigmoid
    hidden = activated * up_pre
    part = hidden * hidden_grad
    total = part[:, :128]
    for j in range(1, chunk // 128):
        total = total + part[:, j * 128 : (j + 1) * 128]
    lanes[...] += total
    hidden_low = (weight * hidden).astype(BF16)
    hidden_grad = weight * hidden_grad
    gate_low = (hidden_grad * up_pre * (sigmoid + activated * (1.0 - sigmoid))).astype(BF16)
    up_low = (hidden_grad * activated).astype(BF16)
    hidden_ref[...] = hidden_low
    both_ref[:, :chunk] = gate_low
    both_ref[:, chunk:] = up_low
    out_acc[...] += dot(hidden_low, wd_ref[...], (1, 0))
    row_acc[...] += dot(both_ref[...], both_w[...], (1, 1))

    @pl.when(step == pl.num_programs(1) - 1)
    def _():
        sums = jnp.sum(lanes[...], axis=-1, keepdims=True)
        gate_ref[...] += jnp.where(lane == first + e, sums, 0.0)
        out_ref[...] = out_acc[...].astype(BF16)
        row_ref[...] = row_acc[...].astype(BF16)


def run_rows(token, at, first, count, x, u, mask, router, w_gate, w_up, w_down, *ready):
    rows, width = x.shape
    ff = w_gate.shape[2]
    steps = ff // CHUNK

    def whole(shape):
        return pl.BlockSpec(
            shape, lambda e, s, a: (0,) * len(shape), pipeline_mode=pl.Buffered(1)
        )

    return pl.pallas_call(
        functools.partial(rows_kernel, first),
        grid_spec=pltpu.PrefetchScalarGridSpec(
            num_scalar_prefetch=1,
            grid=(count, steps),
            in_specs=[
                whole((rows, width)),
                whole((rows, width)),
                whole((rows, 128)),
                whole((width, 128)),
                pl.BlockSpec((None, width, CHUNK), lambda e, s, a: (first + e, 0, s)),
                pl.BlockSpec((None, width, CHUNK), lambda e, s, a: (first + e, 0, s)),
                pl.BlockSpec((None, CHUNK, width), lambda e, s, a: (first + e, s, 0)),
            ]
            + [ANYWHERE] * (1 + len(ready)),
            out_specs=[
                whole((rows, width)),
                whole((rows, width)),
                whole((rows, 128)),
                whole((rows, 128)),
                whole((width, rows)),
                pl.BlockSpec((None, None, rows, 2 * CHUNK), lambda e, s, a: (e, s, 0, 0)),
                pl.BlockSpec((None, None, rows, CHUNK), lambda e, s, a: (e, s, 0, 0)),
                token_spec(),
            ],
            scratch_shapes=[
                pltpu.VMEM((rows, width), F32),
                pltpu.VMEM((rows, width), F32),
                pltpu.VMEM((rows, 128), F32),
                pltpu.VMEM((width, 2 * CHUNK), BF16),
            ],
        ),
        out_shape=[
            jax.ShapeDtypeStruct((rows, width), BF16),
            jax.ShapeDtypeStruct((rows, width), BF16),
            jax.ShapeDtypeStruct((rows, 128), F32),
            jax.ShapeDtypeStruct((rows, 128), F32),
            jax.ShapeDtypeStruct((width, rows), BF16),
            jax.ShapeDtypeStruct((count, steps, rows, 2 * CHUNK), BF16),
            jax.ShapeDtypeStruct((count, steps, rows, CHUNK), BF16),
            TOKEN,
        ],
        compiler_params=pltpu.CompilerParams(vmem_limit_bytes=56 * MIB),
        cost_estimate=pl.CostEstimate(
            flops=12 * rows * width * ff * count,
            bytes_accessed=6 * width * ff * count,
            transcendentals=rows * ff * count,
        ),
        name="rows",
    )(at, x, u, mask, router, w_gate, w_up, w_down, token, *ready)


def grads_kernel(sizes, *refs):
    n = len(sizes)
    turned, ups, boths, hiddens = (refs[i * n : (i + 1) * n] for i in range(4))
    gate_ref, up_ref, down_ref, token_ref, x_all, u_all, both, hidden = refs[-8:]
    token_ref[...] = jnp.zeros_like(token_ref)
    width, chunk = x_all.shape[0], hidden.shape[1]

    spans, at = [], 0
    for size in sizes:
        spans.append(slice(at, at + size))
        at += size

    @pl.when(pl.program_id(0) == 0)
    def _():
        for span, t, u in zip(spans, turned, ups):
            x_all[:, span] = t[...]
            u_all[span, :] = u[...]

    for span, b, h in zip(spans, boths, hiddens):
        both[span, :] = b[...]
        hidden[span, :] = h[...]
    hidden_turned = hidden[...].T
    piece = width // 4
    for p in range(4):
        r = slice(p * piece, (p + 1) * piece)
        got = dot(x_all[r, :], both[...], (1, 0)).astype(BF16)
        gate_ref[r, :] = got[:, :chunk]
        up_ref[r, :] = got[:, chunk:]
        down_ref[:, r] = dot(hidden_turned, u_all[:, r], (1, 0)).astype(BF16)


def run_grads(token, segments):
    turned, ups, boths, hiddens, places = zip(*segments)
    width = turned[0].shape[0]
    sizes = tuple(u.shape[0] for u in ups)
    total = sum(sizes)
    steps = boths[0].shape[1]

    def whole(shape):
        return pl.BlockSpec(shape, lambda s: (0, 0), pipeline_mode=pl.Buffered(1))

    def chunked(size, columns, place):
        return pl.BlockSpec((None, None, size, columns), lambda s: (place, s, 0, 0))

    return pl.pallas_call(
        functools.partial(grads_kernel, sizes),
        grid=(steps,),
        in_specs=[whole((width, size)) for size in sizes]
        + [whole((size, width)) for size in sizes]
        + [chunked(size, 2 * CHUNK, p) for size, p in zip(sizes, places)]
        + [chunked(size, CHUNK, p) for size, p in zip(sizes, places)]
        + [ANYWHERE],
        out_specs=[
            pl.BlockSpec((width, CHUNK), lambda s: (0, s)),
            pl.BlockSpec((width, CHUNK), lambda s: (0, s)),
            pl.BlockSpec((CHUNK, width), lambda s: (s, 0)),
            token_spec(),
        ],
        out_shape=[
            jax.ShapeDtypeStruct((width, steps * CHUNK), BF16),
            jax.ShapeDtypeStruct((width, steps * CHUNK), BF16),
            jax.ShapeDtypeStruct((steps * CHUNK, width), BF16),
            TOKEN,
        ],
        scratch_shapes=[
            pltpu.VMEM((width, total), BF16),
            pltpu.VMEM((total, width), BF16),
            pltpu.VMEM((total, 2 * CHUNK), BF16),
            pltpu.VMEM((total, CHUNK), BF16),
        ],
        compiler_params=pltpu.CompilerParams(vmem_limit_bytes=56 * MIB),
        cost_estimate=pl.CostEstimate(
            flops=6 * total * width * steps * CHUNK,
            bytes_accessed=6 * width * steps * CHUNK + 8 * total * width,
            transcendentals=0,
        ),
        name="grads",
    )(*turned, *ups, *boths, *hiddens, token)


def place_kernel(*refs):
    outs, token_ref = refs[-4:-1], refs[-1]
    token_ref[...] = jnp.zeros_like(token_ref)
    for low, out in zip(refs[:3], outs):
        out[...] = low[...].astype(F32)


def place_grads(token, e, summed, outs, shapes):
    steps = 8

    def cut(shape):
        return pl.BlockSpec((shape[0] // steps, shape[1]), lambda i: (i, 0))

    def cut_out(shape):
        return pl.BlockSpec((None, shape[1] // steps, shape[2]), lambda i: (e, i, 0))

    held = [] if outs is None else list(outs[:3])
    return pl.pallas_call(
        place_kernel,
        grid=(steps,),
        in_specs=[cut(v.shape) for v in summed] + [ANYWHERE] * (1 + len(held)),
        out_specs=[cut_out(s) for s in shapes] + [token_spec()],
        out_shape=[jax.ShapeDtypeStruct(s, F32) for s in shapes] + [TOKEN],
        input_output_aliases={4 + i: i for i in range(len(held))},
        compiler_params=pltpu.CompilerParams(vmem_limit_bytes=60 * MIB),
        cost_estimate=pl.CostEstimate(
            flops=0,
            bytes_accessed=6 * sum(math.prod(v.shape) for v in summed),
            transcendentals=0,
        ),
        name="place",
    )(*summed, token, *held)


def split_kernel(sizes, bits_ref, *refs):
    n = len(sizes)
    turned, ups, boths, hiddens = (refs[i * n : (i + 1) * n] for i in range(4))
    sends = refs[4 * n + 1 : 4 * n + 5]
    keep_ref, token_ref, x_all, u_all, both, hidden = refs[4 * n + 5 :]
    token_ref[...] = jnp.zeros_like(token_ref)
    step = pl.program_id(0)
    width = x_all.shape[0]
    chunk = hidden.shape[1]

    spans, at = [], 0
    for size in sizes:
        spans.append(slice(at, at + size))
        at += size

    @pl.when(step == 0)
    def _():
        for span, t, u in zip(spans, turned, ups):
            x_all[:, span] = t[...]
            u_all[span, :] = u[...]

    for span, b, h in zip(spans, boths, hiddens):
        both[span, :] = b[...]
        hidden[span, :] = h[...]
    hidden_turned = hidden[...].T
    piece_rows = width // PIECES

    def store(mask, place_of):
        for place in range(PIECES):
            ref = place_of(place)
            p = place ^ mask
            r = pl.ds(pl.multiple_of(p * piece_rows, piece_rows), piece_rows)
            got = dot(x_all[r, :], both[...], (1, 0)).astype(BF16)
            ref[0] = got[:, :chunk]
            ref[1] = got[:, chunk:]
            down = dot(hidden_turned, u_all[:, r], (1, 0)).astype(BF16)
            for j in range(piece_rows // chunk):
                ref[2, j * chunk : (j + 1) * chunk, :] = down[:, j * chunk : (j + 1) * chunk]

    def sent(path):
        store(bits_ref[1 + path], lambda place: sends[path * 2 + place // 2].at[place % 2])

    pl.when(step == 0)(functools.partial(sent, 0))
    pl.when(step == 1)(functools.partial(sent, 1))

    @pl.when(step >= 2)
    def _():
        mask = jnp.where(step % 2 == 0, bits_ref[1], bits_ref[2])
        store(mask, lambda place: keep_ref.at[0, place])


def run_split(token, segments, bits):
    turned, ups, boths, hiddens, places = zip(*segments)
    width = turned[0].shape[0]
    sizes = tuple(u.shape[0] for u in ups)
    total = sum(sizes)
    steps = boths[0].shape[1]
    half = steps // 2
    piece_rows = width // PIECES

    def chunk_at(s, b):
        return ((1 - s // half) ^ b[0]) * half + s % half

    def whole(shape):
        return pl.BlockSpec(shape, lambda s, b: (0, 0), pipeline_mode=pl.Buffered(1))

    def chunked(size, columns, place):
        return pl.BlockSpec(
            (None, None, size, columns), lambda s, b: (place, chunk_at(s, b), 0, 0)
        )

    grads = (1, PIECES, 3, piece_rows, CHUNK)
    away = (PIECES // 2,) + grads[2:]
    grads_out = jax.ShapeDtypeStruct((half,) + grads[1:], BF16)
    return pl.pallas_call(
        functools.partial(split_kernel, sizes),
        grid_spec=pltpu.PrefetchScalarGridSpec(
            num_scalar_prefetch=1,
            grid=(steps,),
            in_specs=[whole((width, size)) for size in sizes]
            + [whole((size, width)) for size in sizes]
            + [chunked(size, 2 * CHUNK, p) for size, p in zip(sizes, places)]
            + [chunked(size, CHUNK, p) for size, p in zip(sizes, places)]
            + [ANYWHERE],
            out_specs=[
                pl.BlockSpec(away, lambda s, b: (0, 0, 0, 0), pipeline_mode=pl.Buffered(1))
                for _ in range(4)
            ]
            + [
                pl.BlockSpec(grads, lambda s, b: (jnp.maximum(s - half, 0), 0, 0, 0, 0)),
                token_spec(),
            ],
            scratch_shapes=[
                pltpu.VMEM((width, total), BF16),
                pltpu.VMEM((total, width), BF16),
                pltpu.VMEM((total, 2 * CHUNK), BF16),
                pltpu.VMEM((total, CHUNK), BF16),
            ],
        ),
        out_shape=[jax.ShapeDtypeStruct(away, BF16)] * 4 + [grads_out, TOKEN],
        compiler_params=pltpu.CompilerParams(vmem_limit_bytes=56 * MIB),
        cost_estimate=pl.CostEstimate(
            flops=6 * total * width * steps * CHUNK,
            bytes_accessed=6 * width * steps * CHUNK + 8 * total * width,
            transcendentals=0,
        ),
        name="split",
    )(bits, *turned, *ups, *boths, *hiddens, token)


def add_kernel(picks, joined, *refs):
    *refs, token_ref = refs
    token_ref[...] = jnp.zeros_like(token_ref)
    outs = [refs[-1].at[i] for i in range(len(picks))] if joined else refs[-len(picks) :]

    def at(ref, index):
        return ref[index] if index is not None else ref[...]

    for out, terms in zip(outs, picks):
        left, right = (at(refs[i], index) for i, index in terms)
        out[...] = (left.astype(F32) + right.astype(F32)).astype(BF16)


def add_pieces(token, picks, shapes, ins, joined=False):

    parts = 4

    def cut(shape):
        block = shape[:-2] + (shape[-2] // parts, shape[-1])
        return pl.BlockSpec(block, lambda i: (0,) * (len(shape) - 2) + (i, 0))

    moved = sum(i.size for i in ins) + sum(math.prod(s) for s in shapes)
    return pl.pallas_call(
        functools.partial(add_kernel, picks, joined),
        grid=(parts,),
        in_specs=[cut(i.shape) for i in ins] + [ANYWHERE],
        out_specs=[cut(s) for s in shapes] + [token_spec()],
        out_shape=[jax.ShapeDtypeStruct(s, BF16) for s in shapes] + [TOKEN],
        compiler_params=pltpu.CompilerParams(vmem_limit_bytes=60 * MIB),
        cost_estimate=pl.CostEstimate(flops=moved, bytes_accessed=2 * moved, transcendentals=0),
        name="add_pieces",
    )(*ins, token)


class Summed:
    def __init__(self, order, sends, keep):
        self.order, self.keep = order, keep
        self.ahead = ["halves", "quarters", "finals"]
        self.got = [swap(sends[i], "context", 1) for i in (1, 3, 0, 2)]

    def reach(self, name):
        while name in self.ahead:
            getattr(self, self.ahead.pop(0))()

    def add(self, picks, shapes, ins, joined=False):
        return self.order.run(add_pieces, picks, shapes, ins, joined)

    def halves(self):
        shape = (2,) + self.keep.shape[2:]
        picks = [
            [(0, (path, slice(at, at + 2))), (1 + i * 2 + path, None)]
            for i, at in enumerate((2, 0))
            for path in range(2)
        ]
        outs = self.add(picks, [shape] * 4, [self.keep, *self.got])
        self.coming = [swap(outs[path], *FIRST[path]) for path in range(2)]
        self.kept = outs[2:]

    def quarters(self):
        shape = self.keep.shape[2:]
        picks = [[(path, at), (2 + path, at)] for at in (1, 0) for path in range(2)]
        outs = self.add(picks, [shape] * 4, [*self.kept, *self.coming])
        self.coming = [swap(outs[path], *SECOND[path]) for path in range(2)]
        self.kept = outs[2:]

    def finals(self):
        shape = self.keep.shape[2:]
        picks = [[(path, None), (2 + path, None)] for path in range(2)]
        own = self.add(picks, [(2,) + shape], [*self.kept, *self.coming], True)[0]
        self.all = lax.all_gather(own, ("context", "dp"), axis=0)


def place_pieces_kernel(e, first, *refs):
    source = refs[0]
    outs = refs[2:5] if first else refs[5:8]
    token_ref, low, wide, in_sem, out_sem = refs[-5:]
    rows = low.shape[2]
    count = 2 * source.shape[0]
    token_ref[...] = jnp.zeros_like(token_ref)

    def fetch(i):
        return pltpu.make_async_copy(source.at[i // 2, i % 2], low.at[i % 2], in_sem.at[i % 2])

    def drain(i):
        path, member = i % 2, i // 2
        side, core, dp = member // 4, member // 2 % 2, member % 2
        chunk = core * 2 + path
        piece = (dp * 2 + side, side * 2 + dp)[path]
        columns = pl.ds(chunk * CHUNK, CHUNK)
        copies = []
        for k in range(2):
            copies.append(
                pltpu.make_async_copy(
                    wide.at[i % 2, k],
                    outs[k].at[e, pl.ds(piece * rows, rows), columns],
                    out_sem.at[i % 2, k],
                )
            )
        for j in range(rows // CHUNK):
            copies.append(
                pltpu.make_async_copy(
                    wide.at[i % 2, 2, pl.ds(j * CHUNK, CHUNK)],
                    outs[2].at[e, columns, pl.ds(piece * rows + j * CHUNK, CHUNK)],
                    out_sem.at[i % 2, 2 + j],
                )
            )
        return copies

    fetch(0).start()
    for i in range(count):
        if i + 1 < count:
            fetch(i + 1).start()
        fetch(i).wait()
        if i >= 2:
            for copy in drain(i - 2):
                copy.wait()
        for k in range(3):

            @pl.loop(0, rows // 64)
            def _(t):
                r = pl.ds(pl.multiple_of(t * 64, 64), 64)
                wide[i % 2, k, r, :] = low[i % 2, k, r, :].astype(F32)

        for copy in drain(i):
            copy.start()
    for i in (count - 2, count - 1):
        for copy in drain(i):
            copy.wait()


def place_pieces(token, e, gathered, outs, shapes):
    first = outs is None
    rows = gathered.shape[3]
    operands = [gathered, token] + ([] if first else list(outs[:3]))
    return pl.pallas_call(
        functools.partial(place_pieces_kernel, e, first),
        in_specs=[ANYWHERE] * len(operands),
        out_specs=[ANYWHERE] * 3 + [token_spec()],
        scratch_shapes=[
            pltpu.VMEM((2, 3, rows, CHUNK), BF16),
            pltpu.VMEM((2, 3, rows, CHUNK), F32),
            pltpu.SemaphoreType.DMA((2,)),
            pltpu.SemaphoreType.DMA((2, 2 + rows // CHUNK)),
        ],
        out_shape=[jax.ShapeDtypeStruct(s, F32) for s in shapes] + [TOKEN],
        input_output_aliases={} if first else {2: 0, 3: 1, 4: 2},
        compiler_params=pltpu.CompilerParams(vmem_limit_bytes=60 * MIB),
        cost_estimate=pl.CostEstimate(
            flops=0, bytes_accessed=16 * 9 * rows * CHUNK * 2, transcendentals=0
        ),
        name="place_pieces",
    )(*operands)


def hop_kernel(*refs):
    *parts, got, _, out_ref, token_ref = refs
    token_ref[...] = jnp.zeros_like(token_ref)
    total = parts[0][...].astype(F32)
    for part in parts[1:]:
        total = total + part[...].astype(F32)
    out_ref[...] = (total + got[...].astype(F32)).astype(BF16)


def hop_add(token, parts, got):
    rows, width = got.shape
    half = rows // 2

    def at(place):
        return pl.BlockSpec((half, width), lambda i: (2 * place + i, 0))

    return pl.pallas_call(
        hop_kernel,
        grid=(2,),
        in_specs=[at(p) for _, p in parts] + [at(0), ANYWHERE],
        out_specs=[at(0), token_spec()],
        out_shape=[jax.ShapeDtypeStruct((rows, width), BF16), TOKEN],
        compiler_params=pltpu.CompilerParams(vmem_limit_bytes=60 * MIB),
        cost_estimate=pl.CostEstimate(
            flops=rows * width * 5, bytes_accessed=14 * rows * width, transcendentals=0
        ),
        name="hop",
    )(*(a for a, _ in parts), got, token)


def body(
    hidden_in,
    out_grad,
    routes,
    attn_gain,
    w_query,
    w_key,
    w_value,
    q_gain,
    k_gain,
    w_out,
    ffn_gain,
    w_router,
    w_gate,
    w_up,
    w_down,
):
    groups = lax.axis_size("expert")
    context = lax.axis_size("context")
    my_group = lax.axis_index("expert")
    my_context = lax.axis_index("context")
    my_dp = lax.axis_index("dp")
    tokens = hidden_in.shape[1]
    width = hidden_in.shape[2]
    rows = w_query.shape[0]
    local_experts = w_gate.shape[0]
    experts_all = w_router.shape[1]
    length = tokens * context
    per = HEADS // context
    local = per * HDIM
    core, side = my_context % 2, my_context // 2
    bits = jnp.stack([core, my_dp * 2 + side, side * 2 + my_dp]).astype(jnp.int32)
    ring = [(my_group - s) % groups for s in range(groups)]
    members = [my_context ^ s for s in range(context)]

    def half_columns(weight):
        split = weight.reshape(rows, 2, per // 2, context, HDIM)
        split = lax.dynamic_index_in_dim(split, my_dp, 1, keepdims=False)
        return split.transpose(2, 0, 1, 3).reshape(context, rows, local // 2)

    columns = jnp.concatenate([half_columns(w) for w in (w_query, w_key, w_value)], axis=2)
    pieces = [lax.dynamic_index_in_dim(columns, m, 0, keepdims=False) for m in members]
    pieces = [pieces[0]] + [swap(pieces[s], "context", s) for s in range(1, context)]
    half_w = take(jnp.stack(pieces), members).reshape(context * rows, 3 * local // 2)
    small = jnp.concatenate(
        [attn_gain[None], q_gain[None], k_gain[None], ffn_gain[None], w_router.T], axis=0
    )
    small = [small] + [swap(small, "context", s) for s in range(1, context)]
    small = take(jnp.stack(small), members)
    hidden_all = after(hidden_in[0], half_w)
    hidden_all = jnp.concatenate(context_gather(hidden_all), axis=0)
    small = take(jnp.stack(ring_direct(small)), ring)
    small_all = small.transpose(2, 0, 1, 3).reshape(4 + experts_all, width)
    halves, others = [half_w], [swap(half_w, "dp", 1)]
    for s in range(1, groups):
        halves.append(shift(halves[-1], 1))
        others.append(swap(halves[-1], "dp", 1))
    some = local // 2
    qkv_w = jnp.concatenate(
        [
            jnp.concatenate(
                [w[:, i * some : (i + 1) * some] for i in range(3) for w in pair], axis=1
            )
            for pair in zip(halves, others)
        ],
        axis=0,
    )
    heads = [my_dp * 2, my_dp * 2 + 1, (1 - my_dp) * 2, (1 - my_dp) * 2 + 1]
    whole_heads = rows == HDIM
    routes_ring = ring_direct(after(routes[0], halves[1 % groups]))
    if whole_heads:
        out_all = lax.all_gather(after(w_out, halves[-1]), "expert", axis=0)
    upstream_all = lax.all_gather(after(out_grad[0], halves[-1]), "expert", axis=0)

    gain_attn = small_all[0].astype(F32)
    gain_ffn = small_all[3].astype(F32)
    router_w = small_all[4:]
    router_wide = jnp.pad(router_w.T, ((0, 0), (0, 128 - experts_all)))

    def mine(vector):
        table = vector.reshape(per, context, HDIM)
        table = lax.dynamic_index_in_dim(table, my_context, 1, keepdims=False)
        return take(table, heads).astype(F32)

    gain_query, gain_key = mine(small_all[1]), mine(small_all[2])
    block = width // groups

    def to_ring(values):
        parts = [lax.dynamic_slice_in_dim(values, m * block, block, axis=1) for m in ring]
        return jnp.concatenate(parts, axis=1)

    source_all = hidden_all.astype(F32)
    factor_all = rms_factor(source_all)
    normed = to_ring((source_all * factor_all * gain_attn).astype(BF16))
    source = hidden_in[0].astype(F32)
    factor_one = rms_factor(source)
    qkv = dot(normed, after(qkv_w, *routes_ring[1:]), (1, 0))

    def slots(query, key):
        return jnp.stack([v.reshape(context, tokens) for v in (query, key)])

    def per_row(values):
        return values.reshape(length)[:, None]

    squares = [jnp.sum(jnp.square(qkv[:, i * local : (i + 1) * local]), axis=-1) for i in range(2)]
    squares = context_total(slots(*squares))
    factors = lax.rsqrt(squares / width + epsilon)
    factor_query, factor_key = per_row(factors[0]), per_row(factors[1])
    starts = jnp.stack([m * tokens for m in members])
    positions = (starts[:, None] + jnp.arange(tokens, dtype=jnp.int32)).reshape(length).astype(F32)
    frequency = rope_base ** (-jnp.arange(HDIM // 2, dtype=F32) * 2.0 / HDIM)
    angles = positions[:, None] * frequency[None, :]
    cosine = jnp.tile(jnp.cos(angles), (1, 2))
    sine_part = jnp.sin(angles)
    sine_part = jnp.concatenate([-sine_part, sine_part], axis=1)
    turn = (factor_query, factor_key, gain_query[:, None], gain_key[:, None], cosine, sine_part)
    query_low, key_low, value_low, mixed_low, logsum = attend(qkv, *turn, [])
    if whole_heads:
        out_w = take(out_all, heads).reshape(local, width)
    else:
        out_w = lax.all_gather(w_out, ("expert", "context"), axis=0, tiled=True)
        out_w = out_w.reshape(per, context, HDIM, width)
        out_w = lax.dynamic_index_in_dim(out_w, my_context, 1, keepdims=False)
        out_w = take(out_w, heads).reshape(local, width)
    ids = jnp.arange(128, dtype=jnp.int32)
    masks = [jnp.any(r[:, :, None] == ids, axis=1).astype(F32) for r in routes_ring]
    mixed_out = dot(mixed_low, out_w, (1, 0)).astype(BF16).reshape(context, tokens, width)
    residual = source + context_sum([mixed_out[s] for s in range(context)])
    factor_two = rms_factor(residual)
    normed_two = (residual * factor_two * gain_ffn).astype(BF16)

    at = jnp.reshape(my_group * local_experts, (1,)).astype(jnp.int32)
    order = Order()

    def rows_of(first, count, x, u, mask, *ready):
        return order.run(
            run_rows, at, first, count, x, u, mask, router_wide, w_gate, w_up, w_down, *ready
        )

    near = [[(0, local_experts)], [(0, local_experts)]]
    if local_experts == 4:
        near = [[(0, 2), (2, 2)]] * 2
    blocks = ring_gather(normed_two)
    segments = [([0], []), ([1], [])]

    ups = [out_grad[0]]

    def upstream_of(slot):
        m = ring[slot] + order.token[0, 0].astype(jnp.int32)
        return lax.dynamic_index_in_dim(upstream_all, m, 0, keepdims=False)

    def near_rows(slot, i):
        first, count = near[slot][i]
        ready = [upstream_all] if (slot, i) == (0, 1) else []
        result = rows_of(first, count, blocks[slot], ups[slot], masks[slot], *ready)
        segments[slot][1].append((first, count, result))

    for slot in range(2):
        if slot == 1:
            ups.append(upstream_of(1))
        for i in range(len(near[slot])):
            if (slot, i) != (1, 1):
                near_rows(slot, i)
    far = []
    for slot in range(2, groups, 2):
        pair = [slot, slot + 1]
        x, u, mask = (
            jnp.concatenate(v, axis=0)
            for v in (
                [blocks[s] for s in pair],
                [upstream_of(s) for s in pair],
                [masks[s] for s in pair],
            )
        )
        far.append((x, u, mask))
        segments.append((pair, []))
        ups.append(u)

    def segment_of(segment, e):
        for first, count, result in segments[segment][1]:
            if first <= e < first + count:
                return (result[4], ups[segment], result[5], result[6], e - first)

    summed = []

    def sum_grads():
        e = len(summed)
        if e == local_experts:
            return
        call = functools.partial(run_split, bits=bits) if e else run_grads
        bunches = [[0, 1, 2]] + [[s, s + 1] for s in range(3, len(segments), 2)]
        results = []
        for bunch in bunches:
            bunch = [segment_of(s, e) for s in bunch if s < len(segments)]
            results.append(order.run(call, bunch))
        grads = [
            total_low(list(terms)) if len(terms) > 1 else terms[0] for terms in zip(*results)
        ]
        if e:
            summed.append(Summed(order, grads[:4], grads[4]))
        else:
            summed.append(lax.psum(grads, ("context", "dp")))

    def advance(*events):
        for e, name in events:
            if e < local_experts:
                summed[e].reach(name)

    def parts_of(slot, index):
        for pair, calls in segments:
            if slot in pair:
                return [(result[index], pair.index(slot)) for _, _, result in calls]

    def hop(index, total, slot):
        return order.run(hop_add, parts_of(slot % groups, index), shift(total, 1))[0]

    def first_hop(index):
        return total_low([r[p * tokens : (p + 1) * tokens] for r, p in parts_of(1, index)])

    for e in range(local_experts):
        for i, (x, u, mask) in enumerate(far):
            segments[2 + i][1].append((e, 1, rows_of(e, 1, x, u, mask)))
        if e < 2:
            sum_grads()
        if e == 0 and len(near[1]) > 1:
            near_rows(1, 1)
        if e == 2:
            advance((1, "halves"))
    row_total = hop(1, first_hop(1), 2)
    sum_grads()
    advance((1, "quarters"))

    gate_grad = [
        functools.reduce(
            lambda a, b: a + b,
            [result[2][pair.index(s) * tokens : (pair.index(s) + 1) * tokens] for _, _, result in calls],
        )
        for pair, calls in segments
        for s in pair
    ]
    gate_grad = [g[:, :local_experts].T for g in gate_grad]
    gate_grad = jnp.stack([gate_grad[0]] + [shift(gate_grad[s], -s) for s in range(1, groups)])
    gate_grad = take(gate_grad, [(g - my_group) % groups for g in range(groups)])
    gate_grad = gate_grad.reshape(experts_all, tokens).T

    for slot in range(3, groups + 1):
        row_total = hop(1, row_total, slot)
        if slot == 3:
            sum_grads()
            advance((1, "finals"), (2, "halves"))
    row_back = row_total.astype(F32)
    shapes = (w_gate.shape, w_up.shape, w_down.shape)
    expert_grads = None

    def place(experts):
        outs = expert_grads
        for e in experts:
            if e < local_experts:
                if e:
                    summed[e].reach("finals")
                    outs = order.run(place_pieces, e, summed[e].all, outs, shapes)
                else:
                    outs = order.run(place_grads, e, summed[e], outs, shapes)
        return outs


    upstream = out_grad[0].astype(F32)
    weights_own = segments[0][1][0][2][3][:, :experts_all]
    weighted = jnp.sum(weights_own * gate_grad, axis=-1, keepdims=True)
    logit_grad = (weights_own * (gate_grad - weighted)).astype(BF16)
    router_grad = dot(logit_grad, normed_two, (0, 0))
    normed_two_grad = dot(logit_grad, router_w, (1, 0)) + row_back
    residual_part, ffn_gain_grad = norm_back(normed_two_grad, residual, factor_two, gain_ffn)
    residual_grad = upstream + residual_part

    attn_grad = context_gather(residual_grad.astype(BF16))
    out_total = hop(0, first_hop(0), 2)
    attn_grad = jnp.concatenate(attn_grad, axis=0)
    mixed_grad = dot(attn_grad, out_w, (1, 1)).astype(BF16)
    query_back, key_back, value_grad, query_sum, key_sum, q_gain_grad, k_gain_grad = order.run(
        attend_back, query_low, key_low, value_low, mixed_grad, logsum, qkv, *turn
    )
    out_w_grad = dot(mixed_low, after(attn_grad, order.token), (0, 0)).astype(BF16)
    for slot in range(3, groups):
        out_total = hop(0, out_total, slot)
    sums = context_total(slots(jnp.sum(query_sum, axis=1), jnp.sum(key_sum, axis=1))) / width
    order.token = after(order.token, sums)
    advance((2, "quarters"), (3, "halves"))
    if groups > 2:
        out_total = hop(0, out_total, groups)
    hidden_out = (residual + out_total.astype(F32)).astype(BF16)[None]
    def low_grad(back, raw, factor, gain, total):
        return (
            factor * back * gain.reshape(1, local) - raw * factor**3 * per_row(total)
        ).astype(BF16)

    query_grad = low_grad(query_back, qkv[:, :local], factor_query, gain_query, sums[0])
    key_grad = low_grad(key_back, qkv[:, local : 2 * local], factor_key, gain_key, sums[1])
    qkv_grad = jnp.concatenate([query_grad, key_grad, value_grad], axis=1)
    qkv_w_grad = dot(normed, qkv_grad, (0, 0)).astype(BF16)
    normed_grad = dot(qkv_grad, qkv_w, (1, 1)).astype(BF16)
    order.token = after(order.token, qkv_w_grad, normed_grad)
    normed_grad = normed_grad.reshape(context, tokens, width)
    normed_grad = context_sum([normed_grad[s] for s in range(context)])

    class Ring:
        def __init__(self, terms):
            self.terms, self.size, self.slot = terms, terms.shape[0] // groups, 1
            at = 1 % groups * self.size
            self.total = terms[at : at + self.size]
            self.coming = shift(self.total, 1)

        def hop(self):
            if self.slot < groups:
                self.slot += 1
                self.total = order.run(hop_add, [(self.terms, self.slot % groups)], self.coming)[0]
                self.coming = shift(self.total, 1)

        def whole(self):
            while self.slot < groups:
                self.hop()
            return self.total

    qkv_ring = Ring(qkv_w_grad)
    advance((2, "finals"), (3, "quarters"))
    if whole_heads:
        ordered = take(
            out_w_grad.reshape(per, HDIM, width), [(m // 2 ^ my_dp) * 2 + m % 2 for m in ring]
        )
        out_ring = Ring(ordered.reshape(local, width))
        out_ring.hop()
        out_ring.hop()
    qkv_ring.hop()
    advance((3, "finals"))
    if whole_heads:
        mine_out = out_ring.whole()
        out_w_grad = mine_out.astype(F32) + swap(mine_out, "dp", 1).astype(F32)
    expert_grads = place([0])
    qkv_ring.hop()
    expert_grads = place([1, 2])
    qkv_w_grad = qkv_ring.whole()
    parts = [
        lax.dynamic_slice_in_dim(normed_grad, (my_group - m) % groups * block, block, axis=1)
        for m in range(groups)
    ]
    normed_grad = jnp.concatenate(parts, axis=1)
    source_part, attn_gain_grad = norm_back(normed_grad, source, factor_one, gain_attn)
    input_grad = (residual_grad + source_part).astype(BF16)[None]

    mine_w = qkv_w_grad.reshape(context, rows, 3, 2, some)
    got = swap(mine_w, "dp", 1)
    mine_w = jnp.stack(
        [add_low(mine_w[:, :, :, i], got[:, :, :, 1 - i]) for i in range(2)], axis=3
    )
    pieces = [lax.dynamic_index_in_dim(mine_w, m, 0, keepdims=False) for m in members]
    pieces = [pieces[0]] + [swap(pieces[s], "context", s) for s in range(1, context)]
    dense = take(jnp.stack(pieces), members)
    dense = jnp.where(my_dp == 0, dense, dense[:, :, :, ::-1]).astype(F32)
    dense = dense.reshape(context, rows, 3, per, HDIM).transpose(2, 1, 3, 0, 4)
    dense = dense.reshape(3, rows, width)
    if not whole_heads:
        spread = jnp.zeros((per, context, HDIM, width), BF16)
        for h in range(per):
            term = out_w_grad.reshape(per, HDIM, width)[h][None, None]
            spread = lax.dynamic_update_slice(spread, term, (heads[h], my_context, 0, 0))
        spread = lax.psum_scatter(
            spread.reshape(width, width), ("expert", "context"), scatter_dimension=0, tiled=True
        )
        out_w_grad = lax.psum(spread, "dp").astype(F32)
    gains = jnp.zeros((2, per, context, HDIM), F32)
    for h in range(per):
        pair = jnp.stack([q_gain_grad[h], k_gain_grad[h]])[:, None]
        gains = lax.dynamic_update_slice(gains, pair, (0, heads[h], my_context, 0))
    small_grad = jnp.concatenate(
        [attn_gain_grad[None], ffn_gain_grad[None], gains.reshape(2, width), router_grad], axis=0
    )
    small_grad = small_grad.reshape(4 + experts_all, groups, context, rows).transpose(1, 2, 0, 3)
    small_grad = take(small_grad, ring)
    small_grad = functools.reduce(
        lambda a, b: a + b,
        [small_grad[0]] + [shift(small_grad[s], -s) for s in range(1, groups)],
    )
    small_grad = take(small_grad, members)
    got = swap(jnp.stack([small_grad[1], small_grad[3]]), "context", 1)
    small_grad = small_grad[0] + got[0] + swap(small_grad[2] + got[1], "context", 2)
    small_grad = small_grad + swap(small_grad, "dp", 1)
    expert_grads = place([3])
    return (
        hidden_out,
        input_grad,
        small_grad[0],
        dense[0],
        dense[1],
        dense[2],
        small_grad[2],
        small_grad[3],
        out_w_grad,
        small_grad[1],
        small_grad[4:].T,
        expert_grads[0],
        expert_grads[1],
        expert_grads[2],
    )


def solution(mesh):
    tokens = P(("expert", "dp"), "context", None)
    vector = P(("expert", "context"))
    matrix = P(("expert", "context"), None)
    expert = P("expert", None, None)
    in_specs = (
        tokens,
        tokens,
        tokens,
        vector,
        matrix,
        matrix,
        matrix,
        vector,
        vector,
        matrix,
        vector,
        matrix,
        expert,
        expert,
        expert,
    )
    out_specs = (
        tokens,
        tokens,
        vector,
        matrix,
        matrix,
        matrix,
        vector,
        vector,
        matrix,
        vector,
        matrix,
        expert,
        expert,
        expert,
    )
    return jax.shard_map(body, mesh=mesh, in_specs=in_specs, out_specs=out_specs, check_vma=False)
```

```python
import functools
import math

import jax
import jax.numpy as jnp
from jax import lax
from jax.experimental import pallas as pl
from jax.experimental.pallas import tpu as pltpu
from jax.sharding import PartitionSpec as P

HEADS = 16
HDIM = 128
CHUNK = 256
ROWS = 1024

epsilon = 1e-06
rope_base = 10000.0
F32 = jnp.float32
BF16 = jnp.bfloat16
MIB = 1024 * 1024


def dot(left, right, contract):
    return lax.dot_general(
        left, right, (((contract[0],), (contract[1],)), ((), ())), preferred_element_type=F32
    )


def add_low(left, right):
    return (left.astype(F32) + right.astype(F32)).astype(BF16)


def total_low(terms):
    return functools.reduce(lambda a, b: a + b, [t.astype(F32) for t in terms]).astype(BF16)


FIRST = (("dp", 1), ("context", 2))
SECOND = (("context", 2), ("dp", 1))
PIECES = 4


def nothing_of(values, dtype):
    return (values[(0,) * values.ndim].astype(F32) * 0.0).astype(dtype)


def after(values, *others):
    for other in others:
        values = values + nothing_of(other, values.dtype)
    return values


ANYWHERE = pl.BlockSpec(memory_space=pl.ANY)
TOKEN = jax.ShapeDtypeStruct((8, 128), F32)


def token_spec():
    return pl.BlockSpec((8, 128), lambda *_: (0, 0))


class Order:
    def __init__(self):
        self.token = jnp.zeros((8, 128), F32)

    def run(self, call, *args):
        *results, self.token = call(self.token, *args)
        return results


def rms_factor(values):
    return lax.rsqrt(jnp.mean(values * values, axis=-1, keepdims=True) + epsilon)


def norm_back(grad_out, values, factor, gain_vector):
    scaled = grad_out * gain_vector
    grad_in = factor * scaled - values * factor**3 * jnp.mean(
        scaled * values, axis=-1, keepdims=True
    )
    gain_grad = jnp.sum(grad_out * values * factor, axis=0)
    return (grad_in, gain_grad)


def half_turn(values):
    return pltpu.roll(values, HDIM // 2, 1)


def attend_kernel(
    q_ref, k_ref, v_ref, fq_ref, fk_ref, gq_ref, gk_ref, cos_ref, sin_ref, *refs
):
    ql_ref, kl_ref, vl_ref, mixed_ref, logsum_ref = refs[-5:]
    length = q_ref.shape[0]
    block = min(256, length)
    cosine, sine = cos_ref[...], sin_ref[...]
    query = q_ref[...] * fq_ref[...] * gq_ref[0]
    key = k_ref[...] * fk_ref[...] * gk_ref[0]
    ql_ref[...] = (query * cosine + half_turn(query) * sine).astype(BF16)
    kl_ref[...] = (key * cosine + half_turn(key) * sine).astype(BF16)
    value = v_ref[...].astype(BF16)
    vl_ref[...] = value
    turned = value.T
    for b in range(length // block):
        r = slice(b * block, (b + 1) * block)
        scores = dot(kl_ref[...], ql_ref[r, :], (1, 1)) * HDIM ** (-0.5)
        top = jnp.max(scores, axis=0, keepdims=True)
        raised = jnp.exp(scores - top)
        total = jnp.sum(raised, axis=0, keepdims=True)
        mixed = dot(turned, raised.astype(BF16), (1, 0)) / total
        mixed_ref[r, :] = mixed.T.astype(BF16)
        logsum_ref[0, :, r] = top + jnp.log(total)


def attend_back_kernel(
    ql_ref, kl_ref, vl_ref, grad_ref, logsum_ref, q_ref, k_ref, fq_ref, fk_ref, gq_ref, gk_ref,
    cos_ref, sin_ref, _, qb_ref, kb_ref, vg_ref, qs_ref, ks_ref, qg_ref, kg_ref, token_ref,
    k_acc, v_acc, q_acc,
):
    token_ref[...] = jnp.zeros_like(token_ref)
    length = ql_ref.shape[0]
    block = min(256, length)
    scale = HDIM ** (-0.5)

    @pl.when(pl.program_id(0) == 0)
    def _():
        qs_ref[...] = jnp.zeros_like(qs_ref)
        ks_ref[...] = jnp.zeros_like(ks_ref)

    for b in range(length // block):
        r = slice(b * block, (b + 1) * block)
        query, grad = ql_ref[r, :], grad_ref[r, :]
        scores = dot(kl_ref[...], query, (1, 1)) * scale
        probs = jnp.exp(scores - logsum_ref[0, :, r])
        prob_grad = dot(vl_ref[...], grad, (1, 1))
        moved = jnp.sum(probs * prob_grad, axis=0, keepdims=True)
        score_grad = (probs * (prob_grad - moved)).astype(BF16)
        value_part = dot(probs.astype(BF16), grad, (1, 0))
        key_part = dot(score_grad, query, (1, 0))
        if b == 0:
            v_acc[...] = value_part
            k_acc[...] = key_part
        else:
            v_acc[...] += value_part
            k_acc[...] += key_part
        q_acc[r, :] = dot(score_grad, kl_ref[...], (0, 0))
    vg_ref[...] = v_acc[...].astype(BF16)
    cosine, sine = cos_ref[...], sin_ref[...]
    for acc, back_ref, raw_ref, f_ref, g_ref, sum_ref, gain_ref in (
        (q_acc, qb_ref, q_ref, fq_ref, gq_ref, qs_ref, qg_ref),
        (k_acc, kb_ref, k_ref, fk_ref, gk_ref, ks_ref, kg_ref),
    ):
        turned = acc[...] * scale
        back = turned * cosine - half_turn(turned) * sine
        product = back * raw_ref[...]
        back_ref[...] = back
        sum_ref[...] += product * g_ref[0]
        gain_ref[0] = jnp.sum(product * f_ref[...], axis=0, keepdims=True)


def head_specs(length):
    return {
        "head": pl.BlockSpec((length, HDIM), lambda h: (0, h)),
        "whole": pl.BlockSpec((length, HDIM), lambda h: (0, 0)),
        "column": pl.BlockSpec((length, 1), lambda h: (0, 0)),
        "gain": pl.BlockSpec((1, 1, HDIM), lambda h: (h, 0, 0)),
        "row": pl.BlockSpec((1, 1, length), lambda h: (h, 0, 0)),
    }


def attend(qkv, fq, fk, gq, gk, cosine, sine, before):
    length, heads = qkv.shape[0], gq.shape[0]
    spec = head_specs(length)

    def part(i):
        return pl.BlockSpec((length, HDIM), lambda h: (0, i * heads + h))

    low = jax.ShapeDtypeStruct((length, heads * HDIM), BF16)
    return pl.pallas_call(
        attend_kernel,
        grid=(heads,),
        in_specs=[part(0), part(1), part(2)]
        + [spec[n] for n in ("column", "column", "gain", "gain", "whole", "whole")]
        + [ANYWHERE] * len(before),
        out_specs=[spec["head"]] * 4 + [spec["row"]],
        out_shape=[low] * 4 + [jax.ShapeDtypeStruct((heads, 1, length), F32)],
        compiler_params=pltpu.CompilerParams(vmem_limit_bytes=60 * MIB),
        cost_estimate=pl.CostEstimate(
            flops=10 * heads * length * length * HDIM,
            bytes_accessed=20 * length * heads * HDIM,
            transcendentals=heads * length * length,
        ),
        name="attend",
    )(qkv, qkv, qkv, fq, fk, gq, gk, cosine, sine, *before)


def attend_back(token, ql, kl, vl, grad, logsum, qkv, fq, fk, gq, gk, cosine, sine):
    length, heads = qkv.shape[0], gq.shape[0]
    spec = head_specs(length)

    def part(i):
        return pl.BlockSpec((length, HDIM), lambda h: (0, i * heads + h))

    def shape(kind, *dims):
        return jax.ShapeDtypeStruct(dims, kind)

    return pl.pallas_call(
        attend_back_kernel,
        grid=(heads,),
        in_specs=[spec["head"]] * 4
        + [spec["row"], part(0), part(1)]
        + [spec[n] for n in ("column", "column", "gain", "gain", "whole", "whole")]
        + [ANYWHERE],
        out_specs=[spec["head"]] * 3 + [spec["whole"]] * 2 + [spec["gain"]] * 2 + [token_spec()],
        out_shape=[
            shape(F32, length, heads * HDIM),
            shape(F32, length, heads * HDIM),
            shape(BF16, length, heads * HDIM),
            shape(F32, length, HDIM),
            shape(F32, length, HDIM),
            shape(F32, heads, 1, HDIM),
            shape(F32, heads, 1, HDIM),
            TOKEN,
        ],
        scratch_shapes=[pltpu.VMEM((length, HDIM), F32)] * 3,
        compiler_params=pltpu.CompilerParams(vmem_limit_bytes=60 * MIB),
        cost_estimate=pl.CostEstimate(
            flops=20 * heads * length * length * HDIM,
            bytes_accessed=30 * length * heads * HDIM,
            transcendentals=heads * length * length,
        ),
        name="attend_back",
    )(ql, kl, vl, grad, logsum, qkv, qkv, fq, fk, gq, gk, cosine, sine, token)


def swap(values, axis, bit):
    return lax.ppermute(values, axis, [(i, i ^ bit) for i in range(lax.axis_size(axis))])


def shift(values, by):
    n = lax.axis_size("expert")
    return lax.ppermute(values, "expert", [(i, (i + by) % n) for i in range(n)])


def context_gather(own):
    far = swap(own, "context", 2)
    near = swap(own, "context", 1)
    return [own, near, far, swap(far, "context", 1)]


def context_terms(blocks):
    got = swap(jnp.stack([blocks[1], blocks[3]]), "context", 1)
    return blocks[0], got[0], swap(add_low(blocks[2], got[1]), "context", 2)


def context_sum(blocks):
    own, near, far = context_terms(blocks)
    return own.astype(F32) + near.astype(F32) + far.astype(F32)


def context_total(terms):
    got = swap(terms, "context", 1)
    terms = terms + jnp.stack([got[:, s ^ 1] for s in range(4)], axis=1)
    got = swap(terms, "context", 2)
    return terms + jnp.stack([got[:, s ^ 2] for s in range(4)], axis=1)


def ring_gather(own):
    held = [own]
    for _ in range(lax.axis_size("expert") - 1):
        held.append(shift(held[-1], 1))
    return held


def ring_direct(own):
    return [own] + [shift(own, s) for s in range(1, lax.axis_size("expert"))]


def take(blocks, index):
    return jnp.stack([lax.dynamic_index_in_dim(blocks, i, 0, keepdims=False) for i in index])


def rows_kernel(
    first,
    at_ref,
    x_ref,
    u_ref,
    mask_ref,
    router_ref,
    wg_ref,
    wu_ref,
    wd_ref,
    *refs,
):
    (
        out_ref,
        row_ref,
        gate_ref,
        weights_ref,
        turned_ref,
        both_ref,
        hidden_ref,
        token_ref,
        out_acc,
        row_acc,
        lanes,
        both_w,
    ) = refs[-12:]
    e, step = pl.program_id(0), pl.program_id(1)
    start = jnp.logical_and(e == 0, step == 0)
    rows, width = x_ref.shape
    chunk = wg_ref.shape[1]
    lane = lax.broadcasted_iota(jnp.int32, (rows, 128), 1)
    token_ref[...] = jnp.zeros_like(token_ref)

    @pl.when(start)
    def _():
        out_acc[...] = jnp.zeros_like(out_acc)
        row_acc[...] = jnp.zeros_like(row_acc)
        gate_ref[...] = jnp.zeros_like(gate_ref)
        turned_ref[...] = x_ref[...].T
        logits = dot(x_ref[...], router_ref[...], (1, 0))
        chosen = mask_ref[...] > 0.5
        top = jnp.max(jnp.where(chosen, logits, -1e30), axis=-1, keepdims=True)
        raised = jnp.where(chosen, jnp.exp(jnp.where(chosen, logits - top, 0.0)), 0.0)
        weights_ref[...] = raised / jnp.sum(raised, axis=-1, keepdims=True)

    @pl.when(step == 0)
    def _():
        lanes[...] = jnp.zeros_like(lanes)

    both_w[:, :chunk] = wg_ref[...]
    both_w[:, chunk:] = wu_ref[...]
    weight = jnp.sum(
        jnp.where(lane == at_ref[0] + first + e, weights_ref[...], 0.0), axis=-1, keepdims=True
    )
    pre = dot(x_ref[...], both_w[...], (1, 0))
    gate_pre, up_pre = pre[:, :chunk], pre[:, chunk:]
    hidden_grad = dot(u_ref[...], wd_ref[...], (1, 1))
    sigmoid = 1.0 / (1.0 + jnp.exp(-gate_pre))
    activated = gate_pre * sigmoid
    hidden = activated * up_pre
    part = hidden * hidden_grad
    total = part[:, :128]
    for j in range(1, chunk // 128):
        total = total + part[:, j * 128 : (j + 1) * 128]
    lanes[...] += total
    hidden_low = (weight * hidden).astype(BF16)
    hidden_grad = weight * hidden_grad
    gate_low = (hidden_grad * up_pre * (sigmoid + activated * (1.0 - sigmoid))).astype(BF16)
    up_low = (hidden_grad * activated).astype(BF16)
    hidden_ref[...] = hidden_low
    both_ref[:, :chunk] = gate_low
    both_ref[:, chunk:] = up_low
    out_acc[...] += dot(hidden_low, wd_ref[...], (1, 0))
    row_acc[...] += dot(both_ref[...], both_w[...], (1, 1))

    @pl.when(step == pl.num_programs(1) - 1)
    def _():
        sums = jnp.sum(lanes[...], axis=-1, keepdims=True)
        gate_ref[...] += jnp.where(lane == first + e, sums, 0.0)
        out_ref[...] = out_acc[...].astype(BF16)
        row_ref[...] = row_acc[...].astype(BF16)


def run_rows(token, at, first, count, x, u, mask, router, w_gate, w_up, w_down, *ready):
    rows, width = x.shape
    ff = w_gate.shape[2]
    steps = ff // CHUNK

    def whole(shape):
        return pl.BlockSpec(
            shape, lambda e, s, a: (0,) * len(shape), pipeline_mode=pl.Buffered(1)
        )

    return pl.pallas_call(
        functools.partial(rows_kernel, first),
        grid_spec=pltpu.PrefetchScalarGridSpec(
            num_scalar_prefetch=1,
            grid=(count, steps),
            in_specs=[
                whole((rows, width)),
                whole((rows, width)),
                whole((rows, 128)),
                whole((width, 128)),
                pl.BlockSpec((None, width, CHUNK), lambda e, s, a: (first + e, 0, s)),
                pl.BlockSpec((None, width, CHUNK), lambda e, s, a: (first + e, 0, s)),
                pl.BlockSpec((None, CHUNK, width), lambda e, s, a: (first + e, s, 0)),
            ]
            + [ANYWHERE] * (1 + len(ready)),
            out_specs=[
                whole((rows, width)),
                whole((rows, width)),
                whole((rows, 128)),
                whole((rows, 128)),
                whole((width, rows)),
                pl.BlockSpec((None, None, rows, 2 * CHUNK), lambda e, s, a: (e, s, 0, 0)),
                pl.BlockSpec((None, None, rows, CHUNK), lambda e, s, a: (e, s, 0, 0)),
                token_spec(),
            ],
            scratch_shapes=[
                pltpu.VMEM((rows, width), F32),
                pltpu.VMEM((rows, width), F32),
                pltpu.VMEM((rows, 128), F32),
                pltpu.VMEM((width, 2 * CHUNK), BF16),
            ],
        ),
        out_shape=[
            jax.ShapeDtypeStruct((rows, width), BF16),
            jax.ShapeDtypeStruct((rows, width), BF16),
            jax.ShapeDtypeStruct((rows, 128), F32),
            jax.ShapeDtypeStruct((rows, 128), F32),
            jax.ShapeDtypeStruct((width, rows), BF16),
            jax.ShapeDtypeStruct((count, steps, rows, 2 * CHUNK), BF16),
            jax.ShapeDtypeStruct((count, steps, rows, CHUNK), BF16),
            TOKEN,
        ],
        compiler_params=pltpu.CompilerParams(vmem_limit_bytes=56 * MIB),
        cost_estimate=pl.CostEstimate(
            flops=12 * rows * width * ff * count,
            bytes_accessed=6 * width * ff * count,
            transcendentals=rows * ff * count,
        ),
        name="rows",
    )(at, x, u, mask, router, w_gate, w_up, w_down, token, *ready)


def grads_kernel(sizes, *refs):
    n = len(sizes)
    turned, ups, boths, hiddens = (refs[i * n : (i + 1) * n] for i in range(4))
    gate_ref, up_ref, down_ref, token_ref, x_all, u_all, both, hidden = refs[-8:]
    token_ref[...] = jnp.zeros_like(token_ref)
    width, chunk = x_all.shape[0], hidden.shape[1]

    spans, at = [], 0
    for size in sizes:
        spans.append(slice(at, at + size))
        at += size

    @pl.when(pl.program_id(0) == 0)
    def _():
        for span, t, u in zip(spans, turned, ups):
            x_all[:, span] = t[...]
            u_all[span, :] = u[...]

    for span, b, h in zip(spans, boths, hiddens):
        both[span, :] = b[...]
        hidden[span, :] = h[...]
    hidden_turned = hidden[...].T
    piece = width // 4
    for p in range(4):
        r = slice(p * piece, (p + 1) * piece)
        got = dot(x_all[r, :], both[...], (1, 0)).astype(BF16)
        gate_ref[r, :] = got[:, :chunk]
        up_ref[r, :] = got[:, chunk:]
        down_ref[:, r] = dot(hidden_turned, u_all[:, r], (1, 0)).astype(BF16)


def run_grads(token, segments):
    turned, ups, boths, hiddens, places = zip(*segments)
    width = turned[0].shape[0]
    sizes = tuple(u.shape[0] for u in ups)
    total = sum(sizes)
    steps = boths[0].shape[1]

    def whole(shape):
        return pl.BlockSpec(shape, lambda s: (0, 0), pipeline_mode=pl.Buffered(1))

    def chunked(size, columns, place):
        return pl.BlockSpec((None, None, size, columns), lambda s: (place, s, 0, 0))

    return pl.pallas_call(
        functools.partial(grads_kernel, sizes),
        grid=(steps,),
        in_specs=[whole((width, size)) for size in sizes]
        + [whole((size, width)) for size in sizes]
        + [chunked(size, 2 * CHUNK, p) for size, p in zip(sizes, places)]
        + [chunked(size, CHUNK, p) for size, p in zip(sizes, places)]
        + [ANYWHERE],
        out_specs=[
            pl.BlockSpec((width, CHUNK), lambda s: (0, s)),
            pl.BlockSpec((width, CHUNK), lambda s: (0, s)),
            pl.BlockSpec((CHUNK, width), lambda s: (s, 0)),
            token_spec(),
        ],
        out_shape=[
            jax.ShapeDtypeStruct((width, steps * CHUNK), BF16),
            jax.ShapeDtypeStruct((width, steps * CHUNK), BF16),
            jax.ShapeDtypeStruct((steps * CHUNK, width), BF16),
            TOKEN,
        ],
        scratch_shapes=[
            pltpu.VMEM((width, total), BF16),
            pltpu.VMEM((total, width), BF16),
            pltpu.VMEM((total, 2 * CHUNK), BF16),
            pltpu.VMEM((total, CHUNK), BF16),
        ],
        compiler_params=pltpu.CompilerParams(vmem_limit_bytes=56 * MIB),
        cost_estimate=pl.CostEstimate(
            flops=6 * total * width * steps * CHUNK,
            bytes_accessed=6 * width * steps * CHUNK + 8 * total * width,
            transcendentals=0,
        ),
        name="grads",
    )(*turned, *ups, *boths, *hiddens, token)


def place_kernel(*refs):
    outs, token_ref = refs[-4:-1], refs[-1]
    token_ref[...] = jnp.zeros_like(token_ref)
    for low, out in zip(refs[:3], outs):
        out[...] = low[...].astype(F32)


def place_grads(token, e, summed, outs, shapes):
    steps = 8

    def cut(shape):
        return pl.BlockSpec((shape[0] // steps, shape[1]), lambda i: (i, 0))

    def cut_out(shape):
        return pl.BlockSpec((None, shape[1] // steps, shape[2]), lambda i: (e, i, 0))

    held = [] if outs is None else list(outs[:3])
    return pl.pallas_call(
        place_kernel,
        grid=(steps,),
        in_specs=[cut(v.shape) for v in summed] + [ANYWHERE] * (1 + len(held)),
        out_specs=[cut_out(s) for s in shapes] + [token_spec()],
        out_shape=[jax.ShapeDtypeStruct(s, F32) for s in shapes] + [TOKEN],
        input_output_aliases={4 + i: i for i in range(len(held))},
        compiler_params=pltpu.CompilerParams(vmem_limit_bytes=60 * MIB),
        cost_estimate=pl.CostEstimate(
            flops=0,
            bytes_accessed=6 * sum(math.prod(v.shape) for v in summed),
            transcendentals=0,
        ),
        name="place",
    )(*summed, token, *held)


def split_kernel(sizes, bits_ref, *refs):
    n = len(sizes)
    turned, ups, boths, hiddens = (refs[i * n : (i + 1) * n] for i in range(4))
    *sends, keep_ref, token_ref, x_all, u_all, both, hidden = refs[-10:]
    token_ref[...] = jnp.zeros_like(token_ref)
    step = pl.program_id(0)
    width = x_all.shape[0]
    chunk = hidden.shape[1]

    spans, at = [], 0
    for size in sizes:
        spans.append(slice(at, at + size))
        at += size

    @pl.when(step == 0)
    def _():
        for span, t, u in zip(spans, turned, ups):
            x_all[:, span] = t[...]
            u_all[span, :] = u[...]

    for span, b, h in zip(spans, boths, hiddens):
        both[span, :] = b[...]
        hidden[span, :] = h[...]
    hidden_turned = hidden[...].T
    piece_rows = width // PIECES

    def store(mask, place_of):
        for place in range(PIECES):
            ref = place_of(place)
            p = place ^ mask
            r = pl.ds(pl.multiple_of(p * piece_rows, piece_rows), piece_rows)
            got = dot(x_all[r, :], both[...], (1, 0)).astype(BF16)
            ref[0] = got[:, :chunk]
            ref[1] = got[:, chunk:]
            down = dot(hidden_turned, u_all[:, r], (1, 0)).astype(BF16)
            for j in range(piece_rows // chunk):
                ref[2, j * chunk : (j + 1) * chunk, :] = down[:, j * chunk : (j + 1) * chunk]

    def sent(path):
        store(bits_ref[1 + path], lambda place: sends[path * 2 + place // 2].at[place % 2])

    pl.when(step == 0)(functools.partial(sent, 0))
    pl.when(step == 1)(functools.partial(sent, 1))

    @pl.when(step >= 2)
    def _():
        mask = jnp.where(step % 2 == 0, bits_ref[1], bits_ref[2])
        store(mask, lambda place: keep_ref.at[0, place])


def run_split(token, segments, bits, ready=()):
    turned, ups, boths, hiddens, places = zip(*segments)
    width = turned[0].shape[0]
    sizes = tuple(u.shape[0] for u in ups)
    total = sum(sizes)
    steps = boths[0].shape[1]
    half = steps // 2
    piece_rows = width // PIECES

    def chunk_at(s, b):
        return ((1 - s // half) ^ b[0]) * half + s % half

    def whole(shape):
        return pl.BlockSpec(shape, lambda s, b: (0, 0), pipeline_mode=pl.Buffered(1))

    def chunked(size, columns, place):
        return pl.BlockSpec(
            (None, None, size, columns), lambda s, b: (place, chunk_at(s, b), 0, 0)
        )

    grads = (1, PIECES, 3, piece_rows, CHUNK)
    away = (PIECES // 2,) + grads[2:]
    grads_out = jax.ShapeDtypeStruct((half,) + grads[1:], BF16)
    return pl.pallas_call(
        functools.partial(split_kernel, sizes),
        grid_spec=pltpu.PrefetchScalarGridSpec(
            num_scalar_prefetch=1,
            grid=(steps,),
            in_specs=[whole((width, size)) for size in sizes]
            + [whole((size, width)) for size in sizes]
            + [chunked(size, 2 * CHUNK, p) for size, p in zip(sizes, places)]
            + [chunked(size, CHUNK, p) for size, p in zip(sizes, places)]
            + [ANYWHERE] * (1 + len(ready)),
            out_specs=[
                pl.BlockSpec(away, lambda s, b: (0, 0, 0, 0), pipeline_mode=pl.Buffered(1))
                for _ in range(4)
            ]
            + [
                pl.BlockSpec(grads, lambda s, b: (jnp.maximum(s - half, 0), 0, 0, 0, 0)),
                token_spec(),
            ],
            scratch_shapes=[
                pltpu.VMEM((width, total), BF16),
                pltpu.VMEM((total, width), BF16),
                pltpu.VMEM((total, 2 * CHUNK), BF16),
                pltpu.VMEM((total, CHUNK), BF16),
            ],
        ),
        out_shape=[jax.ShapeDtypeStruct(away, BF16)] * 4 + [grads_out, TOKEN],
        compiler_params=pltpu.CompilerParams(vmem_limit_bytes=56 * MIB),
        cost_estimate=pl.CostEstimate(
            flops=6 * total * width * steps * CHUNK,
            bytes_accessed=6 * width * steps * CHUNK + 8 * total * width,
            transcendentals=0,
        ),
        name="split",
    )(bits, *turned, *ups, *boths, *hiddens, token, *ready)


def add_kernel(picks, joined, *refs):
    *refs, token_ref = refs
    token_ref[...] = jnp.zeros_like(token_ref)
    outs = [refs[-1].at[i] for i in range(len(picks))] if joined else refs[-len(picks) :]

    def at(ref, index):
        return ref[index] if index is not None else ref[...]

    for out, terms in zip(outs, picks):
        left, right = (at(refs[i], index) for i, index in terms)
        out[...] = (left.astype(F32) + right.astype(F32)).astype(BF16)


def add_pieces(token, picks, shapes, ins, ready=(), joined=False):

    parts = 4

    def cut(shape):
        block = shape[:-2] + (shape[-2] // parts, shape[-1])
        return pl.BlockSpec(block, lambda i: (0,) * (len(shape) - 2) + (i, 0))

    moved = sum(i.size for i in ins) + sum(math.prod(s) for s in shapes)
    return pl.pallas_call(
        functools.partial(add_kernel, picks, joined),
        grid=(parts,),
        in_specs=[cut(i.shape) for i in ins] + [ANYWHERE] * (1 + len(ready)),
        out_specs=[cut(s) for s in shapes] + [token_spec()],
        out_shape=[jax.ShapeDtypeStruct(s, BF16) for s in shapes] + [TOKEN],
        compiler_params=pltpu.CompilerParams(vmem_limit_bytes=60 * MIB),
        cost_estimate=pl.CostEstimate(flops=moved, bytes_accessed=2 * moved, transcendentals=0),
        name="add_pieces",
    )(*ins, token, *ready)


class Summed:
    def __init__(self, order, sends, keep):
        self.order, self.keep = order, keep
        self.ahead = ["halves", "quarters", "finals"]
        self.got = [swap(sends[i], "context", 1) for i in (1, 3, 0, 2)]

    def reach(self, name):
        while name in self.ahead:
            getattr(self, self.ahead.pop(0))()

    ready = ()

    def add(self, picks, shapes, ins, joined=False):
        ready, self.ready = self.ready, ()
        return self.order.run(add_pieces, picks, shapes, ins, ready, joined)

    def halves(self):
        shape = (2,) + self.keep.shape[2:]
        picks = [
            [(0, (path, slice(at, at + 2))), (1 + i * 2 + path, None)]
            for i, at in enumerate((2, 0))
            for path in range(2)
        ]
        outs = self.add(picks, [shape] * 4, [self.keep, *self.got])
        self.coming = [swap(outs[path], *FIRST[path]) for path in range(2)]
        self.kept = outs[2:]

    def quarters(self):
        shape = self.keep.shape[2:]
        picks = [[(path, at), (2 + path, at)] for at in (1, 0) for path in range(2)]
        outs = self.add(picks, [shape] * 4, [*self.kept, *self.coming])
        self.coming = [swap(outs[path], *SECOND[path]) for path in range(2)]
        self.kept = outs[2:]

    def finals(self):
        shape = self.keep.shape[2:]
        picks = [[(path, None), (2 + path, None)] for path in range(2)]
        own = self.add(picks, [(2,) + shape], [*self.kept, *self.coming], True)[0]
        self.all = lax.all_gather(own, ("context", "dp"), axis=0)


DEEP = 4


def place_pieces_kernel(e, first, *refs):
    source = refs[0]
    outs = refs[2:5] if first else refs[5:8]
    token_ref, low, wide, in_sem, out_sem = refs[-5:]
    rows = low.shape[2]
    count = 2 * source.shape[0]
    token_ref[...] = jnp.zeros_like(token_ref)

    def fetch(i):
        return pltpu.make_async_copy(source.at[i // 2, i % 2], low.at[i % DEEP], in_sem.at[i % DEEP])

    def drain(i):
        path, member = i % 2, i // 2
        side, core, dp = member // 4, member // 2 % 2, member % 2
        chunk = core * 2 + path
        piece = (dp * 2 + side, side * 2 + dp)[path]
        columns = pl.ds(chunk * CHUNK, CHUNK)
        copies = []
        for k in range(2):
            copies.append(
                pltpu.make_async_copy(
                    wide.at[i % DEEP, k],
                    outs[k].at[e, pl.ds(piece * rows, rows), columns],
                    out_sem.at[i % DEEP, k],
                )
            )
        for j in range(rows // CHUNK):
            copies.append(
                pltpu.make_async_copy(
                    wide.at[i % DEEP, 2, pl.ds(j * CHUNK, CHUNK)],
                    outs[2].at[e, columns, pl.ds(piece * rows + j * CHUNK, CHUNK)],
                    out_sem.at[i % DEEP, 2 + j],
                )
            )
        return copies

    for i in range(DEEP - 1):
        fetch(i).start()
    for i in range(count):
        if i + DEEP - 1 < count:
            fetch(i + DEEP - 1).start()
        fetch(i).wait()
        if i >= DEEP:
            for copy in drain(i - DEEP):
                copy.wait()
        for k in range(3):

            @pl.loop(0, rows // 64)
            def _(t):
                r = pl.ds(pl.multiple_of(t * 64, 64), 64)
                wide[i % DEEP, k, r, :] = low[i % DEEP, k, r, :].astype(F32)

        for copy in drain(i):
            copy.start()
    for i in range(count - DEEP, count):
        for copy in drain(i):
            copy.wait()


def place_pieces(token, e, gathered, outs, shapes):
    first = outs is None
    rows = gathered.shape[3]
    operands = [gathered, token] + ([] if first else list(outs[:3]))
    return pl.pallas_call(
        functools.partial(place_pieces_kernel, e, first),
        in_specs=[ANYWHERE] * len(operands),
        out_specs=[ANYWHERE] * 3 + [token_spec()],
        scratch_shapes=[
            pltpu.VMEM((DEEP, 3, rows, CHUNK), BF16),
            pltpu.VMEM((DEEP, 3, rows, CHUNK), F32),
            pltpu.SemaphoreType.DMA((DEEP,)),
            pltpu.SemaphoreType.DMA((DEEP, 2 + rows // CHUNK)),
        ],
        out_shape=[jax.ShapeDtypeStruct(s, F32) for s in shapes] + [TOKEN],
        input_output_aliases={} if first else {2: 0, 3: 1, 4: 2},
        compiler_params=pltpu.CompilerParams(vmem_limit_bytes=60 * MIB),
        cost_estimate=pl.CostEstimate(
            flops=0, bytes_accessed=16 * 9 * rows * CHUNK * 2, transcendentals=0
        ),
        name="place_pieces",
    )(*operands)


def hop_kernel(*refs):
    *parts, got, _, out_ref, token_ref = refs
    token_ref[...] = jnp.zeros_like(token_ref)
    total = parts[0][...].astype(F32)
    for part in parts[1:]:
        total = total + part[...].astype(F32)
    out_ref[...] = (total + got[...].astype(F32)).astype(BF16)


def hop_add(token, parts, got):
    rows, width = got.shape
    half = rows // 2

    def at(place):
        return pl.BlockSpec((half, width), lambda i: (2 * place + i, 0))

    return pl.pallas_call(
        hop_kernel,
        grid=(2,),
        in_specs=[at(p) for _, p in parts] + [at(0), ANYWHERE],
        out_specs=[at(0), token_spec()],
        out_shape=[jax.ShapeDtypeStruct((rows, width), BF16), TOKEN],
        compiler_params=pltpu.CompilerParams(vmem_limit_bytes=60 * MIB),
        cost_estimate=pl.CostEstimate(
            flops=rows * width * 5, bytes_accessed=14 * rows * width, transcendentals=0
        ),
        name="hop",
    )(*(a for a, _ in parts), got, token)


def body(
    hidden_in,
    out_grad,
    routes,
    attn_gain,
    w_query,
    w_key,
    w_value,
    q_gain,
    k_gain,
    w_out,
    ffn_gain,
    w_router,
    w_gate,
    w_up,
    w_down,
):
    groups = lax.axis_size("expert")
    context = lax.axis_size("context")
    my_group = lax.axis_index("expert")
    my_context = lax.axis_index("context")
    my_dp = lax.axis_index("dp")
    tokens = hidden_in.shape[1]
    width = hidden_in.shape[2]
    rows = w_query.shape[0]
    local_experts = w_gate.shape[0]
    experts_all = w_router.shape[1]
    length = tokens * context
    per = HEADS // context
    local = per * HDIM
    core, side = my_context % 2, my_context // 2
    bits = jnp.stack([core, my_dp * 2 + side, side * 2 + my_dp]).astype(jnp.int32)
    ring = [(my_group - s) % groups for s in range(groups)]
    members = [my_context ^ s for s in range(context)]

    def half_columns(weight):
        split = weight.reshape(rows, 2, per // 2, context, HDIM)
        split = lax.dynamic_index_in_dim(split, my_dp, 1, keepdims=False)
        return split.transpose(2, 0, 1, 3).reshape(context, rows, local // 2)

    columns = jnp.concatenate([half_columns(w) for w in (w_query, w_key, w_value)], axis=2)
    pieces = [lax.dynamic_index_in_dim(columns, m, 0, keepdims=False) for m in members]
    pieces = [pieces[0]] + [swap(pieces[s], "context", s) for s in range(1, context)]
    half_w = take(jnp.stack(pieces), members).reshape(context * rows, 3 * local // 2)
    small = jnp.concatenate(
        [attn_gain[None], q_gain[None], k_gain[None], ffn_gain[None], w_router.T], axis=0
    )
    small = [small] + [swap(small, "context", s) for s in range(1, context)]
    small = take(jnp.stack(small), members)
    hidden_all = after(hidden_in[0], half_w)
    hidden_all = jnp.concatenate(context_gather(hidden_all), axis=0)
    small = take(jnp.stack(ring_direct(small)), ring)
    small_all = small.transpose(2, 0, 1, 3).reshape(4 + experts_all, width)
    halves, others = [half_w], [swap(half_w, "dp", 1)]
    for s in range(1, groups):
        halves.append(shift(halves[-1], 1))
        others.append(swap(halves[-1], "dp", 1))
    some = local // 2
    qkv_w = jnp.concatenate(
        [
            jnp.concatenate(
                [w[:, i * some : (i + 1) * some] for i in range(3) for w in pair], axis=1
            )
            for pair in zip(halves, others)
        ],
        axis=0,
    )
    heads = [my_dp * 2, my_dp * 2 + 1, (1 - my_dp) * 2, (1 - my_dp) * 2 + 1]
    whole_heads = rows == HDIM
    routes_ring = ring_direct(after(routes[0], halves[-1]))
    if whole_heads:
        out_all = lax.all_gather(after(w_out, halves[-1]), "expert", axis=0)
    upstream_all = lax.all_gather(after(out_grad[0], halves[-1]), "expert", axis=0)

    gain_attn = small_all[0].astype(F32)
    gain_ffn = small_all[3].astype(F32)
    router_w = small_all[4:]
    router_wide = jnp.pad(router_w.T, ((0, 0), (0, 128 - experts_all)))

    def mine(vector):
        table = vector.reshape(per, context, HDIM)
        table = lax.dynamic_index_in_dim(table, my_context, 1, keepdims=False)
        return take(table, heads).astype(F32)

    gain_query, gain_key = mine(small_all[1]), mine(small_all[2])
    block = width // groups

    def to_ring(values):
        parts = [lax.dynamic_slice_in_dim(values, m * block, block, axis=1) for m in ring]
        return jnp.concatenate(parts, axis=1)

    source_all = hidden_all.astype(F32)
    factor_all = rms_factor(source_all)
    normed = to_ring((source_all * factor_all * gain_attn).astype(BF16))
    source = hidden_in[0].astype(F32)
    factor_one = rms_factor(source)
    qkv = dot(normed, qkv_w, (1, 0))

    def slots(query, key):
        return jnp.stack([v.reshape(context, tokens) for v in (query, key)])

    def per_row(values):
        return values.reshape(length)[:, None]

    squares = [jnp.sum(jnp.square(qkv[:, i * local : (i + 1) * local]), axis=-1) for i in range(2)]
    squares = context_total(slots(*squares))
    factors = lax.rsqrt(squares / width + epsilon)
    factor_query, factor_key = per_row(factors[0]), per_row(factors[1])
    starts = jnp.stack([m * tokens for m in members])
    positions = (starts[:, None] + jnp.arange(tokens, dtype=jnp.int32)).reshape(length).astype(F32)
    frequency = rope_base ** (-jnp.arange(HDIM // 2, dtype=F32) * 2.0 / HDIM)
    angles = positions[:, None] * frequency[None, :]
    cosine = jnp.tile(jnp.cos(angles), (1, 2))
    sine_part = jnp.sin(angles)
    sine_part = jnp.concatenate([-sine_part, sine_part], axis=1)
    turn = (factor_query, factor_key, gain_query[:, None], gain_key[:, None], cosine, sine_part)
    query_low, key_low, value_low, mixed_low, logsum = attend(qkv, *turn, [])
    if whole_heads:
        out_w = take(out_all, heads).reshape(local, width)
    else:
        out_w = lax.all_gather(w_out, ("expert", "context"), axis=0, tiled=True)
        out_w = out_w.reshape(per, context, HDIM, width)
        out_w = lax.dynamic_index_in_dim(out_w, my_context, 1, keepdims=False)
        out_w = take(out_w, heads).reshape(local, width)
    ids = jnp.arange(128, dtype=jnp.int32)
    masks = [jnp.any(r[:, :, None] == ids, axis=1).astype(F32) for r in routes_ring]
    mixed_out = dot(mixed_low, out_w, (1, 0)).astype(BF16).reshape(context, tokens, width)
    residual = after(source, *routes_ring[1:]) + context_sum([mixed_out[s] for s in range(context)])
    factor_two = rms_factor(residual)
    normed_two = (residual * factor_two * gain_ffn).astype(BF16)

    at = jnp.reshape(my_group * local_experts, (1,)).astype(jnp.int32)
    order = Order()

    def rows_of(first, count, x, u, mask, *ready):
        return order.run(
            run_rows, at, first, count, x, u, mask, router_wide, w_gate, w_up, w_down, *ready
        )

    near = [[(0, local_experts)], [(0, local_experts)]]
    if local_experts == 4:
        near = [[(0, 2), (2, 2)]] * 2
    blocks = ring_gather(normed_two)
    segments = [([0], []), ([1], [])]

    ups = [out_grad[0]]

    def upstream_of(slot):
        m = ring[slot] + order.token[0, 0].astype(jnp.int32)
        return lax.dynamic_index_in_dim(upstream_all, m, 0, keepdims=False)

    def near_rows(slot, i):
        first, count = near[slot][i]
        ready = [upstream_all] if (slot, i) == (0, 1) else []
        result = rows_of(first, count, blocks[slot], ups[slot], masks[slot], *ready)
        segments[slot][1].append((first, count, result))

    for slot in range(2):
        if slot == 1:
            ups.append(upstream_of(1))
        for i in range(len(near[slot])):
            if (slot, i) != (1, 1):
                near_rows(slot, i)
    far = []
    for slot in range(2, groups, 2):
        pair = [slot, slot + 1]
        x, u, mask = (
            jnp.concatenate(v, axis=0)
            for v in (
                [blocks[s] for s in pair],
                [upstream_of(s) for s in pair],
                [masks[s] for s in pair],
            )
        )
        far.append((x, u, mask))
        segments.append((pair, []))
        ups.append(u)

    def segment_of(segment, e):
        for first, count, result in segments[segment][1]:
            if first <= e < first + count:
                return (result[4], ups[segment], result[5], result[6], e - first)

    whole_sums = min(1, local_experts)
    summed = []

    def sum_grads():
        e = len(summed)
        if e == local_experts:
            return
        call = run_grads
        if e >= whole_sums:
            call = functools.partial(run_split, bits=bits)
        bunches = [[0, 1, 2]] + [[s, s + 1] for s in range(3, len(segments), 2)]
        results = []
        for bunch in bunches:
            bunch = [segment_of(s, e) for s in bunch if s < len(segments)]
            results.append(order.run(call, bunch))
        grads = [
            total_low(list(terms)) if len(terms) > 1 else terms[0] for terms in zip(*results)
        ]
        if e < whole_sums:
            summed.append(lax.psum(grads, ("context", "dp")))
        else:
            summed.append(Summed(order, grads[:4], grads[4]))

    def advance(*events):
        for e, name in events:
            if whole_sums <= e < local_experts:
                summed[e].reach(name)

    def parts_of(slot, index):
        for pair, calls in segments:
            if slot in pair:
                return [(result[index], pair.index(slot)) for _, _, result in calls]

    def hop(index, total, slot):
        return order.run(hop_add, parts_of(slot % groups, index), shift(total, 1))[0]

    def first_hop(index):
        return total_low([r[p * tokens : (p + 1) * tokens] for r, p in parts_of(1, index)])

    for e in range(local_experts):
        for i, (x, u, mask) in enumerate(far):
            segments[2 + i][1].append((e, 1, rows_of(e, 1, x, u, mask)))
        if e < 2:
            sum_grads()
        if e == 0 and len(near[1]) > 1:
            near_rows(1, 1)
        if e == 2:
            advance((1, "halves"))
    row_total = hop(1, first_hop(1), 2)
    sum_grads()
    advance((1, "quarters"))

    gate_grad = [
        functools.reduce(
            lambda a, b: a + b,
            [result[2][pair.index(s) * tokens : (pair.index(s) + 1) * tokens] for _, _, result in calls],
        )
        for pair, calls in segments
        for s in pair
    ]
    gate_grad = [g[:, :local_experts].T for g in gate_grad]
    gate_grad = jnp.stack([gate_grad[0]] + [shift(gate_grad[s], -s) for s in range(1, groups)])
    gate_grad = take(gate_grad, [(g - my_group) % groups for g in range(groups)])
    gate_grad = gate_grad.reshape(experts_all, tokens).T

    for slot in range(3, groups + 1):
        row_total = hop(1, row_total, slot)
        if slot == 3:
            sum_grads()
            advance((1, "finals"), (2, "halves"))
    row_back = row_total.astype(F32)
    shapes = (w_gate.shape, w_up.shape, w_down.shape)
    expert_grads = None

    def place(experts):
        outs = expert_grads
        for e in experts:
            if e < local_experts:
                if e >= whole_sums:
                    summed[e].reach("finals")
                    outs = order.run(place_pieces, e, summed[e].all, outs, shapes)
                else:
                    outs = order.run(place_grads, e, summed[e], outs, shapes)
        return outs


    upstream = out_grad[0].astype(F32)
    weights_own = segments[0][1][0][2][3][:, :experts_all]
    weighted = jnp.sum(weights_own * gate_grad, axis=-1, keepdims=True)
    logit_grad = (weights_own * (gate_grad - weighted)).astype(BF16)
    router_grad = dot(logit_grad, normed_two, (0, 0))
    normed_two_grad = dot(logit_grad, router_w, (1, 0)) + row_back
    residual_part, ffn_gain_grad = norm_back(normed_two_grad, residual, factor_two, gain_ffn)
    residual_grad = upstream + residual_part

    attn_grad = context_gather(residual_grad.astype(BF16))
    out_total = hop(0, first_hop(0), 2)
    attn_grad = jnp.concatenate(attn_grad, axis=0)
    mixed_grad = dot(attn_grad, out_w, (1, 1)).astype(BF16)
    query_back, key_back, value_grad, query_sum, key_sum, q_gain_grad, k_gain_grad = order.run(
        attend_back, query_low, key_low, value_low, mixed_grad, logsum, qkv, *turn
    )
    out_w_grad = dot(mixed_low, after(attn_grad, order.token), (0, 0)).astype(BF16)
    advance((2, "quarters"))

    class Ring:
        def __init__(self, terms):
            self.terms, self.size, self.slot = terms, terms.shape[0] // groups, 1
            at = 1 % groups * self.size
            self.total = terms[at : at + self.size]
            self.coming = shift(self.total, 1)

        def hop(self):
            if self.slot < groups:
                self.slot += 1
                self.total = order.run(hop_add, [(self.terms, self.slot % groups)], self.coming)[0]
                self.coming = shift(self.total, 1)

        def whole(self):
            while self.slot < groups:
                self.hop()
            return self.total

    if whole_heads:
        ordered = take(
            out_w_grad.reshape(per, HDIM, width), [(m // 2 ^ my_dp) * 2 + m % 2 for m in ring]
        )
        out_ring = Ring(ordered.reshape(local, width))
    for slot in range(3, groups):
        out_total = hop(0, out_total, slot)
    sums = context_total(slots(jnp.sum(query_sum, axis=1), jnp.sum(key_sum, axis=1))) / width
    order.token = after(order.token, sums)
    advance((3, "halves"))
    if groups > 2:
        out_total = hop(0, out_total, groups)
    hidden_out = (residual + out_total.astype(F32)).astype(BF16)[None]
    if whole_heads:
        out_ring.hop()
    def low_grad(back, raw, factor, gain, total):
        return (
            factor * back * gain.reshape(1, local) - raw * factor**3 * per_row(total)
        ).astype(BF16)

    query_grad = low_grad(query_back, qkv[:, :local], factor_query, gain_query, sums[0])
    key_grad = low_grad(key_back, qkv[:, local : 2 * local], factor_key, gain_key, sums[1])
    qkv_grad = jnp.concatenate([query_grad, key_grad, value_grad], axis=1)
    qkv_w_grad = dot(normed, qkv_grad, (0, 0)).astype(BF16)
    normed_grad = dot(qkv_grad, qkv_w, (1, 1)).astype(BF16)
    order.token = after(order.token, qkv_w_grad, normed_grad)
    normed_grad = normed_grad.reshape(context, tokens, width)
    normed_own, normed_near, normed_far = context_terms([normed_grad[s] for s in range(context)])

    qkv_ring = Ring(qkv_w_grad)
    advance((2, "finals"))
    if whole_heads:
        out_ring.hop()
    advance((3, "quarters"))
    qkv_ring.hop()
    expert_grads = place([0])
    if whole_heads:
        mine_out = out_ring.whole()
        out_w_grad = mine_out.astype(F32) + swap(mine_out, "dp", 1).astype(F32)
    qkv_ring.hop()
    advance((3, "finals"))
    expert_grads = place([1])
    qkv_w_grad = qkv_ring.whole()
    normed_own = after(normed_own, order.token)
    normed_grad = normed_own.astype(F32) + normed_near.astype(F32) + normed_far.astype(F32)
    parts = [
        lax.dynamic_slice_in_dim(normed_grad, (my_group - m) % groups * block, block, axis=1)
        for m in range(groups)
    ]
    normed_grad = jnp.concatenate(parts, axis=1)
    source_part, attn_gain_grad = norm_back(normed_grad, source, factor_one, gain_attn)
    input_grad = (residual_grad + source_part).astype(BF16)[None]

    mine_w = qkv_w_grad.reshape(context, rows, 3, 2, some)
    got = swap(mine_w, "dp", 1)
    expert_grads = place([2])
    mine_w = after(mine_w, order.token)
    mine_w = jnp.stack(
        [add_low(mine_w[:, :, :, i], got[:, :, :, 1 - i]) for i in range(2)], axis=3
    )
    pieces = [lax.dynamic_index_in_dim(mine_w, m, 0, keepdims=False) for m in members]
    pieces = [pieces[0]] + [swap(pieces[s], "context", s) for s in range(1, context)]
    expert_grads = place([3])
    pieces[0] = after(pieces[0], order.token)
    dense = take(jnp.stack(pieces), members)
    dense = jnp.where(my_dp == 0, dense, dense[:, :, :, ::-1]).astype(F32)
    dense = dense.reshape(context, rows, 3, per, HDIM).transpose(2, 1, 3, 0, 4)
    dense = dense.reshape(3, rows, width)
    if not whole_heads:
        spread = jnp.zeros((per, context, HDIM, width), BF16)
        for h in range(per):
            term = out_w_grad.reshape(per, HDIM, width)[h][None, None]
            spread = lax.dynamic_update_slice(spread, term, (heads[h], my_context, 0, 0))
        spread = lax.psum_scatter(
            spread.reshape(width, width), ("expert", "context"), scatter_dimension=0, tiled=True
        )
        out_w_grad = lax.psum(spread, "dp").astype(F32)
    gains = jnp.zeros((2, per, context, HDIM), F32)
    for h in range(per):
        pair = jnp.stack([q_gain_grad[h], k_gain_grad[h]])[:, None]
        gains = lax.dynamic_update_slice(gains, pair, (0, heads[h], my_context, 0))
    small_grad = jnp.concatenate(
        [attn_gain_grad[None], ffn_gain_grad[None], gains.reshape(2, width), router_grad], axis=0
    )
    small_grad = small_grad.reshape(4 + experts_all, groups, context, rows).transpose(1, 2, 0, 3)
    small_grad = after(take(small_grad, ring), qkv_w_grad)
    small_grad = functools.reduce(
        lambda a, b: a + b,
        [small_grad[0]] + [shift(small_grad[s], -s) for s in range(1, groups)],
    )
    small_grad = take(small_grad, members)
    got = swap(jnp.stack([small_grad[1], small_grad[3]]), "context", 1)
    small_grad = small_grad[0] + got[0] + swap(small_grad[2] + got[1], "context", 2)
    small_grad = small_grad + swap(small_grad, "dp", 1)
    return (
        hidden_out,
        input_grad,
        small_grad[0],
        dense[0],
        dense[1],
        dense[2],
        small_grad[2],
        small_grad[3],
        out_w_grad,
        small_grad[1],
        small_grad[4:].T,
        expert_grads[0],
        expert_grads[1],
        expert_grads[2],
    )


def solution(mesh):
    tokens = P(("expert", "dp"), "context", None)
    vector = P(("expert", "context"))
    matrix = P(("expert", "context"), None)
    expert = P("expert", None, None)
    in_specs = (
        tokens,
        tokens,
        tokens,
        vector,
        matrix,
        matrix,
        matrix,
        vector,
        vector,
        matrix,
        vector,
        matrix,
        expert,
        expert,
        expert,
    )
    out_specs = (
        tokens,
        tokens,
        vector,
        matrix,
        matrix,
        matrix,
        vector,
        vector,
        matrix,
        vector,
        matrix,
        expert,
        expert,
        expert,
    )
    return jax.shard_map(body, mesh=mesh, in_specs=in_specs, out_specs=out_specs, check_vma=False)
```

```python
import functools
import math

import jax
import jax.numpy as jnp
from jax import lax
from jax.experimental import pallas as pl
from jax.experimental.pallas import tpu as pltpu
from jax.sharding import PartitionSpec as P

HEADS = 16
HDIM = 128
CHUNK = 256
ROWS = 1024

epsilon = 1e-06
rope_base = 10000.0
F32 = jnp.float32
BF16 = jnp.bfloat16
MIB = 1024 * 1024


def dot(left, right, contract):
    return lax.dot_general(
        left, right, (((contract[0],), (contract[1],)), ((), ())), preferred_element_type=F32
    )


def add_low(left, right):
    return (left.astype(F32) + right.astype(F32)).astype(BF16)


def total_low(terms):
    return functools.reduce(lambda a, b: a + b, [t.astype(F32) for t in terms]).astype(BF16)


FIRST = (("dp", 1), ("context", 2))
SECOND = (("context", 2), ("dp", 1))
PIECES = 4


def nothing_of(values, dtype):
    return (values[(0,) * values.ndim].astype(F32) * 0.0).astype(dtype)


def after(values, *others):
    for other in others:
        values = values + nothing_of(other, values.dtype)
    return values


ANYWHERE = pl.BlockSpec(memory_space=pl.ANY)
TOKEN = jax.ShapeDtypeStruct((8, 128), F32)


def token_spec():
    return pl.BlockSpec((8, 128), lambda *_: (0, 0))


class Order:
    def __init__(self):
        self.token = jnp.zeros((8, 128), F32)

    def run(self, call, *args):
        *results, self.token = call(self.token, *args)
        return results


def rms_factor(values):
    return lax.rsqrt(jnp.mean(values * values, axis=-1, keepdims=True) + epsilon)


def norm_back(grad_out, values, factor, gain_vector):
    scaled = grad_out * gain_vector
    grad_in = factor * scaled - values * factor**3 * jnp.mean(
        scaled * values, axis=-1, keepdims=True
    )
    gain_grad = jnp.sum(grad_out * values * factor, axis=0)
    return (grad_in, gain_grad)


def half_turn(values):
    return pltpu.roll(values, HDIM // 2, 1)


def attend_kernel(
    q_ref, k_ref, v_ref, fq_ref, fk_ref, gq_ref, gk_ref, cos_ref, sin_ref, *refs
):
    ql_ref, kl_ref, vl_ref, mixed_ref, logsum_ref = refs[-5:]
    length = q_ref.shape[0]
    block = min(256, length)
    cosine, sine = cos_ref[...], sin_ref[...]
    query = q_ref[...] * fq_ref[...] * gq_ref[0]
    key = k_ref[...] * fk_ref[...] * gk_ref[0]
    ql_ref[...] = (query * cosine + half_turn(query) * sine).astype(BF16)
    kl_ref[...] = (key * cosine + half_turn(key) * sine).astype(BF16)
    value = v_ref[...].astype(BF16)
    vl_ref[...] = value
    turned = value.T
    for b in range(length // block):
        r = slice(b * block, (b + 1) * block)
        scores = dot(kl_ref[...], ql_ref[r, :], (1, 1)) * HDIM ** (-0.5)
        top = jnp.max(scores, axis=0, keepdims=True)
        raised = jnp.exp(scores - top)
        total = jnp.sum(raised, axis=0, keepdims=True)
        mixed = dot(turned, raised.astype(BF16), (1, 0)) / total
        mixed_ref[r, :] = mixed.T.astype(BF16)
        logsum_ref[0, :, r] = top + jnp.log(total)


def attend_back_kernel(
    ql_ref, kl_ref, vl_ref, grad_ref, logsum_ref, q_ref, k_ref, fq_ref, fk_ref, gq_ref, gk_ref,
    cos_ref, sin_ref, _, qb_ref, kb_ref, vg_ref, qs_ref, ks_ref, qg_ref, kg_ref, token_ref,
    k_acc, v_acc, q_acc,
):
    token_ref[...] = jnp.zeros_like(token_ref)
    length = ql_ref.shape[0]
    block = min(256, length)
    scale = HDIM ** (-0.5)

    @pl.when(pl.program_id(0) == 0)
    def _():
        qs_ref[...] = jnp.zeros_like(qs_ref)
        ks_ref[...] = jnp.zeros_like(ks_ref)

    for b in range(length // block):
        r = slice(b * block, (b + 1) * block)
        query, grad = ql_ref[r, :], grad_ref[r, :]
        scores = dot(kl_ref[...], query, (1, 1)) * scale
        probs = jnp.exp(scores - logsum_ref[0, :, r])
        prob_grad = dot(vl_ref[...], grad, (1, 1))
        moved = jnp.sum(probs * prob_grad, axis=0, keepdims=True)
        score_grad = (probs * (prob_grad - moved)).astype(BF16)
        value_part = dot(probs.astype(BF16), grad, (1, 0))
        key_part = dot(score_grad, query, (1, 0))
        if b == 0:
            v_acc[...] = value_part
            k_acc[...] = key_part
        else:
            v_acc[...] += value_part
            k_acc[...] += key_part
        q_acc[r, :] = dot(score_grad, kl_ref[...], (0, 0))
    vg_ref[...] = v_acc[...].astype(BF16)
    cosine, sine = cos_ref[...], sin_ref[...]
    for acc, back_ref, raw_ref, f_ref, g_ref, sum_ref, gain_ref in (
        (q_acc, qb_ref, q_ref, fq_ref, gq_ref, qs_ref, qg_ref),
        (k_acc, kb_ref, k_ref, fk_ref, gk_ref, ks_ref, kg_ref),
    ):
        turned = acc[...] * scale
        back = turned * cosine - half_turn(turned) * sine
        product = back * raw_ref[...]
        back_ref[...] = back
        sum_ref[...] += product * g_ref[0]
        gain_ref[0] = jnp.sum(product * f_ref[...], axis=0, keepdims=True)


def head_specs(length):
    return {
        "head": pl.BlockSpec((length, HDIM), lambda h: (0, h)),
        "whole": pl.BlockSpec((length, HDIM), lambda h: (0, 0)),
        "column": pl.BlockSpec((length, 1), lambda h: (0, 0)),
        "gain": pl.BlockSpec((1, 1, HDIM), lambda h: (h, 0, 0)),
        "row": pl.BlockSpec((1, 1, length), lambda h: (h, 0, 0)),
    }


def attend(qkv, fq, fk, gq, gk, cosine, sine, before):
    length, heads = qkv.shape[0], gq.shape[0]
    spec = head_specs(length)

    def part(i):
        return pl.BlockSpec((length, HDIM), lambda h: (0, i * heads + h))

    low = jax.ShapeDtypeStruct((length, heads * HDIM), BF16)
    return pl.pallas_call(
        attend_kernel,
        grid=(heads,),
        in_specs=[part(0), part(1), part(2)]
        + [spec[n] for n in ("column", "column", "gain", "gain", "whole", "whole")]
        + [ANYWHERE] * len(before),
        out_specs=[spec["head"]] * 4 + [spec["row"]],
        out_shape=[low] * 4 + [jax.ShapeDtypeStruct((heads, 1, length), F32)],
        compiler_params=pltpu.CompilerParams(vmem_limit_bytes=60 * MIB),
        cost_estimate=pl.CostEstimate(
            flops=10 * heads * length * length * HDIM,
            bytes_accessed=20 * length * heads * HDIM,
            transcendentals=heads * length * length,
        ),
        name="attend",
    )(qkv, qkv, qkv, fq, fk, gq, gk, cosine, sine, *before)


def attend_back(token, ql, kl, vl, grad, logsum, qkv, fq, fk, gq, gk, cosine, sine):
    length, heads = qkv.shape[0], gq.shape[0]
    spec = head_specs(length)

    def part(i):
        return pl.BlockSpec((length, HDIM), lambda h: (0, i * heads + h))

    def shape(kind, *dims):
        return jax.ShapeDtypeStruct(dims, kind)

    return pl.pallas_call(
        attend_back_kernel,
        grid=(heads,),
        in_specs=[spec["head"]] * 4
        + [spec["row"], part(0), part(1)]
        + [spec[n] for n in ("column", "column", "gain", "gain", "whole", "whole")]
        + [ANYWHERE],
        out_specs=[spec["head"]] * 3 + [spec["whole"]] * 2 + [spec["gain"]] * 2 + [token_spec()],
        out_shape=[
            shape(F32, length, heads * HDIM),
            shape(F32, length, heads * HDIM),
            shape(BF16, length, heads * HDIM),
            shape(F32, length, HDIM),
            shape(F32, length, HDIM),
            shape(F32, heads, 1, HDIM),
            shape(F32, heads, 1, HDIM),
            TOKEN,
        ],
        scratch_shapes=[pltpu.VMEM((length, HDIM), F32)] * 3,
        compiler_params=pltpu.CompilerParams(vmem_limit_bytes=60 * MIB),
        cost_estimate=pl.CostEstimate(
            flops=20 * heads * length * length * HDIM,
            bytes_accessed=30 * length * heads * HDIM,
            transcendentals=heads * length * length,
        ),
        name="attend_back",
    )(ql, kl, vl, grad, logsum, qkv, qkv, fq, fk, gq, gk, cosine, sine, token)


def swap(values, axis, bit):
    return lax.ppermute(values, axis, [(i, i ^ bit) for i in range(lax.axis_size(axis))])


def shift(values, by):
    n = lax.axis_size("expert")
    return lax.ppermute(values, "expert", [(i, (i + by) % n) for i in range(n)])


def context_gather(own):
    far = swap(own, "context", 2)
    near = swap(own, "context", 1)
    return [own, near, far, swap(far, "context", 1)]


def context_terms(blocks):
    got = swap(jnp.stack([blocks[1], blocks[3]]), "context", 1)
    return blocks[0], got[0], swap(add_low(blocks[2], got[1]), "context", 2)


def context_sum(blocks):
    own, near, far = context_terms(blocks)
    return own.astype(F32) + near.astype(F32) + far.astype(F32)


def context_total(terms):
    got = swap(terms, "context", 1)
    terms = terms + jnp.stack([got[:, s ^ 1] for s in range(4)], axis=1)
    got = swap(terms, "context", 2)
    return terms + jnp.stack([got[:, s ^ 2] for s in range(4)], axis=1)


def ring_gather(own):
    held = [own]
    for _ in range(lax.axis_size("expert") - 1):
        held.append(shift(held[-1], 1))
    return held


def ring_direct(own):
    return [own] + [shift(own, s) for s in range(1, lax.axis_size("expert"))]


def take(blocks, index):
    return jnp.stack([lax.dynamic_index_in_dim(blocks, i, 0, keepdims=False) for i in index])


def rows_kernel(
    first,
    at_ref,
    x_ref,
    u_ref,
    mask_ref,
    router_ref,
    wg_ref,
    wu_ref,
    wd_ref,
    *refs,
):
    (
        out_ref,
        row_ref,
        gate_ref,
        weights_ref,
        turned_ref,
        both_ref,
        hidden_ref,
        token_ref,
        out_acc,
        row_acc,
        lanes,
        both_w,
    ) = refs[-12:]
    e, step = pl.program_id(0), pl.program_id(1)
    start = jnp.logical_and(e == 0, step == 0)
    rows, width = x_ref.shape
    chunk = wg_ref.shape[1]
    lane = lax.broadcasted_iota(jnp.int32, (rows, 128), 1)
    token_ref[...] = jnp.zeros_like(token_ref)

    @pl.when(start)
    def _():
        out_acc[...] = jnp.zeros_like(out_acc)
        row_acc[...] = jnp.zeros_like(row_acc)
        gate_ref[...] = jnp.zeros_like(gate_ref)
        turned_ref[...] = x_ref[...].T
        logits = dot(x_ref[...], router_ref[...], (1, 0))
        chosen = mask_ref[...] > 0.5
        top = jnp.max(jnp.where(chosen, logits, -1e30), axis=-1, keepdims=True)
        raised = jnp.where(chosen, jnp.exp(jnp.where(chosen, logits - top, 0.0)), 0.0)
        weights_ref[...] = raised / jnp.sum(raised, axis=-1, keepdims=True)

    @pl.when(step == 0)
    def _():
        lanes[...] = jnp.zeros_like(lanes)

    both_w[:, :chunk] = wg_ref[...]
    both_w[:, chunk:] = wu_ref[...]
    weight = jnp.sum(
        jnp.where(lane == at_ref[0] + first + e, weights_ref[...], 0.0), axis=-1, keepdims=True
    )
    pre = dot(x_ref[...], both_w[...], (1, 0))
    gate_pre, up_pre = pre[:, :chunk], pre[:, chunk:]
    hidden_grad = dot(u_ref[...], wd_ref[...], (1, 1))
    sigmoid = 1.0 / (1.0 + jnp.exp(-gate_pre))
    activated = gate_pre * sigmoid
    hidden = activated * up_pre
    part = hidden * hidden_grad
    total = part[:, :128]
    for j in range(1, chunk // 128):
        total = total + part[:, j * 128 : (j + 1) * 128]
    lanes[...] += total
    hidden_low = (weight * hidden).astype(BF16)
    hidden_grad = weight * hidden_grad
    gate_low = (hidden_grad * up_pre * (sigmoid + activated * (1.0 - sigmoid))).astype(BF16)
    up_low = (hidden_grad * activated).astype(BF16)
    hidden_ref[...] = hidden_low
    both_ref[:, :chunk] = gate_low
    both_ref[:, chunk:] = up_low
    out_acc[...] += dot(hidden_low, wd_ref[...], (1, 0))
    row_acc[...] += dot(both_ref[...], both_w[...], (1, 1))

    @pl.when(step == pl.num_programs(1) - 1)
    def _():
        sums = jnp.sum(lanes[...], axis=-1, keepdims=True)
        gate_ref[...] += jnp.where(lane == first + e, sums, 0.0)
        out_ref[...] = out_acc[...].astype(BF16)
        row_ref[...] = row_acc[...].astype(BF16)


def run_rows(token, at, first, count, x, u, mask, router, w_gate, w_up, w_down, *ready):
    rows, width = x.shape
    ff = w_gate.shape[2]
    steps = ff // CHUNK

    def whole(shape):
        return pl.BlockSpec(
            shape, lambda e, s, a: (0,) * len(shape), pipeline_mode=pl.Buffered(1)
        )

    return pl.pallas_call(
        functools.partial(rows_kernel, first),
        grid_spec=pltpu.PrefetchScalarGridSpec(
            num_scalar_prefetch=1,
            grid=(count, steps),
            in_specs=[
                whole((rows, width)),
                whole((rows, width)),
                whole((rows, 128)),
                whole((width, 128)),
                pl.BlockSpec((None, width, CHUNK), lambda e, s, a: (first + e, 0, s)),
                pl.BlockSpec((None, width, CHUNK), lambda e, s, a: (first + e, 0, s)),
                pl.BlockSpec((None, CHUNK, width), lambda e, s, a: (first + e, s, 0)),
            ]
            + [ANYWHERE] * (1 + len(ready)),
            out_specs=[
                whole((rows, width)),
                whole((rows, width)),
                whole((rows, 128)),
                whole((rows, 128)),
                whole((width, rows)),
                pl.BlockSpec((None, None, rows, 2 * CHUNK), lambda e, s, a: (e, s, 0, 0)),
                pl.BlockSpec((None, None, rows, CHUNK), lambda e, s, a: (e, s, 0, 0)),
                token_spec(),
            ],
            scratch_shapes=[
                pltpu.VMEM((rows, width), F32),
                pltpu.VMEM((rows, width), F32),
                pltpu.VMEM((rows, 128), F32),
                pltpu.VMEM((width, 2 * CHUNK), BF16),
            ],
        ),
        out_shape=[
            jax.ShapeDtypeStruct((rows, width), BF16),
            jax.ShapeDtypeStruct((rows, width), BF16),
            jax.ShapeDtypeStruct((rows, 128), F32),
            jax.ShapeDtypeStruct((rows, 128), F32),
            jax.ShapeDtypeStruct((width, rows), BF16),
            jax.ShapeDtypeStruct((count, steps, rows, 2 * CHUNK), BF16),
            jax.ShapeDtypeStruct((count, steps, rows, CHUNK), BF16),
            TOKEN,
        ],
        compiler_params=pltpu.CompilerParams(vmem_limit_bytes=56 * MIB),
        cost_estimate=pl.CostEstimate(
            flops=12 * rows * width * ff * count,
            bytes_accessed=6 * width * ff * count,
            transcendentals=rows * ff * count,
        ),
        name="rows",
    )(at, x, u, mask, router, w_gate, w_up, w_down, token, *ready)


def grads_kernel(sizes, *refs):
    n = len(sizes)
    turned, ups, boths, hiddens = (refs[i * n : (i + 1) * n] for i in range(4))
    gate_ref, up_ref, down_ref, token_ref, x_all, u_all, both, hidden = refs[-8:]
    token_ref[...] = jnp.zeros_like(token_ref)
    width, chunk = x_all.shape[0], hidden.shape[1]

    spans, at = [], 0
    for size in sizes:
        spans.append(slice(at, at + size))
        at += size

    @pl.when(pl.program_id(0) == 0)
    def _():
        for span, t, u in zip(spans, turned, ups):
            x_all[:, span] = t[...]
            u_all[span, :] = u[...]

    for span, b, h in zip(spans, boths, hiddens):
        both[span, :] = b[...]
        hidden[span, :] = h[...]
    hidden_turned = hidden[...].T
    piece = width // 4
    for p in range(4):
        r = slice(p * piece, (p + 1) * piece)
        got = dot(x_all[r, :], both[...], (1, 0)).astype(BF16)
        gate_ref[r, :] = got[:, :chunk]
        up_ref[r, :] = got[:, chunk:]
        down_ref[:, r] = dot(hidden_turned, u_all[:, r], (1, 0)).astype(BF16)


def run_grads(token, segments):
    turned, ups, boths, hiddens, places = zip(*segments)
    width = turned[0].shape[0]
    sizes = tuple(u.shape[0] for u in ups)
    total = sum(sizes)
    steps = boths[0].shape[1]

    def whole(shape):
        return pl.BlockSpec(shape, lambda s: (0, 0), pipeline_mode=pl.Buffered(1))

    def chunked(size, columns, place):
        return pl.BlockSpec((None, None, size, columns), lambda s: (place, s, 0, 0))

    return pl.pallas_call(
        functools.partial(grads_kernel, sizes),
        grid=(steps,),
        in_specs=[whole((width, size)) for size in sizes]
        + [whole((size, width)) for size in sizes]
        + [chunked(size, 2 * CHUNK, p) for size, p in zip(sizes, places)]
        + [chunked(size, CHUNK, p) for size, p in zip(sizes, places)]
        + [ANYWHERE],
        out_specs=[
            pl.BlockSpec((width, CHUNK), lambda s: (0, s)),
            pl.BlockSpec((width, CHUNK), lambda s: (0, s)),
            pl.BlockSpec((CHUNK, width), lambda s: (s, 0)),
            token_spec(),
        ],
        out_shape=[
            jax.ShapeDtypeStruct((width, steps * CHUNK), BF16),
            jax.ShapeDtypeStruct((width, steps * CHUNK), BF16),
            jax.ShapeDtypeStruct((steps * CHUNK, width), BF16),
            TOKEN,
        ],
        scratch_shapes=[
            pltpu.VMEM((width, total), BF16),
            pltpu.VMEM((total, width), BF16),
            pltpu.VMEM((total, 2 * CHUNK), BF16),
            pltpu.VMEM((total, CHUNK), BF16),
        ],
        compiler_params=pltpu.CompilerParams(vmem_limit_bytes=56 * MIB),
        cost_estimate=pl.CostEstimate(
            flops=6 * total * width * steps * CHUNK,
            bytes_accessed=6 * width * steps * CHUNK + 8 * total * width,
            transcendentals=0,
        ),
        name="grads",
    )(*turned, *ups, *boths, *hiddens, token)


def place_kernel(*refs):
    outs, token_ref = refs[-4:-1], refs[-1]
    token_ref[...] = jnp.zeros_like(token_ref)
    for low, out in zip(refs[:3], outs):
        out[...] = low[...].astype(F32)


def place_grads(token, e, summed, outs, shapes):
    steps = 8

    def cut(shape):
        return pl.BlockSpec((shape[0] // steps, shape[1]), lambda i: (i, 0))

    def cut_out(shape):
        return pl.BlockSpec((None, shape[1] // steps, shape[2]), lambda i: (e, i, 0))

    held = [] if outs is None else list(outs[:3])
    return pl.pallas_call(
        place_kernel,
        grid=(steps,),
        in_specs=[cut(v.shape) for v in summed] + [ANYWHERE] * (1 + len(held)),
        out_specs=[cut_out(s) for s in shapes] + [token_spec()],
        out_shape=[jax.ShapeDtypeStruct(s, F32) for s in shapes] + [TOKEN],
        input_output_aliases={4 + i: i for i in range(len(held))},
        compiler_params=pltpu.CompilerParams(vmem_limit_bytes=60 * MIB),
        cost_estimate=pl.CostEstimate(
            flops=0,
            bytes_accessed=6 * sum(math.prod(v.shape) for v in summed),
            transcendentals=0,
        ),
        name="place",
    )(*summed, token, *held)


def split_kernel(sizes, bits_ref, *refs):
    n = len(sizes)
    turned, ups, boths, hiddens = (refs[i * n : (i + 1) * n] for i in range(4))
    *sends, keep_ref, token_ref, x_all, u_all, both, hidden = refs[-10:]
    token_ref[...] = jnp.zeros_like(token_ref)
    step = pl.program_id(0)
    width = x_all.shape[0]
    chunk = hidden.shape[1]

    spans, at = [], 0
    for size in sizes:
        spans.append(slice(at, at + size))
        at += size

    @pl.when(step == 0)
    def _():
        for span, t, u in zip(spans, turned, ups):
            x_all[:, span] = t[...]
            u_all[span, :] = u[...]

    for span, b, h in zip(spans, boths, hiddens):
        both[span, :] = b[...]
        hidden[span, :] = h[...]
    hidden_turned = hidden[...].T
    piece_rows = width // PIECES

    def store(mask, place_of):
        for place in range(PIECES):
            ref = place_of(place)
            p = place ^ mask
            r = pl.ds(pl.multiple_of(p * piece_rows, piece_rows), piece_rows)
            got = dot(x_all[r, :], both[...], (1, 0)).astype(BF16)
            ref[0] = got[:, :chunk]
            ref[1] = got[:, chunk:]
            down = dot(hidden_turned, u_all[:, r], (1, 0)).astype(BF16)
            for j in range(piece_rows // chunk):
                ref[2, j * chunk : (j + 1) * chunk, :] = down[:, j * chunk : (j + 1) * chunk]

    def sent(path):
        store(bits_ref[1 + path], lambda place: sends[path * 2 + place // 2].at[place % 2])

    pl.when(step == 0)(functools.partial(sent, 0))
    pl.when(step == 1)(functools.partial(sent, 1))

    @pl.when(step >= 2)
    def _():
        mask = jnp.where(step % 2 == 0, bits_ref[1], bits_ref[2])
        store(mask, lambda place: keep_ref.at[0, place])


def run_split(token, segments, bits, ready=()):
    turned, ups, boths, hiddens, places = zip(*segments)
    width = turned[0].shape[0]
    sizes = tuple(u.shape[0] for u in ups)
    total = sum(sizes)
    steps = boths[0].shape[1]
    half = steps // 2
    piece_rows = width // PIECES

    def chunk_at(s, b):
        return ((1 - s // half) ^ b[0]) * half + s % half

    def whole(shape):
        return pl.BlockSpec(shape, lambda s, b: (0, 0), pipeline_mode=pl.Buffered(1))

    def chunked(size, columns, place):
        return pl.BlockSpec(
            (None, None, size, columns), lambda s, b: (place, chunk_at(s, b), 0, 0)
        )

    grads = (1, PIECES, 3, piece_rows, CHUNK)
    away = (PIECES // 2,) + grads[2:]
    grads_out = jax.ShapeDtypeStruct((half,) + grads[1:], BF16)
    return pl.pallas_call(
        functools.partial(split_kernel, sizes),
        grid_spec=pltpu.PrefetchScalarGridSpec(
            num_scalar_prefetch=1,
            grid=(steps,),
            in_specs=[whole((width, size)) for size in sizes]
            + [whole((size, width)) for size in sizes]
            + [chunked(size, 2 * CHUNK, p) for size, p in zip(sizes, places)]
            + [chunked(size, CHUNK, p) for size, p in zip(sizes, places)]
            + [ANYWHERE] * (1 + len(ready)),
            out_specs=[
                pl.BlockSpec(away, lambda s, b: (0, 0, 0, 0), pipeline_mode=pl.Buffered(1))
                for _ in range(4)
            ]
            + [
                pl.BlockSpec(grads, lambda s, b: (jnp.maximum(s - half, 0), 0, 0, 0, 0)),
                token_spec(),
            ],
            scratch_shapes=[
                pltpu.VMEM((width, total), BF16),
                pltpu.VMEM((total, width), BF16),
                pltpu.VMEM((total, 2 * CHUNK), BF16),
                pltpu.VMEM((total, CHUNK), BF16),
            ],
        ),
        out_shape=[jax.ShapeDtypeStruct(away, BF16)] * 4 + [grads_out, TOKEN],
        compiler_params=pltpu.CompilerParams(vmem_limit_bytes=56 * MIB),
        cost_estimate=pl.CostEstimate(
            flops=6 * total * width * steps * CHUNK,
            bytes_accessed=6 * width * steps * CHUNK + 8 * total * width,
            transcendentals=0,
        ),
        name="split",
    )(bits, *turned, *ups, *boths, *hiddens, token, *ready)


def add_kernel(picks, joined, *refs):
    *refs, token_ref = refs
    token_ref[...] = jnp.zeros_like(token_ref)
    outs = [refs[-1].at[i] for i in range(len(picks))] if joined else refs[-len(picks) :]

    def at(ref, index):
        return ref[index] if index is not None else ref[...]

    for out, terms in zip(outs, picks):
        left, right = (at(refs[i], index) for i, index in terms)
        out[...] = (left.astype(F32) + right.astype(F32)).astype(BF16)


def add_pieces(token, picks, shapes, ins, ready=(), joined=False):

    parts = 4

    def cut(shape):
        block = shape[:-2] + (shape[-2] // parts, shape[-1])
        return pl.BlockSpec(block, lambda i: (0,) * (len(shape) - 2) + (i, 0))

    moved = sum(i.size for i in ins) + sum(math.prod(s) for s in shapes)
    return pl.pallas_call(
        functools.partial(add_kernel, picks, joined),
        grid=(parts,),
        in_specs=[cut(i.shape) for i in ins] + [ANYWHERE] * (1 + len(ready)),
        out_specs=[cut(s) for s in shapes] + [token_spec()],
        out_shape=[jax.ShapeDtypeStruct(s, BF16) for s in shapes] + [TOKEN],
        compiler_params=pltpu.CompilerParams(vmem_limit_bytes=60 * MIB),
        cost_estimate=pl.CostEstimate(flops=moved, bytes_accessed=2 * moved, transcendentals=0),
        name="add_pieces",
    )(*ins, token, *ready)


class Summed:
    def __init__(self, order, sends, keep):
        self.order, self.keep = order, keep
        self.ahead = ["halves", "quarters", "finals"]
        self.got = [swap(sends[i], "context", 1) for i in (1, 3, 0, 2)]

    def reach(self, name):
        while name in self.ahead:
            getattr(self, self.ahead.pop(0))()

    ready = ()

    def add(self, picks, shapes, ins, joined=False):
        ready, self.ready = self.ready, ()
        return self.order.run(add_pieces, picks, shapes, ins, ready, joined)

    def halves(self):
        shape = (2,) + self.keep.shape[2:]
        picks = [
            [(0, (path, slice(at, at + 2))), (1 + i * 2 + path, None)]
            for i, at in enumerate((2, 0))
            for path in range(2)
        ]
        outs = self.add(picks, [shape] * 4, [self.keep, *self.got])
        self.coming = [swap(outs[path], *FIRST[path]) for path in range(2)]
        self.kept = outs[2:]

    def quarters(self):
        shape = self.keep.shape[2:]
        picks = [[(path, at), (2 + path, at)] for at in (1, 0) for path in range(2)]
        outs = self.add(picks, [shape] * 4, [*self.kept, *self.coming])
        self.coming = [swap(outs[path], *SECOND[path]) for path in range(2)]
        self.kept = outs[2:]

    def finals(self):
        shape = self.keep.shape[2:]
        picks = [[(path, None), (2 + path, None)] for path in range(2)]
        own = self.add(picks, [(2,) + shape], [*self.kept, *self.coming], True)[0]
        self.all = lax.all_gather(own, ("context", "dp"), axis=0)


DEEP = 4


def place_pieces_kernel(e, first, *refs):
    source = refs[0]
    outs = refs[2:5] if first else refs[5:8]
    token_ref, low, wide, in_sem, out_sem = refs[-5:]
    rows = low.shape[2]
    count = 2 * source.shape[0]
    token_ref[...] = jnp.zeros_like(token_ref)

    def fetch(i):
        return pltpu.make_async_copy(source.at[i // 2, i % 2], low.at[i % DEEP], in_sem.at[i % DEEP])

    def drain(i):
        path, member = i % 2, i // 2
        side, core, dp = member // 4, member // 2 % 2, member % 2
        chunk = core * 2 + path
        piece = (dp * 2 + side, side * 2 + dp)[path]
        columns = pl.ds(chunk * CHUNK, CHUNK)
        copies = []
        for k in range(2):
            copies.append(
                pltpu.make_async_copy(
                    wide.at[i % DEEP, k],
                    outs[k].at[e, pl.ds(piece * rows, rows), columns],
                    out_sem.at[i % DEEP, k],
                )
            )
        for j in range(rows // CHUNK):
            copies.append(
                pltpu.make_async_copy(
                    wide.at[i % DEEP, 2, pl.ds(j * CHUNK, CHUNK)],
                    outs[2].at[e, columns, pl.ds(piece * rows + j * CHUNK, CHUNK)],
                    out_sem.at[i % DEEP, 2 + j],
                )
            )
        return copies

    for i in range(DEEP - 1):
        fetch(i).start()
    for i in range(count):
        if i + DEEP - 1 < count:
            fetch(i + DEEP - 1).start()
        fetch(i).wait()
        if i >= DEEP:
            for copy in drain(i - DEEP):
                copy.wait()
        for k in range(3):

            @pl.loop(0, rows // 64)
            def _(t):
                r = pl.ds(pl.multiple_of(t * 64, 64), 64)
                wide[i % DEEP, k, r, :] = low[i % DEEP, k, r, :].astype(F32)

        for copy in drain(i):
            copy.start()
    for i in range(count - DEEP, count):
        for copy in drain(i):
            copy.wait()


def place_pieces(token, e, gathered, outs, shapes):
    first = outs is None
    rows = gathered.shape[3]
    operands = [gathered, token] + ([] if first else list(outs[:3]))
    return pl.pallas_call(
        functools.partial(place_pieces_kernel, e, first),
        in_specs=[ANYWHERE] * len(operands),
        out_specs=[ANYWHERE] * 3 + [token_spec()],
        scratch_shapes=[
            pltpu.VMEM((DEEP, 3, rows, CHUNK), BF16),
            pltpu.VMEM((DEEP, 3, rows, CHUNK), F32),
            pltpu.SemaphoreType.DMA((DEEP,)),
            pltpu.SemaphoreType.DMA((DEEP, 2 + rows // CHUNK)),
        ],
        out_shape=[jax.ShapeDtypeStruct(s, F32) for s in shapes] + [TOKEN],
        input_output_aliases={} if first else {2: 0, 3: 1, 4: 2},
        compiler_params=pltpu.CompilerParams(vmem_limit_bytes=60 * MIB),
        cost_estimate=pl.CostEstimate(
            flops=0, bytes_accessed=16 * 9 * rows * CHUNK * 2, transcendentals=0
        ),
        name="place_pieces",
    )(*operands)


def hop_kernel(*refs):
    *parts, got, _, out_ref, token_ref = refs
    token_ref[...] = jnp.zeros_like(token_ref)
    total = parts[0][...].astype(F32)
    for part in parts[1:]:
        total = total + part[...].astype(F32)
    out_ref[...] = (total + got[...].astype(F32)).astype(BF16)


def hop_add(token, parts, got):
    rows, width = got.shape
    half = rows // 2

    def at(place):
        return pl.BlockSpec((half, width), lambda i: (2 * place + i, 0))

    return pl.pallas_call(
        hop_kernel,
        grid=(2,),
        in_specs=[at(p) for _, p in parts] + [at(0), ANYWHERE],
        out_specs=[at(0), token_spec()],
        out_shape=[jax.ShapeDtypeStruct((rows, width), BF16), TOKEN],
        compiler_params=pltpu.CompilerParams(vmem_limit_bytes=60 * MIB),
        cost_estimate=pl.CostEstimate(
            flops=rows * width * 5, bytes_accessed=14 * rows * width, transcendentals=0
        ),
        name="hop",
    )(*(a for a, _ in parts), got, token)


def body(
    hidden_in,
    out_grad,
    routes,
    attn_gain,
    w_query,
    w_key,
    w_value,
    q_gain,
    k_gain,
    w_out,
    ffn_gain,
    w_router,
    w_gate,
    w_up,
    w_down,
):
    groups = lax.axis_size("expert")
    context = lax.axis_size("context")
    my_group = lax.axis_index("expert")
    my_context = lax.axis_index("context")
    my_dp = lax.axis_index("dp")
    tokens = hidden_in.shape[1]
    width = hidden_in.shape[2]
    rows = w_query.shape[0]
    local_experts = w_gate.shape[0]
    experts_all = w_router.shape[1]
    length = tokens * context
    per = HEADS // context
    local = per * HDIM
    core, side = my_context % 2, my_context // 2
    bits = jnp.stack([core, my_dp * 2 + side, side * 2 + my_dp]).astype(jnp.int32)
    ring = [(my_group - s) % groups for s in range(groups)]
    members = [my_context ^ s for s in range(context)]

    def half_columns(weight):
        split = weight.reshape(rows, 2, per // 2, context, HDIM)
        split = lax.dynamic_index_in_dim(split, my_dp, 1, keepdims=False)
        return split.transpose(2, 0, 1, 3).reshape(context, rows, local // 2)

    columns = jnp.concatenate([half_columns(w) for w in (w_query, w_key, w_value)], axis=2)
    pieces = [lax.dynamic_index_in_dim(columns, m, 0, keepdims=False) for m in members]
    pieces = [pieces[0]] + [swap(pieces[s], "context", s) for s in range(1, context)]
    half_w = take(jnp.stack(pieces), members).reshape(context * rows, 3 * local // 2)
    small = jnp.concatenate(
        [attn_gain[None], q_gain[None], k_gain[None], ffn_gain[None], w_router.T], axis=0
    )
    small = [small] + [swap(small, "context", s) for s in range(1, context)]
    small = take(jnp.stack(small), members)
    hidden_all = after(hidden_in[0], half_w)
    hidden_all = jnp.concatenate(context_gather(hidden_all), axis=0)
    small = take(jnp.stack(ring_direct(small)), ring)
    small_all = small.transpose(2, 0, 1, 3).reshape(4 + experts_all, width)
    halves, others = [half_w], [swap(half_w, "dp", 1)]
    for s in range(1, groups):
        halves.append(shift(halves[-1], 1))
        others.append(swap(halves[-1], "dp", 1))
    some = local // 2
    qkv_w = jnp.concatenate(
        [
            jnp.concatenate(
                [w[:, i * some : (i + 1) * some] for i in range(3) for w in pair], axis=1
            )
            for pair in zip(halves, others)
        ],
        axis=0,
    )
    heads = [my_dp * 2, my_dp * 2 + 1, (1 - my_dp) * 2, (1 - my_dp) * 2 + 1]
    whole_heads = rows == HDIM
    routes_ring = ring_direct(after(routes[0], halves[-1]))
    if whole_heads:
        out_all = lax.all_gather(after(w_out, halves[-1]), "expert", axis=0)
    upstream_all = lax.all_gather(after(out_grad[0], halves[-1]), "expert", axis=0)

    gain_attn = small_all[0].astype(F32)
    gain_ffn = small_all[3].astype(F32)
    router_w = small_all[4:]
    router_wide = jnp.pad(router_w.T, ((0, 0), (0, 128 - experts_all)))

    def mine(vector):
        table = vector.reshape(per, context, HDIM)
        table = lax.dynamic_index_in_dim(table, my_context, 1, keepdims=False)
        return take(table, heads).astype(F32)

    gain_query, gain_key = mine(small_all[1]), mine(small_all[2])
    block = width // groups

    def to_ring(values):
        parts = [lax.dynamic_slice_in_dim(values, m * block, block, axis=1) for m in ring]
        return jnp.concatenate(parts, axis=1)

    source_all = hidden_all.astype(F32)
    factor_all = rms_factor(source_all)
    normed = to_ring((source_all * factor_all * gain_attn).astype(BF16))
    source = hidden_in[0].astype(F32)
    factor_one = rms_factor(source)
    qkv = dot(normed, qkv_w, (1, 0))

    def slots(query, key):
        return jnp.stack([v.reshape(context, tokens) for v in (query, key)])

    def per_row(values):
        return values.reshape(length)[:, None]

    squares = [jnp.sum(jnp.square(qkv[:, i * local : (i + 1) * local]), axis=-1) for i in range(2)]
    squares = context_total(slots(*squares))
    factors = lax.rsqrt(squares / width + epsilon)
    factor_query, factor_key = per_row(factors[0]), per_row(factors[1])
    starts = jnp.stack([m * tokens for m in members])
    positions = (starts[:, None] + jnp.arange(tokens, dtype=jnp.int32)).reshape(length).astype(F32)
    frequency = rope_base ** (-jnp.arange(HDIM // 2, dtype=F32) * 2.0 / HDIM)
    angles = positions[:, None] * frequency[None, :]
    cosine = jnp.tile(jnp.cos(angles), (1, 2))
    sine_part = jnp.sin(angles)
    sine_part = jnp.concatenate([-sine_part, sine_part], axis=1)
    turn = (factor_query, factor_key, gain_query[:, None], gain_key[:, None], cosine, sine_part)
    query_low, key_low, value_low, mixed_low, logsum = attend(qkv, *turn, [])
    if whole_heads:
        out_w = take(out_all, heads).reshape(local, width)
    else:
        out_w = lax.all_gather(w_out, ("expert", "context"), axis=0, tiled=True)
        out_w = out_w.reshape(per, context, HDIM, width)
        out_w = lax.dynamic_index_in_dim(out_w, my_context, 1, keepdims=False)
        out_w = take(out_w, heads).reshape(local, width)
    ids = jnp.arange(128, dtype=jnp.int32)
    masks = [jnp.any(r[:, :, None] == ids, axis=1).astype(F32) for r in routes_ring]
    mixed_out = dot(mixed_low, out_w, (1, 0)).astype(BF16).reshape(context, tokens, width)
    residual = after(source, *routes_ring[1:]) + context_sum([mixed_out[s] for s in range(context)])
    factor_two = rms_factor(residual)
    normed_two = (residual * factor_two * gain_ffn).astype(BF16)

    at = jnp.reshape(my_group * local_experts, (1,)).astype(jnp.int32)
    order = Order()

    def rows_of(first, count, x, u, mask, *ready):
        return order.run(
            run_rows, at, first, count, x, u, mask, router_wide, w_gate, w_up, w_down, *ready
        )

    near = [[(0, local_experts)], [(0, local_experts)]]
    if local_experts == 4:
        near = [[(0, 2), (2, 2)]] * 2
    blocks = ring_gather(normed_two)
    segments = [([0], []), ([1], [])]

    ups = [out_grad[0]]

    def upstream_of(slot):
        m = ring[slot] + order.token[0, 0].astype(jnp.int32)
        return lax.dynamic_index_in_dim(upstream_all, m, 0, keepdims=False)

    def near_rows(slot, i):
        first, count = near[slot][i]
        ready = [upstream_all] if (slot, i) == (0, 1) else []
        result = rows_of(first, count, blocks[slot], ups[slot], masks[slot], *ready)
        segments[slot][1].append((first, count, result))

    for slot in range(2):
        if slot == 1:
            ups.append(upstream_of(1))
        for i in range(len(near[slot])):
            if (slot, i) != (1, 1):
                near_rows(slot, i)
    far = []
    for slot in range(2, groups, 2):
        pair = [slot, slot + 1]
        x, u, mask = (
            jnp.concatenate(v, axis=0)
            for v in (
                [blocks[s] for s in pair],
                [upstream_of(s) for s in pair],
                [masks[s] for s in pair],
            )
        )
        far.append((x, u, mask))
        segments.append((pair, []))
        ups.append(u)

    def segment_of(segment, e):
        for first, count, result in segments[segment][1]:
            if first <= e < first + count:
                return (result[4], ups[segment], result[5], result[6], e - first)

    whole_sums = min(1, local_experts)
    summed = []

    def sum_grads():
        e = len(summed)
        if e == local_experts:
            return
        call = run_grads
        if e >= whole_sums:
            call = functools.partial(run_split, bits=bits)
        bunches = [[0, 1, 2]] + [[s, s + 1] for s in range(3, len(segments), 2)]
        results = []
        for bunch in bunches:
            bunch = [segment_of(s, e) for s in bunch if s < len(segments)]
            results.append(order.run(call, bunch))
        grads = [
            total_low(list(terms)) if len(terms) > 1 else terms[0] for terms in zip(*results)
        ]
        if e < whole_sums:
            summed.append(lax.psum(grads, ("context", "dp")))
        else:
            summed.append(Summed(order, grads[:4], grads[4]))

    def advance(*events):
        for e, name in events:
            if whole_sums <= e < local_experts:
                summed[e].reach(name)

    def parts_of(slot, index):
        for pair, calls in segments:
            if slot in pair:
                return [(result[index], pair.index(slot)) for _, _, result in calls]

    def hop(index, total, slot):
        return order.run(hop_add, parts_of(slot % groups, index), shift(total, 1))[0]

    def first_hop(index):
        return total_low([r[p * tokens : (p + 1) * tokens] for r, p in parts_of(1, index)])

    for e in range(local_experts):
        for i, (x, u, mask) in enumerate(far):
            segments[2 + i][1].append((e, 1, rows_of(e, 1, x, u, mask)))
        if e < 2:
            sum_grads()
        if e == 0 and len(near[1]) > 1:
            near_rows(1, 1)
        if e == 2:
            advance((1, "halves"))
    row_total = hop(1, first_hop(1), 2)
    sum_grads()
    advance((1, "quarters"))

    gate_grad = [
        functools.reduce(
            lambda a, b: a + b,
            [result[2][pair.index(s) * tokens : (pair.index(s) + 1) * tokens] for _, _, result in calls],
        )
        for pair, calls in segments
        for s in pair
    ]
    gate_grad = [g[:, :local_experts].T for g in gate_grad]
    gate_grad = jnp.stack([gate_grad[0]] + [shift(gate_grad[s], -s) for s in range(1, groups)])
    gate_grad = take(gate_grad, [(g - my_group) % groups for g in range(groups)])
    gate_grad = gate_grad.reshape(experts_all, tokens).T

    for slot in range(3, groups + 1):
        row_total = hop(1, row_total, slot)
        if slot == 3:
            sum_grads()
            advance((1, "finals"), (2, "halves"))
    row_back = row_total.astype(F32)
    shapes = (w_gate.shape, w_up.shape, w_down.shape)
    expert_grads = None

    def place(experts):
        outs = expert_grads
        for e in experts:
            if e < local_experts:
                if e >= whole_sums:
                    summed[e].reach("finals")
                    outs = order.run(place_pieces, e, summed[e].all, outs, shapes)
                else:
                    outs = order.run(place_grads, e, summed[e], outs, shapes)
        return outs


    upstream = out_grad[0].astype(F32)
    weights_own = segments[0][1][0][2][3][:, :experts_all]
    weighted = jnp.sum(weights_own * gate_grad, axis=-1, keepdims=True)
    logit_grad = (weights_own * (gate_grad - weighted)).astype(BF16)
    router_grad = dot(logit_grad, normed_two, (0, 0))
    normed_two_grad = dot(logit_grad, router_w, (1, 0)) + row_back
    residual_part, ffn_gain_grad = norm_back(normed_two_grad, residual, factor_two, gain_ffn)
    residual_grad = upstream + residual_part

    attn_grad = context_gather(residual_grad.astype(BF16))
    out_total = hop(0, first_hop(0), 2)
    attn_grad = jnp.concatenate(attn_grad, axis=0)
    mixed_grad = dot(attn_grad, out_w, (1, 1)).astype(BF16)
    query_back, key_back, value_grad, query_sum, key_sum, q_gain_grad, k_gain_grad = order.run(
        attend_back, query_low, key_low, value_low, mixed_grad, logsum, qkv, *turn
    )
    out_w_grad = dot(mixed_low, after(attn_grad, order.token), (0, 0)).astype(BF16)
    advance((2, "quarters"))

    class Ring:
        def __init__(self, terms):
            self.terms, self.size, self.slot = terms, terms.shape[0] // groups, 1
            at = 1 % groups * self.size
            self.total = terms[at : at + self.size]
            self.coming = shift(self.total, 1)

        def hop(self):
            if self.slot < groups:
                self.slot += 1
                self.total = order.run(hop_add, [(self.terms, self.slot % groups)], self.coming)[0]
                self.coming = shift(self.total, 1)

        def whole(self):
            while self.slot < groups:
                self.hop()
            return self.total

    if whole_heads:
        ordered = take(
            out_w_grad.reshape(per, HDIM, width), [(m // 2 ^ my_dp) * 2 + m % 2 for m in ring]
        )
        out_ring = Ring(ordered.reshape(local, width))
    for slot in range(3, groups):
        out_total = hop(0, out_total, slot)
    sums = context_total(slots(jnp.sum(query_sum, axis=1), jnp.sum(key_sum, axis=1))) / width
    order.token = after(order.token, sums)
    advance((3, "halves"))
    if groups > 2:
        out_total = hop(0, out_total, groups)
    hidden_out = (residual + out_total.astype(F32)).astype(BF16)[None]
    if whole_heads:
        out_ring.hop()
    def low_grad(back, raw, factor, gain, total):
        return (
            factor * back * gain.reshape(1, local) - raw * factor**3 * per_row(total)
        ).astype(BF16)

    query_grad = low_grad(query_back, qkv[:, :local], factor_query, gain_query, sums[0])
    key_grad = low_grad(key_back, qkv[:, local : 2 * local], factor_key, gain_key, sums[1])
    qkv_grad = jnp.concatenate([query_grad, key_grad, value_grad], axis=1)
    qkv_w_grad = dot(normed, qkv_grad, (0, 0)).astype(BF16)
    normed_grad = dot(qkv_grad, qkv_w, (1, 1)).astype(BF16)
    order.token = after(order.token, qkv_w_grad, normed_grad)
    normed_grad = normed_grad.reshape(context, tokens, width)
    normed_own, normed_near, normed_far = context_terms([normed_grad[s] for s in range(context)])

    qkv_ring = Ring(qkv_w_grad)
    advance((2, "finals"))
    if whole_heads:
        out_ring.hop()
    advance((3, "quarters"))
    qkv_ring.hop()
    expert_grads = place([0])
    if whole_heads:
        mine_out = out_ring.whole()
        out_w_grad = mine_out.astype(F32) + swap(mine_out, "dp", 1).astype(F32)
    qkv_ring.hop()
    advance((3, "finals"))
    expert_grads = place([1, 2])
    qkv_w_grad = qkv_ring.whole()
    normed_own = after(normed_own, order.token)
    normed_grad = normed_own.astype(F32) + normed_near.astype(F32) + normed_far.astype(F32)
    parts = [
        lax.dynamic_slice_in_dim(normed_grad, (my_group - m) % groups * block, block, axis=1)
        for m in range(groups)
    ]
    normed_grad = jnp.concatenate(parts, axis=1)
    source_part, attn_gain_grad = norm_back(normed_grad, source, factor_one, gain_attn)
    input_grad = (residual_grad + source_part).astype(BF16)[None]

    mine_w = qkv_w_grad.reshape(context, rows, 3, 2, some)
    got = swap(mine_w, "dp", 1)
    expert_grads = place([3])
    mine_w = after(mine_w, order.token)
    mine_w = jnp.stack(
        [add_low(mine_w[:, :, :, i], got[:, :, :, 1 - i]) for i in range(2)], axis=3
    )
    pieces = [lax.dynamic_index_in_dim(mine_w, m, 0, keepdims=False) for m in members]
    pieces = [pieces[0]] + [swap(pieces[s], "context", s) for s in range(1, context)]
    dense = take(jnp.stack(pieces), members)
    dense = jnp.where(my_dp == 0, dense, dense[:, :, :, ::-1]).astype(F32)
    dense = dense.reshape(context, rows, 3, per, HDIM).transpose(2, 1, 3, 0, 4)
    dense = dense.reshape(3, rows, width)
    if not whole_heads:
        spread = jnp.zeros((per, context, HDIM, width), BF16)
        for h in range(per):
            term = out_w_grad.reshape(per, HDIM, width)[h][None, None]
            spread = lax.dynamic_update_slice(spread, term, (heads[h], my_context, 0, 0))
        spread = lax.psum_scatter(
            spread.reshape(width, width), ("expert", "context"), scatter_dimension=0, tiled=True
        )
        out_w_grad = lax.psum(spread, "dp").astype(F32)
    gains = jnp.zeros((2, per, context, HDIM), F32)
    for h in range(per):
        pair = jnp.stack([q_gain_grad[h], k_gain_grad[h]])[:, None]
        gains = lax.dynamic_update_slice(gains, pair, (0, heads[h], my_context, 0))
    small_grad = jnp.concatenate(
        [attn_gain_grad[None], ffn_gain_grad[None], gains.reshape(2, width), router_grad], axis=0
    )
    small_grad = small_grad.reshape(4 + experts_all, groups, context, rows).transpose(1, 2, 0, 3)
    small_grad = after(take(small_grad, ring), qkv_w_grad)
    small_grad = functools.reduce(
        lambda a, b: a + b,
        [small_grad[0]] + [shift(small_grad[s], -s) for s in range(1, groups)],
    )
    small_grad = take(small_grad, members)
    got = swap(jnp.stack([small_grad[1], small_grad[3]]), "context", 1)
    small_grad = small_grad[0] + got[0] + swap(small_grad[2] + got[1], "context", 2)
    small_grad = small_grad + swap(small_grad, "dp", 1)
    return (
        hidden_out,
        input_grad,
        small_grad[0],
        dense[0],
        dense[1],
        dense[2],
        small_grad[2],
        small_grad[3],
        out_w_grad,
        small_grad[1],
        small_grad[4:].T,
        expert_grads[0],
        expert_grads[1],
        expert_grads[2],
    )


def solution(mesh):
    tokens = P(("expert", "dp"), "context", None)
    vector = P(("expert", "context"))
    matrix = P(("expert", "context"), None)
    expert = P("expert", None, None)
    in_specs = (
        tokens,
        tokens,
        tokens,
        vector,
        matrix,
        matrix,
        matrix,
        vector,
        vector,
        matrix,
        vector,
        matrix,
        expert,
        expert,
        expert,
    )
    out_specs = (
        tokens,
        tokens,
        vector,
        matrix,
        matrix,
        matrix,
        vector,
        vector,
        matrix,
        vector,
        matrix,
        expert,
        expert,
        expert,
    )
    return jax.shard_map(body, mesh=mesh, in_specs=in_specs, out_specs=out_specs, check_vma=False)
```
